32 devices in a mesh: tok: 4 (over z), mod: 2 (over core), head: 4 (over y, x).
Axes of the slice: x: 2, y: 2, z: 4, core: 2. Of those that a mesh axis runs over, the one named last changes fastest.
Arguments:
- latents: bfloat16 [16, 128, 768], P('mod'), may hold values from -6 to 6
- video_tokens: bfloat16 [16, 6272, 768], P('mod', 'tok'), may hold values from -6 to 6
- text_tokens: bfloat16 [16, 40, 768], P('mod'), may hold values from -6 to 6
- frame_counts: int32 [16], P('mod'), may hold values from 4 to 16, as said below
- text_lengths: int32 [16], P('mod'), may hold values from 8 to 40
- drop_mask: int32 [16], P('mod'), may hold values from 0 to 1, as said below
- cotangent: bfloat16 [16, 128, 768], P('mod'), may hold values from -6 to 6
- norm_latent_gain: float32 [768], replicated, may hold values from 0.5 to 1.5
- norm_latent_bias: float32 [768], replicated, may hold values from -1.75 to 1.75
- norm_input_gain: float32 [768], replicated, may hold values from 0.5 to 1.5
- norm_input_bias: float32 [768], replicated, may hold values from -0.125 to 0.125
- cross_query: bfloat16 [768, 768], P(None, 'head'), may hold values from -0.21875 to 0.21875
- cross_key: bfloat16 [768, 768], P(None, 'head'), may hold values from -0.21875 to 0.21875
- cross_value: bfloat16 [768, 768], P(None, 'head'), may hold values from -0.21875 to 0.21875
- cross_output: bfloat16 [768, 768], P('head'), may hold values from -10 to 10
- norm_cross_gain: float32 [768], replicated, may hold values from 0.5 to 1.5
- norm_cross_bias: float32 [768], replicated, may hold values from -1.75 to 1.75
- cross_up: bfloat16 [768, 3072], P(None, 'head'), may hold values from -0.21875 to 0.21875
- cross_down: bfloat16 [3072, 768], P('head'), may hold values from -0.15625 to 0.15625
- norm_self_gain: float32 [768], replicated, may hold values from 0.5 to 1.5
- norm_self_bias: float32 [768], replicated, may hold values from -0.3125 to 0.3125
- self_query: bfloat16 [768, 768], P(None, 'head'), may hold values from -0.21875 to 0.21875
- self_key: bfloat16 [768, 768], P(None, 'head'), may hold values from -0.21875 to 0.21875
- self_value: bfloat16 [768, 768], P(None, 'head'), may hold values from -0.21875 to 0.21875
- self_output: bfloat16 [768, 768], P('head'), may hold values from -1.5 to 1.5
- norm_ffn_gain: float32 [768], replicated, may hold values from 0.5 to 1.5
- norm_ffn_bias: float32 [768], replicated, may hold values from -1.75 to 1.75
- self_up: bfloat16 [768, 3072], P(None, 'head'), may hold values from -0.21875 to 0.21875
- self_down: bfloat16 [3072, 768], P('head'), may hold values from -0.15625 to 0.15625
Outputs:
- latents_out: bfloat16 [16, 128, 768], P('mod')
- grad_latents: bfloat16 [16, 128, 768], P('mod')
- grad_video: bfloat16 [16, 6272, 768], P('mod', 'tok')
- grad_text: bfloat16 [16, 40, 768], P('mod')
- grad_norm_latent_gain: float32 [768], replicated
- grad_norm_latent_bias: float32 [768], replicated
- grad_norm_input_gain: float32 [768], replicated
- grad_norm_input_bias: float32 [768], replicated
- grad_cross_query: float32 [768, 768], P(None, 'head')
- grad_cross_key: float32 [768, 768], P(None, 'head')
- grad_cross_value: float32 [768, 768], P(None, 'head')
- grad_cross_output: float32 [768, 768], P('head')
- grad_norm_cross_gain: float32 [768], replicated
- grad_norm_cross_bias: float32 [768], replicated
- grad_cross_up: float32 [768, 3072], P(None, 'head')
- grad_cross_down: float32 [3072, 768], P('head')
- grad_norm_self_gain: float32 [768], replicated
- grad_norm_self_bias: float32 [768], replicated
- grad_self_query: float32 [768, 768], P(None, 'head')
- grad_self_key: float32 [768, 768], P(None, 'head')
- grad_self_value: float32 [768, 768], P(None, 'head')
- grad_self_output: float32 [768, 768], P('head')
- grad_norm_ffn_gain: float32 [768], replicated
- grad_norm_ffn_bias: float32 [768], replicated
- grad_self_up: float32 [768, 3072], P(None, 'head')
- grad_self_down: float32 [3072, 768], P('head')
The draws below stay inside these ranges and needn't reach their ends.
Inputs may be any that keep to these rules, and one draw needn't show every extreme that they name: `frame_counts`: the clips form two halves, the first 8 and the rest; in each half one clip, drawn at random, has 16 frames, 40 text tokens and is never dropped. `drop_mask`: in each half of the clips at least one clip is dropped.
All inputs are finite; a program needn't handle non-finite values.
Results may differ from the reference program's by a relative error of at most 0.035.
Values may be sent and summed in bfloat16 or wider, within the bound.
No kernel may reach another device: no remote copies, remote signals or barrier semaphores. Data moves between devices by JAX's collectives and lax.ppermute only.
A program may use at most 256 MiB of HBM per device.

```python
import jax
import jax.numpy as jnp
from jax import lax

D = 768
HEADS = 12
HEAD = 64
FF = 3072
LAT = 128
PATCH = 392
MAXF = 16
TEXT = 40
CLIPS = 16
N_MOD = 2


def long_choice(key):
    per_half = CLIPS // N_MOD
    return jax.random.randint(jax.random.fold_in(key, 11), (N_MOD,), 0, per_half)


def clip_plan(key):
    per_half = CLIPS // N_MOD
    chosen = long_choice(key)
    return jnp.arange(CLIPS) % per_half == jnp.repeat(chosen, per_half)


def draw_frame_counts(key, part):
    long_clip = clip_plan(key)
    key = jax.random.fold_in(key, 1)
    counts = jax.random.randint(key, (CLIPS,), 4, MAXF + 1)
    return jnp.where(long_clip, MAXF, counts).astype(jnp.int32)


def draw_text_lengths(key, part):
    long_clip = clip_plan(key)
    key = jax.random.fold_in(key, 2)
    counts = jax.random.randint(key, (CLIPS,), max(1, TEXT // 5), TEXT + 1)
    return jnp.where(long_clip, TEXT, counts).astype(jnp.int32)


def draw_drop_mask(key, part):
    per_half = CLIPS // N_MOD
    chosen = long_choice(key)
    long_clip = clip_plan(key)
    key = jax.random.fold_in(key, 3)
    offsets = jax.random.randint(jax.random.fold_in(key, 5), (N_MOD,), 1, per_half)
    dropped_index = (chosen + offsets) % per_half
    dropped = jnp.arange(CLIPS) % per_half == jnp.repeat(dropped_index, per_half)
    flags = jax.random.randint(key, (CLIPS,), 0, 2)
    return jnp.where(long_clip, 0, jnp.where(dropped, 1, flags)).astype(jnp.int32)


def block_scale(rng, shape, pieces, low, top_value):
    loudness = 1.0
    for dim, blocks in pieces:
        steps = jax.random.uniform(jax.random.fold_in(jax.random.fold_in(rng, 6), dim), (blocks,), jnp.float32, low / len(pieces), top_value / len(pieces))
        loudness = loudness * jnp.repeat(jnp.exp(steps), shape[dim] // blocks).reshape((-1,) + (1,) * (len(shape) - 1 - dim))
    return loudness


def normal_values(stream_key, extent, spread, bound, split=(), kind=jnp.bfloat16):
    entries = jax.random.normal(stream_key, extent, jnp.float32) * spread
    if len(split) > 0:
        entries = block_scale(stream_key, extent, split, -0.22, 0.18) * entries
    return jnp.clip(entries, min=-bound, max=bound).astype(kind)


def setup_inputs(seed: int = 0) -> dict:
    key_of = jax.random.split(jax.random.key(seed), 30)
    latents = normal_values(key_of[0], (CLIPS, LAT, D), 1.0, 6.0, ((0, 2),))
    video_tokens = normal_values(key_of[1], (CLIPS, MAXF * PATCH, D), 1.0, 6.0, ((0, 2), (1, 4)))
    text_tokens = normal_values(key_of[2], (CLIPS, TEXT, D), 1.0, 6.0, ((0, 2),))
    frame_counts = draw_frame_counts(jax.random.fold_in(key_of[29], 71), 0)
    text_lengths = draw_text_lengths(jax.random.fold_in(key_of[29], 71), 0)
    drop_mask = draw_drop_mask(jax.random.fold_in(key_of[29], 71), 0)
    cotangent = normal_values(key_of[6], (CLIPS, LAT, D), 1.0, 6.0, ((0, 2),))
    norm_latent_gain = jnp.clip(1.0 + 0.1 * jax.random.normal(key_of[7], (D,), jnp.float32), 0.5, 1.5)
    norm_latent_bias = normal_values(key_of[8], (D,), 0.3, 1.75, (), jnp.float32)
    norm_input_gain = jnp.clip(1.0 + 0.1 * jax.random.normal(key_of[9], (D,), jnp.float32), 0.5, 1.5)
    norm_input_bias = normal_values(key_of[10], (D,), 0.02, 0.125, (), jnp.float32)
    cross_query = normal_values(key_of[11], (D, D), D ** -0.5, 0.21875, ((1, 4),))
    cross_key = normal_values(key_of[12], (D, D), D ** -0.5, 0.21875, ((1, 4),))
    cross_value = normal_values(key_of[13], (D, D), D ** -0.5, 0.21875, ((1, 4),))
    cross_output = normal_values(key_of[14], (D, D), ((MAXF * PATCH) ** 0.5 * (3 * D) ** -0.5), 10.0, ((0, 4),))
    norm_cross_gain = jnp.clip(1.0 + 0.1 * jax.random.normal(key_of[15], (D,), jnp.float32), 0.5, 1.5)
    norm_cross_bias = normal_values(key_of[16], (D,), 0.3, 1.75, (), jnp.float32)
    cross_up = normal_values(key_of[17], (D, FF), D ** -0.5, 0.21875, ((1, 4),))
    cross_down = normal_values(key_of[18], (FF, D), (FF // 2) ** -0.5, 0.15625, ((0, 4),))
    norm_self_gain = jnp.clip(1.0 + 0.1 * jax.random.normal(key_of[19], (D,), jnp.float32), 0.5, 1.5)
    norm_self_bias = normal_values(key_of[20], (D,), 0.05, 0.3125, (), jnp.float32)
    self_query = normal_values(key_of[21], (D, D), D ** -0.5, 0.21875, ((1, 4),))
    self_key = normal_values(key_of[22], (D, D), D ** -0.5, 0.21875, ((1, 4),))
    self_value = normal_values(key_of[23], (D, D), D ** -0.5, 0.21875, ((1, 4),))
    self_output = normal_values(key_of[24], (D, D), (LAT ** 0.5 * (3 * D) ** -0.5), 1.5, ((0, 4),))
    norm_ffn_gain = jnp.clip(1.0 + 0.1 * jax.random.normal(key_of[25], (D,), jnp.float32), 0.5, 1.5)
    norm_ffn_bias = normal_values(key_of[26], (D,), 0.3, 1.75, (), jnp.float32)
    self_up = normal_values(key_of[27], (D, FF), D ** -0.5, 0.21875, ((1, 4),))
    self_down = normal_values(key_of[28], (FF, D), (FF // 2) ** -0.5, 0.15625, ((0, 4),))
    return {"latents": latents, "video_tokens": video_tokens, "text_tokens": text_tokens, "frame_counts": frame_counts, "text_lengths": text_lengths, "drop_mask": drop_mask, "cotangent": cotangent, "norm_latent_gain": norm_latent_gain, "norm_latent_bias": norm_latent_bias, "norm_input_gain": norm_input_gain, "norm_input_bias": norm_input_bias, "cross_query": cross_query, "cross_key": cross_key, "cross_value": cross_value, "cross_output": cross_output, "norm_cross_gain": norm_cross_gain, "norm_cross_bias": norm_cross_bias, "cross_up": cross_up, "cross_down": cross_down, "norm_self_gain": norm_self_gain, "norm_self_bias": norm_self_bias, "self_query": self_query, "self_key": self_key, "self_value": self_value, "self_output": self_output, "norm_ffn_gain": norm_ffn_gain, "norm_ffn_bias": norm_ffn_bias, "self_up": self_up, "self_down": self_down}


@jax.custom_vjp
def low(v):
    return lax.optimization_barrier(v.astype(jnp.bfloat16)).astype(jnp.float32)

@jax.custom_vjp
def low_back(v):
    return v

def low_keep(v):
    return (low(v), None)

def low_pass(kept, grad):
    return (grad,)

def back_keep(v):
    return (v, None)

def back_low(kept, grad):
    return (low(grad),)
low.defvjp(low_keep, low_pass)
low_back.defvjp(back_keep, back_low)
EPSILON = 1e-05
NEGATIVE = -1e+30

def layer_norm(rows, gain, bias):
    mean = lax.optimization_barrier(jnp.mean(rows, -1, keepdims=True))
    centered = rows - mean
    variance = lax.optimization_barrier(jnp.mean(centered * centered, -1, keepdims=True))
    return centered * lax.rsqrt(variance + EPSILON) * gain + bias

def product(rows, weight):
    return jnp.einsum('...d,df->...f', rows, weight, precision=lax.Precision.HIGHEST)

def attention(queries, keys, values, valid):
    scale = HEAD ** (-0.5)
    rows = queries.shape[0]
    count = keys.shape[0]
    heads_q = queries.reshape(rows, HEADS, HEAD)
    heads_k = keys.reshape(count, HEADS, HEAD)
    heads_v = values.reshape(count, HEADS, HEAD)
    scores = low_back(jnp.einsum('lhe,nhe->lhn', heads_q, heads_k, precision=lax.Precision.HIGHEST) * scale)
    masked = jnp.where(valid[None, None, :], scores, NEGATIVE)
    peak = lax.optimization_barrier(jnp.max(masked, -1, keepdims=True))
    weights = jnp.where(valid[None, None, :], jnp.exp(masked - peak), 0.0)
    total = lax.optimization_barrier(jnp.sum(weights, -1, keepdims=True))
    summed = jnp.einsum('lhn,nhe->lhe', low(weights), heads_v, precision=lax.Precision.HIGHEST)
    return (summed / total).reshape(rows, HEADS * HEAD)

def cross_clip(parts):
    return attention(parts[0], parts[1], parts[2], parts[3])

def self_clip(parts):
    valid = jnp.ones((parts[1].shape[0],), dtype=bool)
    return attention(parts[0], parts[1], parts[2], valid)

def feed_forward(rows, gain, bias, upper, lower):
    inner = low(layer_norm(rows, gain, bias))
    pre = low_back(product(inner, upper))
    hidden = low(jax.nn.gelu(pre, approximate=False))
    return low_back(product(hidden, lower))

def reference(latents, video_tokens, text_tokens, frame_counts, text_lengths, drop_mask, cotangent, norm_latent_gain, norm_latent_bias, norm_input_gain, norm_input_bias, cross_query, cross_key, cross_value, cross_output, norm_cross_gain, norm_cross_bias, cross_up, cross_down, norm_self_gain, norm_self_bias, self_query, self_key, self_value, self_output, norm_ffn_gain, norm_ffn_bias, self_up, self_down):
    video_valid = jnp.arange(MAXF * PATCH)[None, :] // PATCH < frame_counts[:, None]
    text_valid = jnp.arange(TEXT)[None, :] < text_lengths[:, None]
    key_valid = jnp.concatenate([video_valid, text_valid], axis=1)
    keep = (1 - drop_mask).astype(jnp.float32)[:, None, None]
    floats = [item.astype(jnp.float32) for item in (latents, video_tokens, text_tokens, norm_latent_gain, norm_latent_bias, norm_input_gain, norm_input_bias, cross_query, cross_key, cross_value, cross_output, norm_cross_gain, norm_cross_bias, cross_up, cross_down, norm_self_gain, norm_self_bias, self_query, self_key, self_value, self_output, norm_ffn_gain, norm_ffn_bias, self_up, self_down)]

    def layer(state, video_rows, text_rows, lat_gain, lat_bias, in_gain, in_bias, c_query, c_key, c_value, c_output, c_gain, c_bias, c_up, c_down, s_gain, s_bias, s_query, s_key, s_value, s_output, f_gain, f_bias, s_up, s_down):
        queries_in = low(layer_norm(state, lat_gain, lat_bias))
        query = low(low_back(product(queries_in, c_query)))
        inputs_in = jnp.concatenate([low(layer_norm(video_rows, in_gain, in_bias)), low(layer_norm(text_rows, in_gain, in_bias))], axis=1)
        key = low(low_back(product(inputs_in, c_key)))
        value = low(low_back(product(inputs_in, c_value)))
        attended = low(low_back(lax.map(jax.checkpoint(cross_clip), (query, key, value, key_valid))))
        first = state + keep * low_back(product(attended, c_output))
        second = first + feed_forward(first, c_gain, c_bias, c_up, c_down)
        self_in = low(layer_norm(second, s_gain, s_bias))
        self_q = low(low_back(product(self_in, s_query)))
        self_k = low(low_back(product(self_in, s_key)))
        self_v = low(low_back(product(self_in, s_value)))
        self_attended = low(low_back(lax.map(jax.checkpoint(self_clip), (self_q, self_k, self_v))))
        third = second + low_back(product(self_attended, s_output))
        return third + feed_forward(third, f_gain, f_bias, s_up, s_down)
    output, pullback = jax.vjp(layer, *floats)
    grads = pullback(cotangent.astype(jnp.float32))
    return (output.astype(jnp.bfloat16), grads[0].astype(jnp.bfloat16), grads[1].astype(jnp.bfloat16), grads[2].astype(jnp.bfloat16), grads[3], grads[4], grads[5], grads[6], grads[7], grads[8], grads[9], grads[10], grads[11], grads[12], grads[13], grads[14], grads[15], grads[16], grads[17], grads[18], grads[19], grads[20], grads[21], grads[22], grads[23], grads[24])
```

```python
import jax
import jax.numpy as jnp
from jax import lax
from jax.experimental import pallas as pl
from jax.experimental.pallas import tpu as pltpu
from jax.sharding import PartitionSpec as P

HEAD = 64
PATCH = 392


EPSILON = 1e-05
NEGATIVE = -1e30


def combined_all(x, axis, combine):
    everything = jax.tree.map(
        lambda part, kind: lax.all_gather(part.astype(kind), axis),
        x,
        (jnp.bfloat16, jnp.bfloat16, jnp.bfloat16),
    )

    def take(k):
        return jax.tree.map(lambda part, own: part[k].astype(own.dtype), everything, x)

    return lax.fori_loop(
        1, lax.axis_size(axis), lambda k, so_far: combine(so_far, take(k)), take(0)
    )


def normalize(rows):
    mean = jnp.mean(rows, -1, keepdims=True)
    centered = rows - mean
    rstd = lax.rsqrt(jnp.mean(centered * centered, -1, keepdims=True) + EPSILON)
    return (centered * rstd, rstd)


def norm_back(grad_out, normed, rstd, gain):
    scaled = grad_out * gain
    grad_in = rstd * (
        scaled
        - jnp.mean(scaled, -1, keepdims=True)
        - normed * jnp.mean(scaled * normed, -1, keepdims=True)
    )
    leading = tuple(range(grad_out.ndim - 1))
    return (grad_in, jnp.sum(grad_out * normed, leading), jnp.sum(grad_out, leading))


def project(rows, weight):
    return jnp.einsum("...d,df->...f", rows, weight, preferred_element_type=jnp.float32)


def project_back(grad, weight):
    return jnp.einsum("...f,df->...d", grad, weight, preferred_element_type=jnp.float32)


def flatten_rows(rows):
    return rows.reshape(-1, rows.shape[-1])


def weight_grad(rows, grad):
    return lax.dot_general(
        flatten_rows(rows),
        flatten_rows(grad),
        (((0,), (0,)), ((), ())),
        preferred_element_type=jnp.float32,
    )


def split_heads(rows):
    return rows.reshape(rows.shape[:-1] + (rows.shape[-1] // HEAD, HEAD))


def head_rows(partial_rows):
    return lax.psum(partial_rows.astype(jnp.bfloat16), "head").astype(jnp.float32)


def head_grads(partial_rows):
    return lax.psum(partial_rows.astype(jnp.bfloat16), "head").astype(jnp.float32)


def attend_part(queries, keys, values, valid):
    scale = HEAD ** (-0.5)
    scores = (
        jnp.einsum("clhe,cnhe->clhn", queries, keys, preferred_element_type=jnp.float32) * scale
    )
    mask = valid[:, None, None, :]
    masked = jnp.where(mask, scores, NEGATIVE)
    peak = jnp.max(masked, -1)
    weights = jnp.where(mask, jnp.exp(masked - peak[..., None]), 0.0)
    total = jnp.sum(weights, -1)
    summed = jnp.einsum(
        "clhn,cnhe->clhe", weights.astype(jnp.bfloat16), values, preferred_element_type=jnp.float32
    )
    return (peak, total, summed)


def combine_parts(former, latter):
    top = jnp.maximum(former[0], latter[0])
    first_factor = jnp.exp(former[0] - top)
    second_factor = jnp.exp(latter[0] - top)
    total = former[1] * first_factor + latter[1] * second_factor
    summed = former[2] * first_factor[..., None] + latter[2] * second_factor[..., None]
    return (top, total, summed)


def attend_back(queries, keys, values, valid, log_total, d_attended, delta):
    scale = HEAD ** (-0.5)
    scores = (
        jnp.einsum("clhe,cnhe->clhn", queries, keys, preferred_element_type=jnp.float32) * scale
    )
    probs = jnp.where(valid[:, None, None, :], jnp.exp(scores - log_total[..., None]), 0.0)
    d_probs = jnp.einsum("clhe,cnhe->clhn", d_attended, values, preferred_element_type=jnp.float32)
    d_scores = (probs * (d_probs - delta[..., None])).astype(jnp.bfloat16)
    d_query = (
        jnp.einsum("clhn,cnhe->clhe", d_scores, keys, preferred_element_type=jnp.float32) * scale
    )
    d_key = (
        jnp.einsum("clhn,clhe->cnhe", d_scores, queries, preferred_element_type=jnp.float32) * scale
    )
    d_value = jnp.einsum(
        "clhn,clhe->cnhe",
        probs.astype(jnp.bfloat16),
        d_attended,
        preferred_element_type=jnp.float32,
    )
    return (d_query, d_key, d_value)


def gelu_exact(values):
    return jax.nn.gelu(values, approximate=False)


def feed_forward(rows, gain, bias, upper, lower):
    normed, rstd = normalize(rows)
    inner = (normed * gain + bias).astype(jnp.bfloat16)
    pre = project(inner, upper)
    hidden = gelu_exact(pre).astype(jnp.bfloat16)
    return (head_rows(project(hidden, lower)), (normed, rstd, inner, pre, hidden))


def feed_back(grad_rows, saved, gain, upper, lower):
    normed, rstd, inner, pre, hidden = saved
    grad_low = grad_rows.astype(jnp.bfloat16)
    d_hidden = project_back(grad_low, lower)
    unused, gelu_pull = jax.vjp(gelu_exact, pre)
    d_pre = gelu_pull(d_hidden)[0].astype(jnp.bfloat16)
    d_inner = head_grads(project_back(d_pre, upper))
    d_rows, d_gain, d_bias = norm_back(d_inner, normed, rstd, gain)
    return (grad_rows + d_rows, d_gain, d_bias, (inner, d_pre, hidden, grad_low))


LOG2E=1.4426950408889634
def dot(a,b): return jnp.dot(a,b,preferred_element_type=jnp.float32)
def dot_t(a,b): return lax.dot_general(a,b,(((0,),(0,)),((),())),preferred_element_type=jnp.float32)

def group_mask(lat, transposed):
    if transposed:
        r=lax.broadcasted_iota(jnp.int32,(4*HEAD,4*lat),0)//HEAD
        c=lax.broadcasted_iota(jnp.int32,(4*HEAD,4*lat),1)//lat
    else:
        r=lax.broadcasted_iota(jnp.int32,(4*lat,4*HEAD),0)//lat
        c=lax.broadcasted_iota(jnp.int32,(4*lat,4*HEAD),1)//HEAD
    return r==c

def row_sums(a):
    n, width = a.shape
    if n % 8:
        a = jnp.concatenate([a, jnp.zeros((8 - n % 8, width), a.dtype)], 0)
    return jnp.sum(a.reshape(-1, 8, width), 0)


def tokens_back_kernel(order_ref,valid_ref,tvalid_ref,tshare_ref,
    video_ref,text_ref,gain_ref,bias_ref,wkv_ref,wkvt_ref,q_ref,qt_ref,do_ref,dot_ref,lse_ref,delta_ref,
    dvideo_ref,dtext_ref,dw_ref,dq_ref,sums_ref,
    qbd,qbdt,dobd,dobdt):
    slot=pl.program_id(0); j=pl.program_id(1)
    lat=q_ref.shape[1]; width=q_ref.shape[2]; groups=width//(4*HEAD)
    rows=video_ref.shape[1]
    nvalid=valid_ref[slot]-j*rows
    ntext=tvalid_ref[slot]
    alive=ntext>0
    @pl.when((slot==0)&(j==0))
    def _():
        dw_ref[...]=jnp.zeros_like(dw_ref); sums_ref[...]=jnp.zeros_like(sums_ref)
    @pl.when(j==0)
    def _():
        dq_ref[...]=jnp.zeros_like(dq_ref)
    @pl.when((j==0)&alive)
    def _():
        m=group_mask(lat,False); mt=group_mask(lat,True)
        for g in range(groups):
            cols=slice(4*HEAD*g,4*HEAD*(g+1))
            for src,srct,dst,dstt in ((q_ref,qt_ref,qbd,qbdt),(do_ref,dot_ref,dobd,dobdt)):
                a=src[0,:,cols].astype(jnp.float32)
                dst[g]=jnp.where(m,jnp.concatenate([a]*4,0),0.).astype(jnp.bfloat16)
                b=srct[0,cols,:].astype(jnp.float32)
                dstt[g]=jnp.where(mt,jnp.concatenate([b]*4,1),0.).astype(jnp.bfloat16)
    def block(x, limit, out_ref, share):
        counted=(lambda a: a) if share is None else (lambda a: a*share)
        x=x.astype(jnp.float32)
        n=x.shape[0]
        mean=jnp.mean(x,-1,keepdims=True)
        xc=x-mean
        rstd=lax.rsqrt(jnp.mean(xc*xc,-1,keepdims=True)+EPSILON)
        xhat=xc*rstd
        xin=(xhat*gain_ref[...]+bias_ref[...]).astype(jnp.bfloat16)
        key=dot(xin,wkv_ref[:,:width]).astype(jnp.bfloat16)
        val=dot(xin,wkv_ref[:,width:]).astype(jnp.bfloat16)
        mask=lax.broadcasted_iota(jnp.int32,(n,1),0)<limit
        dks=[];dvs=[]
        for g in range(groups):
            cols=slice(4*HEAD*g,4*HEAD*(g+1))
            hl=slice(4*lat*g,4*lat*(g+1))
            s=dot(key[:,cols],qbdt[g])
            dp=dot(val[:,cols],dobdt[g])
            p=jnp.where(mask,jnp.exp2(s*LOG2E-lse_ref[0,:,hl]),0.)
            ds=(p*(dp-delta_ref[0,:,hl])).astype(jnp.bfloat16)
            dvs.append(dot(p.astype(jnp.bfloat16),dobd[g]).astype(jnp.bfloat16))
            dks.append(dot(ds,qbd[g]).astype(jnp.bfloat16))
            if g==0:
                t=dot_t(key[:,cols],ds)
                for h in range(3):
                    blk=t[HEAD*h:HEAD*(h+1),lat*h:lat*(h+1)]
                    dq_ref[0,HEAD*h:HEAD*(h+1),:]+=counted(blk)
        dk=jnp.concatenate(dks,1); dv=jnp.concatenate(dvs,1)
        din=dot(dk,wkvt_ref[:width])+dot(dv,wkvt_ref[width:])
        dw_ref[:256]+=counted(dot_t(dks[0],xin))
        dw_ref[256:]+=counted(dot_t(dvs[0],xin))
        sums_ref[0]+=counted(row_sums(din*xhat))
        sums_ref[1]+=counted(row_sums(din))
        sc=din*gain_ref[...]
        dx=rstd*(sc-jnp.mean(sc,-1,keepdims=True)-xhat*jnp.mean(sc*xhat,-1,keepdims=True))
        out_ref[0]=dx.astype(jnp.bfloat16)
    @pl.when(nvalid>0)
    def _():
        block(video_ref[0],nvalid,dvideo_ref,None)
    @pl.when(nvalid<=0)
    def _():
        dvideo_ref[...]=jnp.zeros_like(dvideo_ref)
    @pl.when((j==0)&alive)
    def _():
        block(text_ref[0],ntext,dtext_ref,tshare_ref[0].astype(jnp.float32))
    @pl.when((j==0)&jnp.logical_not(alive))
    def _():
        dtext_ref[...]=jnp.zeros_like(dtext_ref)

def tokens_back(order,valid,tvalid,tshare,video,text,gain,bias,wkv,wkvt,q,qt,do,dot_,lse,delta,rows):
    clips,span,width=video.shape; lat=q.shape[1]; groups=width//(4*HEAD)
    nb=span//rows
    one=pl.Buffered(1)
    full=lambda a: pl.BlockSpec(a.shape,lambda s,j,*_:(0,)*a.ndim,pipeline_mode=one)
    per=lambda a: pl.BlockSpec((1,)+a.shape[1:],lambda s,j,*_:(s,)+(0,)*(a.ndim-1))
    vspec=pl.BlockSpec((1,rows,width),lambda s,j,o,*_:(o[s],j,0))
    tspec=pl.BlockSpec((1,)+text.shape[1:],lambda s,j,o,*_:(o[s],0,0))
    out_shape=(jax.ShapeDtypeStruct(video.shape,jnp.bfloat16),jax.ShapeDtypeStruct(text.shape,jnp.bfloat16),
       jax.ShapeDtypeStruct((512,width),jnp.float32),jax.ShapeDtypeStruct((clips,3*HEAD,lat),jnp.float32),jax.ShapeDtypeStruct((2,8,width),jnp.float32))
    out_specs=(vspec,tspec,pl.BlockSpec((512,width),lambda s,j,*_:(0,0)),pl.BlockSpec((1,3*HEAD,lat),lambda s,j,*_:(s,0,0)),pl.BlockSpec((2,8,width),lambda s,j,*_:(0,0,0)))
    return pl.pallas_call(tokens_back_kernel,
      grid_spec=pltpu.PrefetchScalarGridSpec(num_scalar_prefetch=4,grid=(clips,nb),
        in_specs=[vspec,tspec,full(gain),full(bias),full(wkv),full(wkvt),per(q),per(qt),per(do),per(dot_),per(lse),per(delta)],
        out_specs=out_specs,
        scratch_shapes=[pltpu.VMEM((groups,4*lat,4*HEAD),jnp.bfloat16),pltpu.VMEM((groups,4*HEAD,4*lat),jnp.bfloat16)]*2),
      out_shape=out_shape,
      compiler_params=pltpu.CompilerParams(vmem_limit_bytes=60*2**20,dimension_semantics=("arbitrary","arbitrary")),
      name="tokens_back",
    )(order,valid,tvalid,tshare,video,text,gain,bias,wkv,wkvt,q,qt,do,dot_,lse,delta)


def head_cat(part, axis):
    n = lax.axis_size("head")
    others = [lax.ppermute(part, "head", [(i, i ^ k) for i in range(n)]) for k in (1, 2, 3)]
    return jnp.concatenate([part] + others, axis)


def on_device(
    latents,
    video_tokens,
    text_tokens,
    frame_counts,
    text_lengths,
    drop_mask,
    cotangent,
    norm_latent_gain,
    norm_latent_bias,
    norm_input_gain,
    norm_input_bias,
    cross_query,
    cross_key,
    cross_value,
    cross_output,
    norm_cross_gain,
    norm_cross_bias,
    cross_up,
    cross_down,
    norm_self_gain,
    norm_self_bias,
    self_query,
    self_key,
    self_value,
    self_output,
    norm_ffn_gain,
    norm_ffn_bias,
    self_up,
    self_down,
):
    clips, lat_rows, width = latents.shape
    span = video_tokens.shape[1]
    text_span = text_tokens.shape[1]
    half_width = cross_key.shape[1]
    self_width = self_query.shape[1]
    keep_clip = (1 - drop_mask).astype(jnp.float32)
    keep = keep_clip[:, None, None]
    positions = lax.axis_index("tok") * span + jnp.arange(span)
    video_valid = positions[None, :] // PATCH < frame_counts[:, None]
    text_valid = jnp.arange(text_span)[None, :] < text_lengths[:, None]
    first_shard = (lax.axis_index("tok") == 0).astype(jnp.float32)
    state = latents.astype(jnp.float32)
    latent_normed, latent_rstd = normalize(state)
    queries_in = (latent_normed * norm_latent_gain + norm_latent_bias).astype(jnp.bfloat16)
    query_heads = split_heads(project(queries_in, cross_query).astype(jnp.bfloat16))
    video_normed, video_rstd = normalize(video_tokens.astype(jnp.float32))
    text_normed, text_rstd = normalize(text_tokens.astype(jnp.float32))
    video_in = (video_normed * norm_input_gain + norm_input_bias).astype(jnp.bfloat16)
    text_in = (text_normed * norm_input_gain + norm_input_bias).astype(jnp.bfloat16)
    key_value = jnp.concatenate([cross_key, cross_value], axis=1)
    video_pair = project(video_in, key_value).astype(jnp.bfloat16)
    text_pair = project(text_in, key_value).astype(jnp.bfloat16)
    video_keys = split_heads(video_pair[..., :half_width])
    video_values = split_heads(video_pair[..., half_width:])
    text_keys = split_heads(text_pair[..., :half_width])
    text_values = split_heads(text_pair[..., half_width:])
    triple = jnp.concatenate([self_query, self_key, self_value], axis=1)
    peak, total, summed = attend_part(query_heads, video_keys, video_values, video_valid)
    peak, total, summed = combined_all((peak, total, summed), "tok", combine_parts)
    peak, total, summed = combine_parts(
        (peak, total, summed), attend_part(query_heads, text_keys, text_values, text_valid)
    )
    cross_attended = summed / total[..., None]
    cross_log_total = peak + jnp.log(total)
    cross_low = cross_attended.reshape(clips, lat_rows, -1).astype(jnp.bfloat16)
    first = state + keep * head_rows(project(cross_low, cross_output))
    cross_mlp, cross_saved = feed_forward(
        first, norm_cross_gain, norm_cross_bias, cross_up, cross_down
    )
    second = first + cross_mlp
    self_normed, self_rstd = normalize(second)
    self_in = (self_normed * norm_self_gain + norm_self_bias).astype(jnp.bfloat16)
    triple_rows = project(self_in, triple).astype(jnp.bfloat16)
    self_q = split_heads(triple_rows[..., :self_width])
    self_k = split_heads(triple_rows[..., self_width : 2 * self_width])
    self_v = split_heads(triple_rows[..., 2 * self_width :])
    all_valid = jnp.ones((clips, lat_rows), dtype=bool)
    self_peak, self_total, self_summed = attend_part(self_q, self_k, self_v, all_valid)
    self_attended = self_summed / self_total[..., None]
    self_log_total = self_peak + jnp.log(self_total)
    self_low = self_attended.reshape(clips, lat_rows, -1).astype(jnp.bfloat16)
    third = second + head_rows(project(self_low, self_output))
    self_mlp, self_saved = feed_forward(third, norm_ffn_gain, norm_ffn_bias, self_up, self_down)
    latents_out = (third + self_mlp).astype(jnp.bfloat16)
    grad = cotangent.astype(jnp.float32)
    grad_third, ffn_gain_grad, ffn_bias_grad, self_ffn_pairs = feed_back(
        grad, self_saved, norm_ffn_gain, self_up, self_down
    )
    self_branch = grad_third.astype(jnp.bfloat16)
    d_self_att = split_heads(project_back(self_branch, self_output).astype(jnp.bfloat16))
    self_delta = jnp.sum(d_self_att.astype(jnp.float32) * self_attended, -1)
    dq_self, dk_self, dv_self = attend_back(
        self_q, self_k, self_v, all_valid, self_log_total, d_self_att, self_delta
    )
    d_triple = jnp.concatenate(
        [
            dq_self.reshape(clips, lat_rows, -1),
            dk_self.reshape(clips, lat_rows, -1),
            dv_self.reshape(clips, lat_rows, -1),
        ],
        axis=-1,
    ).astype(jnp.bfloat16)
    d_self_in = head_grads(project_back(d_triple, triple))
    d_second, self_gain_grad, self_bias_grad = norm_back(
        d_self_in, self_normed, self_rstd, norm_self_gain
    )
    grad_second = grad_third + d_second
    grad_first, cross_gain_grad, cross_bias_grad, cross_ffn_pairs = feed_back(
        grad_second, cross_saved, norm_cross_gain, cross_up, cross_down
    )
    cross_branch = (keep * grad_first).astype(jnp.bfloat16)
    d_cross_att = split_heads(project_back(cross_branch, cross_output).astype(jnp.bfloat16))
    cross_delta = jnp.sum(d_cross_att.astype(jnp.float32) * cross_attended, -1)
    order = jnp.arange(clips, dtype=jnp.int32)
    live = 1 - drop_mask
    shard = lax.axis_index("tok")
    video_count = jnp.clip(frame_counts * PATCH - shard * span, 0, span) * live
    text_count = text_lengths * live
    all_queries = head_cat((query_heads.astype(jnp.float32) / 8.0).astype(jnp.bfloat16).reshape(clips, lat_rows, -1), 2)
    all_d_att = head_cat(d_cross_att.reshape(clips, lat_rows, -1), 2)
    stats = jnp.stack([cross_log_total * LOG2E, cross_delta]).transpose(0, 1, 3, 2)
    stats = head_cat(stats.reshape(2, clips, 1, -1), 3)
    all_key_value = jnp.concatenate([head_cat(cross_key, 1), head_cat(cross_value, 1)], 1)
    text_share = (shard == lax.axis_size("tok") - 1).astype(jnp.int32).reshape(1)
    d_video, d_text, pair_t, dq_t, sums = tokens_back(
        order, video_count, text_count, text_share, video_tokens, text_tokens,
        norm_input_gain[None], norm_input_bias[None], all_key_value, all_key_value.T,
        all_queries, all_queries.swapaxes(1, 2), all_d_att, all_d_att.swapaxes(1, 2),
        stats[0], stats[1], 784 if span % 784 == 0 else span)
    pair_partial = jnp.concatenate([pair_t[:half_width], pair_t[256 : 256 + half_width]], 0).T
    pair_sum, sums = lax.psum((pair_partial, jnp.sum(sums, 1)), ("tok", "mod"))
    input_gain_grad, input_bias_grad = sums[0], sums[1]
    d_query = (
        lax.psum((dq_t.swapaxes(1, 2) * 0.125).astype(jnp.bfloat16), "tok")
    )
    d_queries_in = head_grads(project_back(d_query, cross_query))
    d_latent, latent_gain_grad, latent_bias_grad = norm_back(
        d_queries_in, latent_normed, latent_rstd, norm_latent_gain
    )
    grad_latents = (grad_first + d_latent).astype(jnp.bfloat16)
    cross_inner, cross_d_pre, cross_hidden, cross_grad_low = cross_ffn_pairs
    self_inner, self_d_pre, self_hidden, self_grad_low = self_ffn_pairs
    shares = (
        lax.psum_scatter(
            weight_grad(queries_in, d_query).astype(jnp.bfloat16),
            "mod",
            scatter_dimension=0,
            tiled=True,
        ).astype(jnp.float32),
        lax.psum_scatter(
            weight_grad(cross_low, cross_branch).astype(jnp.bfloat16),
            "mod",
            scatter_dimension=0,
            tiled=True,
        ).astype(jnp.float32),
        lax.psum_scatter(
            weight_grad(cross_inner, cross_d_pre).astype(jnp.bfloat16),
            "mod",
            scatter_dimension=0,
            tiled=True,
        ).astype(jnp.float32),
        lax.psum_scatter(
            weight_grad(cross_hidden, cross_grad_low).astype(jnp.bfloat16),
            "mod",
            scatter_dimension=0,
            tiled=True,
        ).astype(jnp.float32),
        lax.psum_scatter(
            weight_grad(self_in, d_triple).astype(jnp.bfloat16),
            "mod",
            scatter_dimension=0,
            tiled=True,
        ).astype(jnp.float32),
        lax.psum_scatter(
            weight_grad(self_low, self_branch).astype(jnp.bfloat16),
            "mod",
            scatter_dimension=0,
            tiled=True,
        ).astype(jnp.float32),
        lax.psum_scatter(
            weight_grad(self_inner, self_d_pre).astype(jnp.bfloat16),
            "mod",
            scatter_dimension=0,
            tiled=True,
        ).astype(jnp.float32),
        lax.psum_scatter(
            weight_grad(self_hidden, self_grad_low).astype(jnp.bfloat16),
            "mod",
            scatter_dimension=0,
            tiled=True,
        ).astype(jnp.float32),
        lax.psum_scatter(
            latent_gain_grad.astype(jnp.bfloat16), "mod", scatter_dimension=0, tiled=True
        ).astype(jnp.float32),
        lax.psum_scatter(
            latent_bias_grad.astype(jnp.bfloat16), "mod", scatter_dimension=0, tiled=True
        ).astype(jnp.float32),
        lax.psum_scatter(
            cross_gain_grad.astype(jnp.bfloat16), "mod", scatter_dimension=0, tiled=True
        ).astype(jnp.float32),
        lax.psum_scatter(
            cross_bias_grad.astype(jnp.bfloat16), "mod", scatter_dimension=0, tiled=True
        ).astype(jnp.float32),
        lax.psum_scatter(
            self_gain_grad.astype(jnp.bfloat16), "mod", scatter_dimension=0, tiled=True
        ).astype(jnp.float32),
        lax.psum_scatter(
            self_bias_grad.astype(jnp.bfloat16), "mod", scatter_dimension=0, tiled=True
        ).astype(jnp.float32),
        lax.psum_scatter(
            ffn_gain_grad.astype(jnp.bfloat16), "mod", scatter_dimension=0, tiled=True
        ).astype(jnp.float32),
        lax.psum_scatter(
            ffn_bias_grad.astype(jnp.bfloat16), "mod", scatter_dimension=0, tiled=True
        ).astype(jnp.float32),
    )
    summed_grads = (
        lax.all_gather(shares[0].astype(jnp.bfloat16), "mod", axis=0, tiled=True).astype(
            jnp.float32
        ),
        lax.all_gather(shares[1].astype(jnp.bfloat16), "mod", axis=0, tiled=True).astype(
            jnp.float32
        ),
        lax.all_gather(shares[2].astype(jnp.bfloat16), "mod", axis=0, tiled=True).astype(
            jnp.float32
        ),
        lax.all_gather(shares[3].astype(jnp.bfloat16), "mod", axis=0, tiled=True).astype(
            jnp.float32
        ),
        lax.all_gather(shares[4].astype(jnp.bfloat16), "mod", axis=0, tiled=True).astype(
            jnp.float32
        ),
        lax.all_gather(shares[5].astype(jnp.bfloat16), "mod", axis=0, tiled=True).astype(
            jnp.float32
        ),
        lax.all_gather(shares[6].astype(jnp.bfloat16), "mod", axis=0, tiled=True).astype(
            jnp.float32
        ),
        lax.all_gather(shares[7].astype(jnp.bfloat16), "mod", axis=0, tiled=True).astype(
            jnp.float32
        ),
        lax.all_gather(shares[8].astype(jnp.bfloat16), "mod", axis=0, tiled=True).astype(
            jnp.float32
        ),
        lax.all_gather(shares[9].astype(jnp.bfloat16), "mod", axis=0, tiled=True).astype(
            jnp.float32
        ),
        lax.all_gather(shares[10].astype(jnp.bfloat16), "mod", axis=0, tiled=True).astype(
            jnp.float32
        ),
        lax.all_gather(shares[11].astype(jnp.bfloat16), "mod", axis=0, tiled=True).astype(
            jnp.float32
        ),
        lax.all_gather(shares[12].astype(jnp.bfloat16), "mod", axis=0, tiled=True).astype(
            jnp.float32
        ),
        lax.all_gather(shares[13].astype(jnp.bfloat16), "mod", axis=0, tiled=True).astype(
            jnp.float32
        ),
        lax.all_gather(shares[14].astype(jnp.bfloat16), "mod", axis=0, tiled=True).astype(
            jnp.float32
        ),
        lax.all_gather(shares[15].astype(jnp.bfloat16), "mod", axis=0, tiled=True).astype(
            jnp.float32
        ),
    )
    triple_grad = summed_grads[4]
    return (
        latents_out,
        grad_latents,
        d_video,
        d_text,
        summed_grads[8],
        summed_grads[9],
        input_gain_grad,
        input_bias_grad,
        summed_grads[0],
        pair_sum[:, :half_width],
        pair_sum[:, half_width:],
        summed_grads[1],
        summed_grads[10],
        summed_grads[11],
        summed_grads[2],
        summed_grads[3],
        summed_grads[12],
        summed_grads[13],
        triple_grad[:, :self_width],
        triple_grad[:, self_width : 2 * self_width],
        triple_grad[:, 2 * self_width :],
        summed_grads[5],
        summed_grads[14],
        summed_grads[15],
        summed_grads[6],
        summed_grads[7],
    )


def solution(mesh):
    in_specs = (
        P("mod", None, None),
        P("mod", "tok", None),
        P("mod", None, None),
        P("mod"),
        P("mod"),
        P("mod"),
        P("mod", None, None),
        P(),
        P(),
        P(),
        P(),
        P(None, "head"),
        P(None, "head"),
        P(None, "head"),
        P("head", None),
        P(),
        P(),
        P(None, "head"),
        P("head", None),
        P(),
        P(),
        P(None, "head"),
        P(None, "head"),
        P(None, "head"),
        P("head", None),
        P(),
        P(),
        P(None, "head"),
        P("head", None),
    )
    out_specs = (
        P("mod", None, None),
        P("mod", None, None),
        P("mod", "tok", None),
        P("mod", None, None),
        P(),
        P(),
        P(),
        P(),
        P(None, "head"),
        P(None, "head"),
        P(None, "head"),
        P("head", None),
        P(),
        P(),
        P(None, "head"),
        P("head", None),
        P(),
        P(),
        P(None, "head"),
        P(None, "head"),
        P(None, "head"),
        P("head", None),
        P(),
        P(),
        P(None, "head"),
        P("head", None),
    )
    return jax.shard_map(
        on_device, mesh=mesh, in_specs=in_specs, out_specs=out_specs, check_vma=False
    )
```

```python
import jax
import jax.numpy as jnp
from jax import lax
from jax.experimental import pallas as pl
from jax.experimental.pallas import tpu as pltpu
from jax.sharding import PartitionSpec as P

HEAD = 64
PATCH = 392
EPSILON = 1e-05
NEGATIVE = -1e30
LOG2E = 1.4426950408889634
STAT = 16
BF = jnp.bfloat16
F32 = jnp.float32
VMEM_LIMIT = 60 * 2**20


def dot(a, b):
    return jnp.dot(a, b, preferred_element_type=F32)


def dot_tn(a, b):
    return lax.dot_general(a, b, (((0,), (0,)), ((), ())), preferred_element_type=F32)


def dot_nt(a, b):
    return lax.dot_general(a, b, (((1,), (1,)), ((), ())), preferred_element_type=F32)


def normalize(rows):
    mean = jnp.mean(rows, -1, keepdims=True)
    centered = rows - mean
    rstd = lax.rsqrt(jnp.mean(centered * centered, -1, keepdims=True) + EPSILON)
    return centered * rstd, rstd


def normed_rows(rows, gain, bias):
    return (normalize(rows)[0] * gain + bias).astype(BF)


def norm_back(grad_out, rows, gain):
    normed, rstd = normalize(rows)
    scaled = grad_out * gain
    grad_in = rstd * (
        scaled
        - jnp.mean(scaled, -1, keepdims=True)
        - normed * jnp.mean(scaled * normed, -1, keepdims=True)
    )
    return grad_in, jnp.sum(grad_out * normed, 0, keepdims=True), jnp.sum(grad_out, 0, keepdims=True)


def row_sums(a):
    n, width = a.shape
    if n % 8:
        a = jnp.concatenate([a, jnp.zeros((8 - n % 8, width), a.dtype)], 0)
    return jnp.sum(a.reshape(-1, 8, width), 0)


def erf(x):
    x = jnp.clip(x, -4.0, 4.0)
    s = x * x
    top = -2.72614225801306e-10
    for c in (
        2.77068142495902e-08,
        -2.10102402082508e-06,
        -5.69250639462346e-05,
        -7.34990630326855e-04,
        -2.95459980854025e-03,
        -1.60960333262415e-02,
    ):
        top = top * s + c
    low = -1.45660718464996e-05
    for c in (
        -2.13374055278905e-04,
        -1.68282697438203e-03,
        -7.37332916720468e-03,
        -1.42647390514189e-02,
    ):
        low = low * s + c
    return x * top / low


def gelu_share(x):
    return 0.5 * (1.0 + erf(x * 0.7071067811865476))


def gelu_slope(x):
    return gelu_share(x) + x * (0.3989422804014327 * jnp.exp(-0.5 * x * x))


def parts_of(value, count):
    parts = []
    for _ in range(count):
        part = value.astype(BF).astype(F32)
        parts.append(part)
        value = value - part
    return parts


def stat_tile(rows, height):
    place = lax.broadcasted_iota(jnp.int32, (height, rows[0].shape[1]), 0)
    tile = jnp.zeros(place.shape, F32)
    for k, row in enumerate(rows):
        tile = jnp.where(place == k, row, tile)
    return tile.astype(BF)


def diagonal(rows, row_block, column_block, count):
    shape = (row_block * count, column_block * count)
    r = lax.broadcasted_iota(jnp.int32, shape, 0) // row_block
    c = lax.broadcasted_iota(jnp.int32, shape, 1) // column_block
    return jnp.where(r == c, rows, 0.0).astype(BF)


def blocks_down(rows, count):
    return diagonal(jnp.concatenate([rows] * count, 0), rows.shape[0], HEAD, count)


def blocks_across(rows_t, count):
    return diagonal(jnp.concatenate([rows_t] * count, 1), HEAD, rows_t.shape[1], count)


def diagonal_parts(table, lat, count):
    return [
        table[HEAD * h : HEAD * (h + 1), lat * h : lat * (h + 1)] for h in range(count)
    ]


def kernel_call(body, outs, *args, name, scalars=()):
    spec = pl.BlockSpec(memory_space=pltpu.VMEM)
    smem = pl.BlockSpec(memory_space=pltpu.SMEM)
    return pl.pallas_call(
        body,
        out_shape=[jax.ShapeDtypeStruct(s, t) for s, t in outs],
        in_specs=[smem] * len(scalars) + [spec] * len(args),
        out_specs=[spec] * len(outs),
        compiler_params=pltpu.CompilerParams(vmem_limit_bytes=VMEM_LIMIT),
        name=name,
    )(*scalars, *args)


def tokens_forward_kernel(
    clip_ref, count_ref, text_count_ref,
    video_ref, text_ref, latents_ref, lat_gain_ref, lat_bias_ref, gain_ref, bias_ref,
    key_ref, value_ref, query_t_ref,
    out_ref, rows_t_ref,
    blocks, peak, total, summed,
):
    place, j = pl.program_id(0), pl.program_id(1)
    rows = video_ref.shape[1]
    lat = latents_ref.shape[1]
    width = key_ref.shape[1]
    heads = width // HEAD
    count = count_ref[place] - j * rows

    @pl.when(j == 0)
    def _():
        queries_in = normed_rows(latents_ref[0].astype(F32), lat_gain_ref[...], lat_bias_ref[...])
        rows_t = dot_nt(query_t_ref[...], queries_in).astype(BF).astype(F32) * HEAD**-0.5
        rows_t_ref[0] = rows_t.astype(BF)
        blocks[...] = blocks_across(rows_t, heads)
        peak[...] = jnp.full_like(peak, NEGATIVE).astype(BF).astype(F32)
        total[...] = jnp.zeros_like(total)
        summed[...] = jnp.zeros_like(summed)

    def block(x, limit):
        inputs_in = normed_rows(x.astype(F32), gain_ref[...], bias_ref[...])
        key = dot(inputs_in, key_ref[...]).astype(BF)
        value = dot(inputs_in, value_ref[...]).astype(BF)
        mask = lax.broadcasted_iota(jnp.int32, (x.shape[0], 1), 0) < limit
        scores = jnp.where(mask, dot(key, blocks[...]) * LOG2E, NEGATIVE)
        before = peak[...]
        top = jnp.maximum(before, jnp.max(scores, 0, keepdims=True)).astype(BF).astype(F32)
        weights = jnp.exp2(scores - top)
        factor = jnp.exp2(before - top)
        peak[...] = top
        total[...] = total[...] * factor + jnp.sum(weights, 0, keepdims=True)
        table = dot_tn(value, weights.astype(BF))
        for h, part in enumerate(diagonal_parts(table, lat, heads)):
            r = slice(HEAD * h, HEAD * (h + 1))
            summed[r] = summed[r] * factor[:, lat * h : lat * (h + 1)] + part

    @pl.when(count > 0)
    def _():
        block(video_ref[0], count)

    @pl.when((j == 0) & (text_count_ref[place] > 0))
    def _():
        block(text_ref[0], text_count_ref[place])

    @pl.when(j == pl.num_programs(1) - 1)
    def _():
        out_ref[0, :width] = summed[...].astype(BF)
        of = [slice(lat * h, lat * (h + 1)) for h in range(heads)]
        totals = [parts_of(total[:, c], 2) for c in of]
        stats = [peak[:, c] for c in of] + [t[0] for t in totals] + [t[1] for t in totals]
        out_ref[0, width:] = stat_tile(stats, STAT)


def tokens_forward(clip_of, count, text_count, video, text, latents, params, rows):
    clips, span, width = video.shape
    lat = latents.shape[1]
    own = params[-1].shape[0]
    full = lambda a: pl.BlockSpec(a.shape, lambda s, j, *_: (0,) * a.ndim)
    out = lambda height: pl.BlockSpec((1, height, lat), lambda s, j, *_: (s, 0, 0))
    clip_spec = lambda a: pl.BlockSpec((1,) + a.shape[1:], lambda s, j, c, *_: (c[s], 0, 0))
    return pl.pallas_call(
        tokens_forward_kernel,
        grid_spec=pltpu.PrefetchScalarGridSpec(
            num_scalar_prefetch=3,
            grid=(clips, span // rows),
            in_specs=[
                pl.BlockSpec((1, rows, width), lambda s, j, c, *_: (c[s], j, 0)),
                clip_spec(text),
                clip_spec(latents),
            ]
            + [full(a) for a in params],
            out_specs=[out(own + STAT), out(own)],
            scratch_shapes=[
                pltpu.VMEM((own, own // HEAD * lat), BF),
                pltpu.VMEM((1, own // HEAD * lat), F32),
                pltpu.VMEM((1, own // HEAD * lat), F32),
                pltpu.VMEM((own, lat), F32),
            ],
        ),
        out_shape=[
            jax.ShapeDtypeStruct((clips, own + STAT, lat), BF),
            jax.ShapeDtypeStruct((clips, own, lat), BF),
        ],
        compiler_params=pltpu.CompilerParams(
            vmem_limit_bytes=VMEM_LIMIT, dimension_semantics=("arbitrary", "arbitrary")
        ),
        name="tokens_forward",
    )(clip_of, count, text_count, video, text, latents, *params)


GROUP = 4


def tokens_back_kernel(
    clip_ref, query_place_ref, count_ref, text_count_ref, text_share_ref,
    video_ref, text_ref, latents_ref, lat_gain_ref, lat_bias_ref, gain_ref, bias_ref,
    pair_ref, pair_t_ref, q0, q1, q2, q3, d0, d1, d2, d3,
    d_video_ref, d_text_ref, weights_ref, d_query_ref,
    q_down, q_across, d_down, d_across, lse, delta, d_query,
):
    place, j = pl.program_id(0), pl.program_id(1)
    rows, width = video_ref.shape[1:]
    own, lat = q0.shape[1:]
    own_heads = own // HEAD
    groups = width // (GROUP * HEAD)
    count = count_ref[place] - j * rows
    text_count = text_count_ref[place]
    alive = text_count > 0

    @pl.when((place == 0) & (j == 0))
    def _():
        weights_ref[...] = jnp.zeros_like(weights_ref)

    @pl.when(j == 0)
    def _():
        d_query[...] = jnp.zeros_like(d_query)

    @pl.when((j == 0) & alive)
    def _():
        mine = lax.rem(place, 2) == 0
        first = [jnp.where(mine, a[0, :own].astype(F32), b[0, own : 2 * own].astype(F32)) for a, b in ((d0, d2), (d1, d3))]
        second = [jnp.where(mine, a[0, own : 2 * own].astype(F32), b[0, :own].astype(F32)) for a, b in ((d0, d2), (d1, d3))]
        for pieces, down, across in (
            ([q[0].astype(F32) for q in (q0, q1, q2, q3)], q_down, q_across),
            (first + second, d_down, d_across),
        ):
            rows_t = jnp.concatenate(pieces, 0)
            natural = rows_t.T
            for g in range(groups):
                cut = slice(GROUP * HEAD * g, GROUP * HEAD * (g + 1))
                down[g] = blocks_down(natural[:, cut], GROUP)
                across[g] = blocks_across(rows_t[cut], GROUP)
        tiles = [d[0, 2 * own :].astype(F32) for d in (d0, d1, d2, d3)]
        n = 2 * own_heads
        for kind, first_row, count_of in ((delta, 0, 2), (lse, 2 * n, 3)):
            for shard in range(4):
                a, b = tiles[shard % 2], tiles[2 + shard % 2]
                for h in range(own_heads):
                    at_a = first_row + h + own_heads * (shard // 2)
                    at_b = first_row + h + own_heads * (1 - shard // 2)
                    row = sum(
                        jnp.where(mine, a[at_a + n * i : at_a + n * i + 1], b[at_b + n * i : at_b + n * i + 1])
                        for i in range(count_of)
                    )
                    head = shard * own_heads + h
                    kind[:, lat * head : lat * (head + 1)] = row

    def block(x, limit, out_ref, share):
        counted = (lambda a: a) if share is None else (lambda a: a * share)
        normed, rstd = normalize(x.astype(F32))
        inputs_in = (normed * gain_ref[...] + bias_ref[...]).astype(BF)
        key = dot(inputs_in, pair_ref[:, :width]).astype(BF)
        value = dot(inputs_in, pair_ref[:, width:]).astype(BF)
        mask = lax.broadcasted_iota(jnp.int32, (x.shape[0], 1), 0) < limit
        d_keys, d_values = [], []
        for g in range(groups):
            cut = slice(GROUP * HEAD * g, GROUP * HEAD * (g + 1))
            lanes = slice(GROUP * lat * g, GROUP * lat * (g + 1))
            scores = dot(key[:, cut], q_across[g])
            d_probs = dot(value[:, cut], d_across[g])
            probs = jnp.where(mask, jnp.exp2(scores * LOG2E - lse[:, lanes]), 0.0)
            d_scores = (probs * (d_probs - delta[:, lanes])).astype(BF)
            d_values.append(dot(probs.astype(BF), d_down[g]).astype(BF))
            d_keys.append(dot(d_scores, q_down[g]).astype(BF))
            if g == 0:
                table = dot_tn(key[:, cut], d_scores)
                for h, part in enumerate(diagonal_parts(table, lat, own_heads)):
                    d_query[HEAD * h : HEAD * (h + 1)] += counted(part)
        d_key, d_value = jnp.concatenate(d_keys, 1), jnp.concatenate(d_values, 1)
        d_in = dot(d_key, pair_t_ref[:width]) + dot(d_value, pair_t_ref[width:])
        weights_ref[:own] += counted(dot_tn(d_keys[0], inputs_in)[:own])
        weights_ref[own : 2 * own] += counted(dot_tn(d_values[0], inputs_in)[:own])
        weights_ref[3 * own : 3 * own + 8] += counted(row_sums(d_in * normed))
        weights_ref[3 * own + 8 : 3 * own + 16] += counted(row_sums(d_in))
        scaled = d_in * gain_ref[...]
        d_x = rstd * (
            scaled
            - jnp.mean(scaled, -1, keepdims=True)
            - normed * jnp.mean(scaled * normed, -1, keepdims=True)
        )
        out_ref[0] = d_x.astype(BF)

    @pl.when(count > 0)
    def _():
        block(video_ref[0], count, d_video_ref, None)

    @pl.when(count <= 0)
    def _():
        d_video_ref[...] = jnp.zeros_like(d_video_ref)

    @pl.when((j == 0) & alive)
    def _():
        block(text_ref[0], text_count, d_text_ref, text_share_ref[0].astype(F32))

    @pl.when((j == 0) & jnp.logical_not(alive))
    def _():
        d_text_ref[...] = jnp.zeros_like(d_text_ref)

    @pl.when(j == pl.num_programs(1) - 1)
    def _():
        d_rows = (d_query[...] * HEAD**-0.5).astype(BF)
        d_query_ref[0] = d_rows

        @pl.when(alive)
        def _():
            queries_in = normed_rows(
                latents_ref[0].astype(F32), lat_gain_ref[...], lat_bias_ref[...]
            )
            weights_ref[2 * own : 3 * own] += dot(d_rows, queries_in)


WEIGHT_ROWS = 32


def tokens_back(scalars, video, text, latents, params, queries, d_attended, rows):
    clips, span, width = video.shape
    own, lat = queries[0].shape[1:]
    groups = width // (GROUP * HEAD)
    full = lambda a: pl.BlockSpec(
        a.shape, lambda s, j, *_: (0,) * a.ndim, pipeline_mode=pl.Buffered(1)
    )
    clip_spec = lambda a: pl.BlockSpec((1,) + a.shape[1:], lambda s, j, c, *_: (c[s], 0, 0))
    video_spec = pl.BlockSpec((1, rows, width), lambda s, j, c, *_: (c[s], j, 0))
    query_spec = pl.BlockSpec((1, own, lat), lambda s, j, c, q, *_: (q[s], 0, 0))
    d_spec = pl.BlockSpec((1,) + d_attended[0].shape[1:], lambda s, j, *_: (s // 2, 0, 0))
    weight_shape = (3 * own + WEIGHT_ROWS, width)
    return pl.pallas_call(
        tokens_back_kernel,
        grid_spec=pltpu.PrefetchScalarGridSpec(
            num_scalar_prefetch=len(scalars),
            grid=(clips, span // rows),
            in_specs=[video_spec, clip_spec(text), clip_spec(latents)]
            + [full(a) for a in params]
            + [query_spec] * 4
            + [d_spec] * 4,
            out_specs=[
                video_spec,
                clip_spec(text),
                pl.BlockSpec(weight_shape, lambda s, j, *_: (0, 0)),
                pl.BlockSpec((1, own, lat), lambda s, j, *_: (s, 0, 0)),
            ],
            scratch_shapes=[
                pltpu.VMEM((groups, GROUP * lat, GROUP * HEAD), BF),
                pltpu.VMEM((groups, GROUP * HEAD, GROUP * lat), BF),
                pltpu.VMEM((groups, GROUP * lat, GROUP * HEAD), BF),
                pltpu.VMEM((groups, GROUP * HEAD, GROUP * lat), BF),
                pltpu.VMEM((1, groups * GROUP * lat), F32),
                pltpu.VMEM((1, groups * GROUP * lat), F32),
                pltpu.VMEM((own, lat), F32),
            ],
        ),
        out_shape=[
            jax.ShapeDtypeStruct(video.shape, BF),
            jax.ShapeDtypeStruct(text.shape, BF),
            jax.ShapeDtypeStruct(weight_shape, F32),
            jax.ShapeDtypeStruct((clips, own, lat), BF),
        ],
        compiler_params=pltpu.CompilerParams(
            vmem_limit_bytes=VMEM_LIMIT, dimension_semantics=("arbitrary", "arbitrary")
        ),
        name="tokens_back",
    )(*scalars, video, text, latents, *params, *queries, *d_attended)


def combine_kernel(side_ref, *refs):
    parts, mine_ref, other_ref = refs[:-2], refs[-2], refs[-1]
    own = parts[0].shape[1] - STAT
    lat = parts[0].shape[2]
    heads = own // HEAD
    results = []
    for y in range(2):
        tiles = [p[y, own:].astype(F32) for p in parts]
        attended, logs = [], []
        for h in range(heads):
            peaks = [t[h : h + 1] for t in tiles]
            top = peaks[0]
            for p in peaks[1:]:
                top = jnp.maximum(top, p)
            total = jnp.zeros((1, lat), F32)
            summed = jnp.zeros((HEAD, lat), F32)
            for p, t, peak in zip(parts, tiles, peaks):
                factor = jnp.exp2(peak - top)
                a = t[heads + h : heads + h + 1] + t[2 * heads + h : 2 * heads + h + 1]
                total = total + a * factor
                summed = summed + p[y, HEAD * h : HEAD * (h + 1)].astype(F32) * factor
            some = total > 0.0
            safe = jnp.where(some, total, 1.0)
            attended.append(jnp.where(some, summed / safe, 0.0))
            logs.append(parts_of(jnp.where(some, top + jnp.log2(safe), 0.0), 3))
        stats = [logs[h][i] for i in range(3) for h in range(heads)]
        results.append((jnp.concatenate(attended, 0), stat_tile(stats, STAT).astype(F32)))
    first = side_ref[0] == 0
    for ref, (a, b) in ((mine_ref, results), (other_ref, results[::-1])):
        ref[:own] = jnp.where(first, a[0], b[0]).astype(BF)
        ref[own:] = jnp.where(first, a[1], b[1]).astype(BF)


def cross_forward_kernel(
    a0, a1, a2, a3, o0, o1, o2, o3, latents_ref, keep_ref, gain_ref, bias_ref,
    up0, up1, down0, down1,
    first_ref, inner_ref, pre_ref, hidden_ref, part_ref,
):
    own = o0.shape[0]
    branch = sum(dot_tn(a[:own], o[...]) for a, o in ((a0, o0), (a1, o1), (a2, o2), (a3, o3)))
    first = latents_ref[...].astype(F32) + keep_ref[...] * branch
    first_ref[...] = first
    inner = normed_rows(first, gain_ref[...], bias_ref[...])
    inner_ref[...] = inner
    out = None
    for k, (up, down) in enumerate(((up0, down0), (up1, down1))):
        pre = dot(inner, up[...])
        pre_ref[k] = pre
        hidden = (pre * gelu_share(pre)).astype(BF)
        hidden_ref[k] = hidden
        term = dot(hidden, down[...])
        out = term if out is None else out + term
    part_ref[...] = out.astype(BF)


def self_forward_kernel(
    first_ref, part0, part1, gain_ref, bias_ref, w0, w1, wt0, wt1, o0, o1,
    second_ref, inner_ref, rows_ref, query_t_ref, attended_ref, lse_ref, part_ref,
):
    second = first_ref[...] + (part0[...].astype(F32) + part1[...].astype(F32))
    second_ref[...] = second
    inner = normed_rows(second, gain_ref[...], bias_ref[...])
    inner_ref[...] = inner
    lat = inner.shape[0]
    out = None
    for k, (w, wt, o) in enumerate(((w0, wt0, o0), (w1, wt1, o1))):
        own = w.shape[2]
        heads = own // HEAD
        query = (dot(inner, w[0]).astype(BF).astype(F32) * HEAD**-0.5).astype(BF)
        key = dot(inner, w[1]).astype(BF)
        value = dot(inner, w[2]).astype(BF)
        for i, a in enumerate((query, key, value)):
            rows_ref[k, i] = a
        query_t = dot_nt(wt[...], inner).astype(BF).astype(F32) * HEAD**-0.5
        query_t_ref[k] = query_t.astype(BF)
        scores = dot(key, blocks_across(query_t, heads)) * LOG2E
        top = jnp.max(scores, 0, keepdims=True)
        weights = jnp.exp2(scores - top)
        total = jnp.sum(weights, 0, keepdims=True)
        table = dot_tn(value, weights.astype(BF))
        attended = jnp.concatenate(
            [
                part / total[:, lat * h : lat * (h + 1)]
                for h, part in enumerate(diagonal_parts(table, lat, heads))
            ],
            0,
        )
        attended_ref[k] = attended
        lse_ref[k] = top + jnp.log2(total)
        term = dot_tn(attended.astype(BF), o[...])
        out = term if out is None else out + term
    part_ref[...] = out.astype(BF)


def hidden_back(grad_low, pre, inner_parts, up, down):
    d_hidden = dot_nt(grad_low, down[...])
    d_pre = (d_hidden * gelu_slope(pre)).astype(BF)
    return d_pre, dot_nt(d_pre, up[...])


def last_back_kernel(
    second_ref, part0, part1, cotangent_ref, gain_ref, bias_ref, up0, up1, down0, down1,
    third_ref, inner_ref, hidden_ref, d_pre_ref, part_ref,
):
    third = second_ref[...] + (part0[...].astype(F32) + part1[...].astype(F32))
    third_ref[...] = third
    inner = normed_rows(third, gain_ref[...], bias_ref[...])
    inner_ref[...] = inner
    grad_low = cotangent_ref[...]
    out = None
    for k, (up, down) in enumerate(((up0, down0), (up1, down1))):
        pre = dot(inner, up[...])
        hidden_ref[k] = (pre * gelu_share(pre)).astype(BF)
        d_pre, term = hidden_back(grad_low, pre, None, up, down)
        d_pre_ref[k] = d_pre
        out = term if out is None else out + term
    part_ref[...] = out.astype(BF)


def down_kernel(hidden_ref, down0, down1, part_ref):
    part_ref[...] = (dot(hidden_ref[0], down0[...]) + dot(hidden_ref[1], down1[...])).astype(BF)


def self_back_kernel(
    cotangent_ref, third_ref, part0, part1, gain_ref,
    rows_ref, query_t_ref, attended_ref, lse_ref, w0, w1, o0, o1,
    grad_ref, sums_ref, branch_ref, d_rows_ref, low_ref, part_ref,
):
    d_inner = part0[...].astype(F32) + part1[...].astype(F32)
    d_x, d_gain, d_bias = norm_back(d_inner, third_ref[...], gain_ref[...])
    grad = cotangent_ref[...].astype(F32) + d_x
    grad_ref[...] = grad
    sums_ref[0:1] = d_gain
    sums_ref[1:2] = d_bias
    branch = grad.astype(BF)
    branch_ref[...] = branch
    lat = grad.shape[0]
    out = None
    for k, (w, o) in enumerate(((w0, o0), (w1, o1))):
        own = w.shape[2]
        heads = own // HEAD
        query, key, value = rows_ref[k, 0], rows_ref[k, 1], rows_ref[k, 2]
        d_att = dot_nt(branch, o[...]).astype(BF).astype(F32)
        d_att_t = dot_nt(o[...], branch).astype(BF).astype(F32)
        attended = attended_ref[k]
        low_ref[k] = attended.astype(BF)
        product = d_att_t * attended
        delta = jnp.concatenate(
            [
                jnp.sum(product[HEAD * h : HEAD * (h + 1)], 0, keepdims=True)
                for h in range(heads)
            ],
            1,
        )
        scores = dot(key, blocks_across(query_t_ref[k].astype(F32), heads))
        d_probs = dot(value, blocks_across(d_att_t, heads))
        probs = jnp.exp2(scores * LOG2E - lse_ref[k])
        d_scores = (probs * (d_probs - delta)).astype(BF)
        d_value = dot(probs.astype(BF), blocks_down(d_att, heads)).astype(BF)
        d_key = dot(d_scores, blocks_down(query.astype(F32), heads)).astype(BF)
        table = dot_tn(d_scores, key)
        column = lax.broadcasted_iota(jnp.int32, (lat, own), 1) // HEAD
        d_query = sum(
            jnp.where(column == h, table[lat * h : lat * (h + 1)], 0.0) for h in range(heads)
        )
        d_query = (d_query * HEAD**-0.5).astype(BF)
        for i, a in enumerate((d_query, d_key, d_value)):
            d_rows_ref[k, i] = a
            term = dot_nt(a, w[i])
            out = term if out is None else out + term
    part_ref[...] = out.astype(BF)


def cross_back_kernel(
    grad_ref, second_ref, part0, part1, gain_ref, pre_ref, up0, up1, down0, down1,
    out_ref, sums_ref, low_ref, d_pre_ref, part_ref,
):
    d_inner = part0[...].astype(F32) + part1[...].astype(F32)
    d_x, d_gain, d_bias = norm_back(d_inner, second_ref[...], gain_ref[...])
    grad = grad_ref[...] + d_x
    out_ref[...] = grad
    sums_ref[0:1] = d_gain
    sums_ref[1:2] = d_bias
    grad_low = grad.astype(BF)
    low_ref[...] = grad_low
    out = None
    for k, (up, down) in enumerate(((up0, down0), (up1, down1))):
        d_pre, term = hidden_back(grad_low, pre_ref[k], None, up, down)
        d_pre_ref[k] = d_pre
        out = term if out is None else out + term
    part_ref[...] = out.astype(BF)


def attended_back_kernel(
    grad_ref, first_ref, part0, part1, gain_ref, keep_ref, a0, a2, o0, o2,
    out_ref, sums_ref, branch_ref, packed_ref,
):
    d_inner = part0[...].astype(F32) + part1[...].astype(F32)
    d_x, d_gain, d_bias = norm_back(d_inner, first_ref[...], gain_ref[...])
    grad = grad_ref[...] + d_x
    out_ref[...] = grad
    sums_ref[0:1] = d_gain
    sums_ref[1:2] = d_bias
    branch = (keep_ref[...] * grad).astype(BF)
    branch_ref[...] = branch
    own = o0.shape[0]
    heads = own // HEAD
    deltas, logs = [], []
    for k, (a, o) in enumerate(((a0, o0), (a2, o2))):
        d_att_t = dot_nt(o[...], branch).astype(BF)
        packed_ref[own * k : own * (k + 1)] = d_att_t
        product = d_att_t.astype(F32) * a[:own].astype(F32)
        tile = a[own:].astype(F32)
        for h in range(heads):
            deltas.append(
                parts_of(jnp.sum(product[HEAD * h : HEAD * (h + 1)], 0, keepdims=True), 2)
            )
            logs.append([tile[heads * i + h : heads * i + h + 1] for i in range(3)])
    rows = [d[i] for i in range(2) for d in deltas] + [g[i] for i in range(3) for g in logs]
    packed_ref[2 * own :] = stat_tile(rows, 2 * STAT)


def latent_back_kernel(
    grad_ref, latents_ref, gain_ref, d0, d1, d2, d3, query_t_ref, out_ref, sums_ref
):
    own = d0.shape[0]
    d_in = sum(
        dot_tn(d[...], query_t_ref[own * k : own * (k + 1)]) for k, d in enumerate((d0, d1, d2, d3))
    )
    d_x, d_gain, d_bias = norm_back(d_in, latents_ref[...].astype(F32), gain_ref[...])
    out_ref[...] = (grad_ref[...] + d_x).astype(BF)
    sums_ref[0:1] = d_gain
    sums_ref[1:2] = d_bias


def weight_grads_kernel(*refs):
    count = len(refs) // 5
    for k in range(count):
        a0, b0, a1, b1 = refs[4 * k : 4 * k + 4]
        refs[4 * count + k][...] = (dot_tn(a0[...], b0[...]) + dot_tn(a1[...], b1[...])).astype(BF)


def weight_grads(pairs, name):
    outs = [((a0.shape[1], b0.shape[1]), BF) for a0, b0, a1, b1 in pairs]
    return kernel_call(
        weight_grads_kernel, outs, *[a for pair in pairs for a in pair], name=name
    )


def head_move(x, k):
    n = lax.axis_size("head")
    return lax.ppermute(x, "head", [(i, i ^ k) for i in range(n)])


def mod_move(x):
    return lax.ppermute(x, "mod", [(0, 1), (1, 0)])


def tok_move(x, shift):
    n = lax.axis_size("tok")
    return lax.ppermute(x, "tok", [(i, (i - shift) % n) for i in range(n)])


def after(x, *earlier):
    return lax.optimization_barrier((x, *earlier))[0]


def shared_head_move(x, k, axis):
    mod = lax.axis_index("mod")
    half = x.shape[axis] // 2
    part = head_move(lax.dynamic_slice_in_dim(x, mod * half, half, axis), k)
    other = mod_move(part)
    low = jnp.where(mod == 0, part, other)
    high = jnp.where(mod == 0, other, part)
    return jnp.concatenate([low, high], axis), part


def gather_latent_rows(rows, side_x):
    stages = jnp.stack([rows] + [tok_move(rows, k) for k in range(1, 4)])
    same, up, across = (head_move(stages, k) for k in (1, 2, 3))
    pick = lambda a, b: jnp.where(side_x == 0, a, b)
    mine = jnp.stack([pick(stages, same), pick(same, stages)], 1)
    other = jnp.stack([pick(up, across), pick(across, up)], 1)
    return jnp.stack([mine, other], 1)


def sum_over_tok_mod(x):
    n = lax.axis_size("tok")
    mod, tok = lax.axis_index("mod"), lax.axis_index("tok")
    half = x.shape[1] // 2
    low, high = x[:, :half], x[:, half:]
    own = jnp.where(mod == 0, low, high)
    own = own + mod_move(jnp.where(mod == 0, high, low).astype(BF)).astype(F32)
    if n != 4:
        own = lax.psum(own.astype(BF), "tok")
    else:
        step = x.shape[0] // n
        cut = lambda k: lax.dynamic_slice_in_dim(own, lax.rem(tok + k, n) * step, step, 0)
        received = [tok_move(cut(n - k).astype(BF), k) for k in range(1, n)]
        share = (cut(0) + sum(r.astype(F32) for r in received)).astype(BF)
        shares = [share] + [tok_move(share, k) for k in range(1, n)]
        own = jnp.zeros((x.shape[0], half), BF)
        for k, s in enumerate(shares):
            own = lax.dynamic_update_slice_in_dim(own, s, lax.rem(tok + k, n) * step, 0)
    other = mod_move(own)
    low = jnp.where(mod == 0, own, other)
    high = jnp.where(mod == 0, other, own)
    return jnp.concatenate([low, high], 1).astype(F32)


def on_device(
    latents,
    video_tokens,
    text_tokens,
    frame_counts,
    text_lengths,
    drop_mask,
    cotangent,
    norm_latent_gain,
    norm_latent_bias,
    norm_input_gain,
    norm_input_bias,
    cross_query,
    cross_key,
    cross_value,
    cross_output,
    norm_cross_gain,
    norm_cross_bias,
    cross_up,
    cross_down,
    norm_self_gain,
    norm_self_bias,
    self_query,
    self_key,
    self_value,
    self_output,
    norm_ffn_gain,
    norm_ffn_bias,
    self_up,
    self_down,
):
    clips, lat, width = latents.shape
    span = video_tokens.shape[1]
    own = cross_key.shape[1]
    shards = lax.axis_size("tok")
    zones = clips // 2
    tok, mod, head = lax.axis_index("tok"), lax.axis_index("mod"), lax.axis_index("head")
    zone = lax.rem(tok, zones)
    side_x, side_y = lax.rem(head, 2), head // 2
    rows = 784 if span % 784 == 0 else span
    row = lambda v: v[None]

    numbers = jnp.arange(clips, dtype=jnp.int32)
    live = 1 - drop_mask
    sort_key = drop_mask * clips + numbers
    rank = jnp.sum((sort_key[None, :] < sort_key[:, None]).astype(jnp.int32), 1)
    order = jnp.sum(jnp.where(rank[None, :] == numbers[:, None], numbers[None, :], 0), 1)
    pick = lambda table, at: jnp.sum(
        jnp.where(at[:, None] == numbers[None, :], table[None, :], 0), 1
    ).astype(jnp.int32)
    zone_of_place = lax.rem(zone + numbers // 2, zones)
    clip_plain = pick(order, 2 * zone_of_place + numbers % 2)
    query_place = 2 * (numbers // 2) + (numbers % 2 + side_y) % 2
    clip_place = pick(clip_plain, query_place)
    place_of_clip = jnp.sum(
        jnp.where(clip_place[None, :] == numbers[:, None], numbers[None, :], 0), 1
    )
    my_clip = clip_place[0]
    video_count = jnp.clip(frame_counts * PATCH - tok * span, 0, span) * live
    text_count = text_lengths * live
    last = (tok == shards - 1).astype(jnp.int32)

    my_latents = lax.dynamic_index_in_dim(latents, my_clip, 0, False)
    my_cotangent = lax.dynamic_index_in_dim(cotangent, my_clip, 0, False)
    other_cotangent = lax.dynamic_index_in_dim(cotangent, clip_place[1], 0, False)
    keep = lax.dynamic_index_in_dim(live, my_clip, 0, False).astype(F32) * jnp.ones((1, width), F32)

    outputs = [cross_output] + [head_move(cross_output, k) for k in (1, 2, 3)]
    cross_up_y, sent = shared_head_move(after(cross_up, *outputs), 2, 1)
    cross_down_y, sent = shared_head_move(after(cross_down, sent), 2, 0)
    self_w = jnp.stack([self_query, self_key, self_value])
    self_w_y, sent = shared_head_move(after(self_w, sent), 2, 1)
    self_output_y, sent = shared_head_move(after(self_output, sent), 2, 1)
    self_up_y, sent = shared_head_move(after(self_up, sent), 2, 1)
    self_down_y, sent = shared_head_move(after(self_down, sent), 2, 0)
    tables_t = jnp.stack([cross_key.T, cross_value.T, cross_query.T])
    others = []
    for k in (1, 2, 3):
        moved, sent = shared_head_move(after(tables_t, sent), k, 2)
        others.append(moved)
    tables = jnp.concatenate([tables_t] + others, 1)
    pair_t = tables[:2].reshape(2 * width, width)
    pair = pair_t.T
    all_query_t = tables[2]

    partial, query_t = tokens_forward(
        clip_plain, pick(video_count, clip_plain), pick(text_count, clip_plain) * last,
        video_tokens, text_tokens, latents,
        (row(norm_latent_gain), row(norm_latent_bias), row(norm_input_gain), row(norm_input_bias),
         cross_key, cross_value, cross_query.T),
        rows,
    )
    partial = partial.reshape(zones, 2, *partial.shape[1:])
    received = [tok_move(partial[(-k) % zones], k) for k in range(1, shards)]
    mine, other = kernel_call(
        combine_kernel, [(partial.shape[2:], BF)] * 2, partial[0], *received,
        name="combine", scalars=(side_y.reshape(1),),
    )
    attended = [mine, head_move(mine, 1), head_move(other, 2), head_move(other, 3)]
    queries = [query_t] + [head_move(after(query_t, attended[3]), k) for k in (1, 2, 3)]

    lw = (lat, width)
    first, inner1, pre1, hidden1, part = kernel_call(
        cross_forward_kernel,
        [(lw, F32), (lw, BF), ((2,) + lw, F32), ((2,) + lw, BF), (lw, BF)],
        *attended, *outputs, my_latents, keep, row(norm_cross_gain), row(norm_cross_bias),
        cross_up, cross_up_y, cross_down, cross_down_y, name="cross_forward",
    )
    heads = own // HEAD
    second, self_in, self_rows, self_query_t, self_attended, self_lse, part = kernel_call(
        self_forward_kernel,
        [(lw, F32), (lw, BF), ((2, 3, lat, own), BF), ((2, own, lat), BF), ((2, own, lat), F32),
         ((2, 1, heads * lat), F32), (lw, BF)],
        first, part, head_move(part, 1), row(norm_self_gain), row(norm_self_bias),
        self_w, self_w_y, self_query.T, self_w_y[0].T, self_output, self_output_y,
        name="self_forward",
    )
    third, inner2, hidden2, d_pre2, part = kernel_call(
        last_back_kernel,
        [(lw, F32), (lw, BF), ((2,) + lw, BF), ((2,) + lw, BF), (lw, BF)],
        second, part, head_move(part, 1), my_cotangent, row(norm_ffn_gain), row(norm_ffn_bias),
        self_up, self_up_y, self_down, self_down_y, name="last_back",
    )
    received = head_move(part, 1)
    (out_part,) = kernel_call(
        down_kernel, [(lw, BF)], after(hidden2, part), self_down, self_down_y, name="down"
    )
    grad_third, ffn_sums, self_branch, self_d_rows, self_low, part = kernel_call(
        self_back_kernel,
        [(lw, F32), ((2, width), F32), (lw, BF), ((2, 3, lat, own), BF), ((2, own, lat), BF), (lw, BF)],
        my_cotangent, third, part, received, row(norm_ffn_gain),
        self_rows, self_query_t, self_attended, self_lse, self_w, self_w_y, self_output, self_output_y,
        name="self_back",
    )
    grad_second, self_sums, low1, d_pre1, part = kernel_call(
        cross_back_kernel,
        [(lw, F32), ((2, width), F32), (lw, BF), ((2,) + lw, BF), (lw, BF)],
        grad_third, second, part, head_move(part, 1), row(norm_self_gain), pre1,
        cross_up, cross_up_y, cross_down, cross_down_y, name="cross_back",
    )
    grad_first, cross_sums, cross_branch, packed = kernel_call(
        attended_back_kernel,
        [(lw, F32), ((2, width), F32), (lw, BF), ((2 * own + 2 * STAT, lat), BF)],
        grad_second, first, part, head_move(part, 1), row(norm_cross_gain), keep,
        attended[0], attended[2], outputs[0], outputs[2], name="attended_back",
    )

    stages = jnp.stack([packed] + [tok_move(packed, k) for k in range(1, 4)])
    d_attended = [stages] + [head_move(stages, k) for k in (1, 2, 3)]
    d_video, d_text, token_weights, d_query_t = tokens_back(
        (clip_place, query_place, pick(video_count, clip_place), pick(text_count, clip_place),
         last.reshape(1)),
        video_tokens, text_tokens, latents,
        (row(norm_latent_gain), row(norm_latent_bias), row(norm_input_gain), row(norm_input_bias),
         pair, pair_t),
        queries, d_attended, rows,
    )

    out_rows = third + (out_part.astype(F32) + head_move(out_part, 1).astype(F32))
    half_of = lambda a: lax.dynamic_slice_in_dim(a, side_x * (lat // 2), lat // 2, 0)
    in_clip_order = lambda a: jnp.take(a.reshape(clips, lat, width), place_of_clip, axis=0)
    latents_out = in_clip_order(gather_latent_rows(half_of(out_rows).astype(BF), side_x))

    move_y = lambda a: head_move(a, 2)
    up2, down2 = weight_grads(
        [(inner2, d_pre2[0], move_y(inner2), move_y(d_pre2[1])),
         (hidden2[0], my_cotangent, move_y(hidden2[1]), other_cotangent)], "last_weights",
    )
    self_in_y, branch_y = move_y(self_in), move_y(self_branch)
    d_rows_y, low_y = move_y(self_d_rows[1]), move_y(self_low[1])
    wq, wk, wv, wo = weight_grads(
        [(self_in, self_d_rows[0, i], self_in_y, d_rows_y[i]) for i in range(3)]
        + [(self_low[0].T, self_branch, low_y.T, branch_y)], "self_weights",
    )
    up1, down1, co = weight_grads(
        [(inner1, d_pre1[0], move_y(inner1), move_y(d_pre1[1])),
         (hidden1[0], low1, move_y(hidden1[1]), move_y(low1)),
         (mine[:own].T, cross_branch, other[:own].T, move_y(cross_branch))], "cross_weights",
    )
    if shards > zones:
        counts = tok < zones
        up1, down1, co, wq, wk, wv, wo, up2, down2 = (
            jnp.where(counts, a, 0) for a in (up1, down1, co, wq, wk, wv, wo, up2, down2)
        )
    both = ("tok", "mod")
    up2, down2 = lax.psum((up2, down2), both)
    wq, wk, wv, wo = lax.psum(after((wq, wk, wv, wo), up2), both)
    up1, down1, co = lax.psum(after((up1, down1, co), wq), both)

    d_query_t = d_query_t.reshape(zones, 2, own, lat)
    received = [tok_move(d_query_t[(-k) % zones], k) for k in range(1, shards)]
    d_query = (d_query_t[0].astype(F32) + sum(r.astype(F32) for r in received)).astype(BF)
    d_queries = [d_query[0], head_move(d_query[0], 1), head_move(d_query[1], 2), head_move(d_query[1], 3)]
    my_grad, latent_sums = kernel_call(
        latent_back_kernel, [(lw, BF), ((2, width), F32)],
        grad_first, my_latents, row(norm_latent_gain), *d_queries, all_query_t, name="latent_back",
    )
    norm_sums = jnp.concatenate(
        [latent_sums, cross_sums, self_sums, ffn_sums, jnp.zeros((8, width), F32)], 0
    )
    gathered = gather_latent_rows(
        jnp.concatenate([half_of(my_grad), norm_sums.astype(BF)], 0), side_x
    )
    grad_latents = in_clip_order(gathered[:, :, :, : lat // 2])
    norm_sums = jnp.sum(gathered[:, :, 0, lat // 2 : lat // 2 + 8].astype(F32), (0, 1))
    norm_sums = norm_sums + mod_move(norm_sums)
    token_weights = sum_over_tok_mod(token_weights)
    input_sums = jnp.sum(token_weights[3 * own : 3 * own + 16].reshape(2, 8, width), 1)
    f32 = lambda a: a.astype(F32)
    return (
        latents_out,
        grad_latents,
        d_video,
        d_text,
        norm_sums[0],
        norm_sums[1],
        input_sums[0],
        input_sums[1],
        token_weights[2 * own : 3 * own].T,
        token_weights[:own].T,
        token_weights[own : 2 * own].T,
        f32(co),
        norm_sums[2],
        norm_sums[3],
        f32(up1),
        f32(down1),
        norm_sums[4],
        norm_sums[5],
        f32(wq),
        f32(wk),
        f32(wv),
        f32(wo),
        norm_sums[6],
        norm_sums[7],
        f32(up2),
        f32(down2),
    )


def solution(mesh):
    in_specs = (
        P("mod", None, None),
        P("mod", "tok", None),
        P("mod", None, None),
        P("mod"),
        P("mod"),
        P("mod"),
        P("mod", None, None),
        P(),
        P(),
        P(),
        P(),
        P(None, "head"),
        P(None, "head"),
        P(None, "head"),
        P("head", None),
        P(),
        P(),
        P(None, "head"),
        P("head", None),
        P(),
        P(),
        P(None, "head"),
        P(None, "head"),
        P(None, "head"),
        P("head", None),
        P(),
        P(),
        P(None, "head"),
        P("head", None),
    )
    out_specs = (
        P("mod", None, None),
        P("mod", None, None),
        P("mod", "tok", None),
        P("mod", None, None),
        P(),
        P(),
        P(),
        P(),
        P(None, "head"),
        P(None, "head"),
        P(None, "head"),
        P("head", None),
        P(),
        P(),
        P(None, "head"),
        P("head", None),
        P(),
        P(),
        P(None, "head"),
        P(None, "head"),
        P(None, "head"),
        P("head", None),
        P(),
        P(),
        P(None, "head"),
        P("head", None),
    )
    return jax.shard_map(
        on_device, mesh=mesh, in_specs=in_specs, out_specs=out_specs, check_vma=False
    )
```

```python
import functools

import jax
import jax.numpy as jnp
from jax import lax
from jax.experimental import pallas as pl
from jax.experimental.pallas import tpu as pltpu
from jax.sharding import PartitionSpec as P

HEAD = 64
PATCH = 392
EPSILON = 1e-05
NEGATIVE = -1e30
LOG2E = 1.4426950408889634
STAT = 16
BF = jnp.bfloat16
F32 = jnp.float32
VMEM_LIMIT = 60 * 2**20
SIDE_X, SIDE_Y, MOD = range(3)


def dot(a, b):
    return jnp.dot(a, b, preferred_element_type=F32)


def dot_tn(a, b):
    return lax.dot_general(a, b, (((0,), (0,)), ((), ())), preferred_element_type=F32)


def dot_nt(a, b):
    return lax.dot_general(a, b, (((1,), (1,)), ((), ())), preferred_element_type=F32)


def normalize(rows):
    mean = jnp.mean(rows, -1, keepdims=True)
    centered = rows - mean
    rstd = lax.rsqrt(jnp.mean(centered * centered, -1, keepdims=True) + EPSILON)
    return centered * rstd, rstd


def normed_rows(rows, gain, bias):
    return (normalize(rows)[0] * gain + bias).astype(BF)


def norm_back(grad_out, rows, gain):
    normed, rstd = normalize(rows)
    scaled = grad_out * gain
    grad_in = rstd * (
        scaled
        - jnp.mean(scaled, -1, keepdims=True)
        - normed * jnp.mean(scaled * normed, -1, keepdims=True)
    )
    return grad_in, jnp.sum(grad_out * normed, 0, keepdims=True), jnp.sum(grad_out, 0, keepdims=True)


def row_sums(a):
    n, width = a.shape
    if n % 8:
        a = jnp.concatenate([a, jnp.zeros((8 - n % 8, width), a.dtype)], 0)
    return jnp.sum(a.reshape(-1, 8, width), 0)


def erf(x):
    x = jnp.clip(x, -4.0, 4.0)
    s = x * x
    top = -2.72614225801306e-10
    for c in (
        2.77068142495902e-08,
        -2.10102402082508e-06,
        -5.69250639462346e-05,
        -7.34990630326855e-04,
        -2.95459980854025e-03,
        -1.60960333262415e-02,
    ):
        top = top * s + c
    low = -1.45660718464996e-05
    for c in (
        -2.13374055278905e-04,
        -1.68282697438203e-03,
        -7.37332916720468e-03,
        -1.42647390514189e-02,
    ):
        low = low * s + c
    return x * top / low


def gelu_share(x):
    return 0.5 * (1.0 + erf(x * 0.7071067811865476))


def gelu_slope(x):
    return gelu_share(x) + x * (0.3989422804014327 * jnp.exp(-0.5 * x * x))


def parts_of(value, count):
    parts = []
    for _ in range(count):
        part = value.astype(BF).astype(F32)
        parts.append(part)
        value = value - part
    return parts


def stat_tile(rows, height):
    place = lax.broadcasted_iota(jnp.int32, (height, rows[0].shape[1]), 0)
    tile = jnp.zeros(place.shape, F32)
    for k, row in enumerate(rows):
        tile = jnp.where(place == k, row, tile)
    return tile.astype(BF)


def diagonal(rows, row_block, column_block, count):
    shape = (row_block * count, column_block * count)
    r = lax.broadcasted_iota(jnp.int32, shape, 0) // row_block
    c = lax.broadcasted_iota(jnp.int32, shape, 1) // column_block
    return jnp.where(r == c, rows, 0.0).astype(BF)


def blocks_down(rows, count):
    return diagonal(jnp.concatenate([rows] * count, 0), rows.shape[0], HEAD, count)


def blocks_across(rows_t, count):
    return diagonal(jnp.concatenate([rows_t] * count, 1), HEAD, rows_t.shape[1], count)


def diagonal_parts(table, lat, count):
    return [
        table[HEAD * h : HEAD * (h + 1), lat * h : lat * (h + 1)] for h in range(count)
    ]


def cost_of(us):
    return pl.CostEstimate(flops=int(us * 1e9), bytes_accessed=0, transcendentals=0)


NO_COST = cost_of(0)


def kernel_call(body, outs, *args, name, scalars=(), scratch=(), deps=(), beside=0.0):
    spec = pl.BlockSpec(memory_space=pltpu.VMEM)
    smem = pl.BlockSpec(memory_space=pltpu.SMEM)
    first, count = len(scalars) + len(args), len(deps)
    return pl.pallas_call(
        lambda *refs: body(*refs[:first], *refs[first + count :]),
        out_shape=[jax.ShapeDtypeStruct(s, t) for s, t in outs],
        in_specs=[smem] * len(scalars)
        + [spec] * len(args)
        + [pl.BlockSpec(memory_space=pl.ANY)] * len(deps),
        out_specs=[spec] * len(outs),
        scratch_shapes=[pltpu.VMEM(s, t) for s, t in scratch],
        compiler_params=pltpu.CompilerParams(vmem_limit_bytes=VMEM_LIMIT),
        cost_estimate=cost_of(beside),
        name=name,
    )(*scalars, *args, *deps)


def tie(x, *deps):
    anywhere = pl.BlockSpec(memory_space=pl.ANY)
    return pl.pallas_call(
        lambda *refs: None,
        out_shape=jax.ShapeDtypeStruct(x.shape, x.dtype),
        in_specs=[anywhere] * (1 + len(deps)),
        out_specs=anywhere,
        input_output_aliases={0: 0},
        cost_estimate=NO_COST,
        name="tie",
    )(x, *deps)


def stack_kernel(*refs):
    for k, ref in enumerate(refs[:-1]):
        refs[-1][k] = ref[...]


def concat_kernel(*refs):
    row = 0
    for ref in refs[:-1]:
        refs[-1][row : row + ref.shape[0]] = ref[...]
        row += ref.shape[0]


def join_halves(target, part, other, mod, at, n):
    target[pl.ds(pl.multiple_of(mod * n, 16), n)] = part[at : at + n]
    target[pl.ds(pl.multiple_of((1 - mod) * n, 16), n)] = other[at : at + n]


def pack_kernel(plan, *refs, counts):
    outs = refs[-len(counts) :]
    at = 0
    for out, count in zip(outs, counts):
        row = 0
        for ref in refs[at : at + count]:
            out[row : row + ref.shape[0]] = ref[...]
            row += ref.shape[0]
        at += count


def pack_halves(at, plan, groups):
    arrays = [a for g in groups for a in g]
    spec = lambda a: pl.BlockSpec((a.shape[0] // 2, a.shape[1]), lambda i, p: (p[at.mod], 0))
    shapes = [(sum(a.shape[0] // 2 for a in g), g[0].shape[1]) for g in groups]
    return pl.pallas_call(
        functools.partial(pack_kernel, counts=[len(g) for g in groups]),
        grid_spec=pltpu.PrefetchScalarGridSpec(
            num_scalar_prefetch=1,
            grid=(1,),
            in_specs=[spec(a) for a in arrays],
            out_specs=[pl.BlockSpec(s, lambda i, m: (0, 0)) for s in shapes],
        ),
        out_shape=[jax.ShapeDtypeStruct(s, BF) for s in shapes],
        compiler_params=pltpu.CompilerParams(vmem_limit_bytes=VMEM_LIMIT),
        cost_estimate=NO_COST,
        name="pack_halves",
    )(plan, *arrays)


def tables_kernel(plan, gathered_ref, pair_ref, pair_t_ref, query_t_ref):
    parts, _, rows, width = gathered_ref.shape
    own = parts * rows // 3
    for k in range(4):
        x, y = lax.rem(plan[SIDE_X] + k % 2, 2), lax.rem(plan[SIDE_Y] + k // 2, 2)
        shard = 2 * y + x
        for i, (target, start) in enumerate(((pair_t_ref, 0), (pair_t_ref, width), (query_t_ref, 0))):
            for p in range(parts):
                low, high = max(own * i, rows * p), min(own * (i + 1), rows * (p + 1))
                if low < high:
                    to = start + own * k + low - own * i
                    target[to : to + high - low] = gathered_ref[
                        p, shard, low - rows * p : high - rows * p
                    ]
    for c in range(0, 2 * width, 256):
        pair_ref[:, c : c + 256] = pair_t_ref[c : c + 256].astype(F32).T.astype(BF)


class Plan:
    def __init__(self, clips, blocks):
        steps = clips * blocks
        self.clips, self.blocks, self.size = clips, blocks, 0
        for name, length in (
            ("side_x", 1), ("side_y", 1), ("mod", 1), ("share", 1), ("some", 2), ("keep", 1), ("tok", 1),
            ("clip_plain", clips), ("count_plain", clips), ("text_plain", clips),
            ("read_clip", steps), ("read_block", steps), ("zero_clip", steps), ("zero_block", steps),
            ("clip", clips), ("count", clips), ("text", clips),
            ("back_clip", steps), ("back_block", steps),
        ):
            setattr(self, name, self.size)
            self.size += length

    def calls(self):
        return ((0, 1), (1, self.clips - 1))


def plan_kernel(place_ref, frames_ref, lengths_ref, drop_ref, plan, order, *, at, rows, span):
    clips, blocks = at.clips, at.blocks
    zones = clips // 2
    tok, side_x, side_y, mod, last = (place_ref[i] for i in range(5))
    zone = lax.rem(tok, zones)
    plan[at.side_x], plan[at.side_y], plan[at.mod], plan[at.share] = side_x, side_y, mod, last
    plan[at.tok] = tok
    drops = [drop_ref[c] for c in range(clips)]
    for c in range(clips):
        rank = sum(
            (drops[o] < drops[c]).astype(jnp.int32)
            if o > c
            else (drops[o] <= drops[c]).astype(jnp.int32)
            for o in range(clips)
            if o != c
        )
        order[rank] = c

    def tables(side, clip_at, count_at, text_at, share):
        flags = []
        for p in range(clips):
            clip = order[2 * lax.rem(zone + p // 2, zones) + lax.rem(p + side, 2)]
            live = 1 - drop_ref[clip]
            count = jnp.clip(frames_ref[clip] * PATCH - tok * span, 0, span) * live
            plan[clip_at + p] = clip
            plan[count_at + p] = count
            plan[text_at + p] = lengths_ref[clip] * live * share
            flags += [((count > b * rows).astype(jnp.int32), clip, b) for b in range(blocks)]
        return flags

    def hold(flags, wanted, clip_at, block_at):
        clip, block = flags[0][1], jnp.int32(0)
        for flag, c, b in flags[::-1]:
            clip = jnp.where(flag == wanted, c, clip)
            block = jnp.where(flag == wanted, b, block)
        for i, (flag, c, b) in enumerate(flags):
            clip = jnp.where(flag == wanted, c, clip)
            block = jnp.where(flag == wanted, b, block)
            plan[clip_at + i] = clip
            plan[block_at + i] = block

    flags = tables(0, at.clip_plain, at.count_plain, at.text_plain, last)
    hold(flags, 1, at.read_clip, at.read_block)
    hold(flags, 0, at.zero_clip, at.zero_block)
    flags = tables(side_y, at.clip, at.count, at.text, 1)
    for i, (first, count) in enumerate(at.calls()):
        part = flags[first * blocks : (first + count) * blocks]
        hold(part, 1, at.back_clip + first * blocks, at.back_block + first * blocks)
        plan[at.some + i] = sum(f for f, _, _ in part)
    plan[at.keep] = 1 - drop_ref[plan[at.clip]]


def make_plan(at, places, frames, lengths, drops, rows, span):
    smem = pl.BlockSpec(memory_space=pltpu.SMEM)
    return pl.pallas_call(
        functools.partial(plan_kernel, at=at, rows=rows, span=span),
        out_shape=jax.ShapeDtypeStruct((at.size,), jnp.int32),
        in_specs=[smem] * 4,
        out_specs=smem,
        scratch_shapes=[pltpu.SMEM((at.clips,), jnp.int32)],
        cost_estimate=NO_COST,
        name="plan",
    )(places, frames, lengths, drops)


def own_rows_kernel(plan, latents, mine, other, latents_ref, mine_ref, other_ref, keep_ref, *, at):
    latents_ref[...] = latents[0]
    mine_ref[...] = mine[0]
    other_ref[...] = other[0]
    keep_ref[...] = jnp.full(keep_ref.shape, plan[at.keep].astype(F32))


def own_rows(at, plan, latents, cotangent):
    lat, width = latents.shape[1:]
    spec = lambda k: pl.BlockSpec((1, lat, width), lambda i, p: (p[at.clip + k], 0, 0))
    whole = lambda *shape: pl.BlockSpec(shape, lambda i, p: (0,) * len(shape))
    return pl.pallas_call(
        functools.partial(own_rows_kernel, at=at),
        grid_spec=pltpu.PrefetchScalarGridSpec(
            num_scalar_prefetch=1,
            grid=(1,),
            in_specs=[spec(0), spec(0), spec(1)],
            out_specs=[whole(lat, width)] * 3 + [whole(1, width)],
        ),
        out_shape=[
            *[jax.ShapeDtypeStruct((lat, width), BF)] * 3,
            jax.ShapeDtypeStruct((1, width), F32),
        ],
        cost_estimate=NO_COST,
        name="own_rows",
    )(plan, latents, cotangent, cotangent)


def tokens_forward_kernel(
    plan, video_ref, text_ref, latents_ref, norms_ref, key_t_ref, value_t_ref, query_t_ref,
    zero_ref, *refs, at,
):
    outs, (key_ref, value_ref, blocks, peak, total, summed) = refs[:-6], refs[-6:]
    place, j = pl.program_id(0), pl.program_id(1)
    rows = video_ref.shape[1]
    lat = latents_ref.shape[1]
    width = key_ref.shape[1]
    heads = width // HEAD
    clip_count = plan[at.count_plain + place]
    text_count = plan[at.text_plain + place]
    count = clip_count - j * rows
    lat_gain, lat_bias, gain, bias = (norms_ref[i : i + 1] for i in range(4))

    @pl.when((place == 0) & (j == 0))
    def _():
        key_ref[...] = key_t_ref[...].astype(F32).T.astype(BF)
        value_ref[...] = value_t_ref[...].astype(F32).T.astype(BF)

    @pl.when(count <= 0)
    def _():
        zero_ref[...] = jnp.zeros_like(zero_ref)

    @pl.when((j == 0) & ((clip_count > 0) | (text_count > 0)))
    def _():
        queries_in = normed_rows(latents_ref[0].astype(F32), lat_gain, lat_bias)
        rows_t = dot_nt(query_t_ref[...], queries_in).astype(BF).astype(F32) * HEAD**-0.5
        blocks[...] = blocks_across(rows_t, heads)

    @pl.when(j == 0)
    def _():
        peak[...] = jnp.full_like(peak, NEGATIVE).astype(BF).astype(F32)
        total[...] = jnp.zeros_like(total)
        summed[...] = jnp.zeros_like(summed)

    def block(x, limit):
        inputs_in = normed_rows(x.astype(F32), gain, bias)
        key = dot(inputs_in, key_ref[...]).astype(BF)
        value = dot(inputs_in, value_ref[...]).astype(BF)
        mask = lax.broadcasted_iota(jnp.int32, (x.shape[0], 1), 0) < limit
        scores = jnp.where(mask, dot(key, blocks[...]) * LOG2E, NEGATIVE)
        before = peak[...]
        top = jnp.maximum(before, jnp.max(scores, 0, keepdims=True)).astype(BF).astype(F32)
        weights = jnp.exp2(scores - top)
        factor = jnp.exp2(before - top)
        peak[...] = top
        total[...] = total[...] * factor + jnp.sum(weights, 0, keepdims=True)
        table = dot_tn(value, weights.astype(BF))
        for h, part in enumerate(diagonal_parts(table, lat, heads)):
            r = slice(HEAD * h, HEAD * (h + 1))
            summed[r] = summed[r] * factor[:, lat * h : lat * (h + 1)] + part

    @pl.when(count > 0)
    def _():
        block(video_ref[0], count)

    @pl.when((j == 0) & (text_count > 0))
    def _():
        block(text_ref[0], text_count)

    for zone, out_ref in enumerate(outs):

        @pl.when((j == pl.num_programs(1) - 1) & (place // 2 == zone))
        def _(out_ref=out_ref):
            out_ref[0, :width] = summed[...].astype(BF)
            of = [slice(lat * h, lat * (h + 1)) for h in range(heads)]
            totals = [parts_of(total[:, c], 2) for c in of]
            stats = [peak[:, c] for c in of] + [t[0] for t in totals] + [t[1] for t in totals]
            out_ref[0, width:] = stat_tile(stats, STAT)


def tokens_forward(at, plan, video, text, latents, params, rows):
    clips, span, width = video.shape
    lat = latents.shape[1]
    own = params[-1].shape[0]
    blocks = span // rows
    full = lambda a: pl.BlockSpec(a.shape, lambda s, j, *_: (0,) * a.ndim)
    clip_spec = lambda a: pl.BlockSpec(
        (1,) + a.shape[1:], lambda s, j, p: (p[at.clip_plain + s], 0, 0)
    )
    block_spec = lambda clip, block: pl.BlockSpec(
        (1, rows, width), lambda s, j, p: (p[clip + s * blocks + j], p[block + s * blocks + j], 0)
    )
    return pl.pallas_call(
        functools.partial(tokens_forward_kernel, at=at),
        grid_spec=pltpu.PrefetchScalarGridSpec(
            num_scalar_prefetch=1,
            grid=(clips, blocks),
            in_specs=[
                block_spec(at.read_clip, at.read_block),
                clip_spec(text),
                clip_spec(latents),
            ]
            + [full(a) for a in params],
            out_specs=[block_spec(at.zero_clip, at.zero_block)]
            + [
                pl.BlockSpec(
                    (1, own + STAT, lat), lambda s, j, p, z=z: (jnp.clip(s - 2 * z, 0, 1), 0, 0)
                )
                for z in range(clips // 2)
            ],
            scratch_shapes=[
                pltpu.VMEM((width, own), BF),
                pltpu.VMEM((width, own), BF),
                pltpu.VMEM((own, own // HEAD * lat), BF),
                pltpu.VMEM((1, own // HEAD * lat), F32),
                pltpu.VMEM((1, own // HEAD * lat), F32),
                pltpu.VMEM((own, lat), F32),
            ],
        ),
        out_shape=[jax.ShapeDtypeStruct(video.shape, BF)]
        + [jax.ShapeDtypeStruct((2, own + STAT, lat), BF)] * (clips // 2),
        compiler_params=pltpu.CompilerParams(
            vmem_limit_bytes=VMEM_LIMIT, dimension_semantics=("arbitrary", "arbitrary")
        ),
        cost_estimate=cost_of(30.0),
        name="tokens_forward",
    )(plan, video, text, latents, *params)


GROUP = 4


def tokens_back_kernel(
    plan, *refs, at, call, carried, extra,
):
    video_ref, text_ref, latents_ref, norms_ref, pair_ref, pair_t_ref, query_t_ref = refs[:7]
    d0, d1, d2, d3 = refs[7:11]
    refs = refs[13:]
    if carried:
        before_ref, refs = refs[0], refs[1:]
    refs = refs[extra:]
    d_video_ref, d_text_ref, weights_ref, d_query_ref = refs[:4]
    final = call == len(at.calls()) - 1
    if final:
        keep_ref, send_ref = refs[4:6]
        refs = refs[2:]
    q_down, q_across, d_down, d_across, lse, delta, d_query, queries = refs[4:]
    step, j = pl.program_id(0), pl.program_id(1)
    place = step + at.calls()[call][0]
    rows, width = video_ref.shape[1:]
    lat = latents_ref.shape[1]
    own = query_t_ref.shape[0] // 4
    own_heads = own // HEAD
    groups = width // (GROUP * HEAD)
    count = plan[at.count + place] - j * rows
    text_count = plan[at.text + place]
    alive = text_count > 0
    lat_gain, lat_bias, gain, bias = (norms_ref[i : i + 1] for i in range(4))

    @pl.when((step == 0) & (j == 0))
    def _():
        weights_ref[...] = before_ref[...] if carried else jnp.zeros_like(weights_ref)
        for ref in (q_down, q_across, d_down, d_across):
            ref[...] = jnp.zeros_like(ref)

    @pl.when(j == 0)
    def _():
        d_query[...] = jnp.zeros_like(d_query)

    @pl.when((j == 0) & alive)
    def _():
        mine = lax.rem(place, 2) == 0
        first = [jnp.where(mine, a[0, :own].astype(F32), b[0, own : 2 * own].astype(F32)) for a, b in ((d0, d2), (d1, d3))]
        second = [jnp.where(mine, a[0, own : 2 * own].astype(F32), b[0, :own].astype(F32)) for a, b in ((d0, d2), (d1, d3))]
        queries_in = normed_rows(latents_ref[0].astype(F32), lat_gain, lat_bias)
        queries[...] = queries_in
        query = dot_nt(queries_in, query_t_ref[...]).astype(BF).astype(F32) * HEAD**-0.5
        d_rows_t = jnp.concatenate(first + second, 0)
        column = lax.broadcasted_iota(jnp.int32, (lat, 2 * HEAD), 1) // HEAD
        for natural, rows_t, down, across in (
            (query, query.T, q_down, q_across),
            (d_rows_t.T, d_rows_t, d_down, d_across),
        ):
            for head in range(groups * GROUP):
                g, h = divmod(head, GROUP)
                across[g, HEAD * h : HEAD * (h + 1), lat * h : lat * (h + 1)] = rows_t[
                    HEAD * head : HEAD * (head + 1)
                ].astype(BF)
                pair = natural[:, 2 * HEAD * (head // 2) : 2 * HEAD * (head // 2 + 1)]
                at = 2 * HEAD * (h // 2)
                down[g, lat * h : lat * (h + 1), at : at + 2 * HEAD] = jnp.where(
                    column == h % 2, pair, 0.0
                ).astype(BF)
        tiles = [d[0, 2 * own : 2 * own + 2 * STAT].astype(F32) for d in (d0, d1, d2, d3)]
        n = 2 * own_heads
        for kind, first_row, count_of in ((delta, 0, 2), (lse, 2 * n, 3)):
            for shard in range(4):
                a, b = tiles[shard % 2], tiles[2 + shard % 2]
                for h in range(own_heads):
                    at_a = first_row + h + own_heads * (shard // 2)
                    at_b = first_row + h + own_heads * (1 - shard // 2)
                    row = sum(
                        jnp.where(mine, a[at_a + n * i : at_a + n * i + 1], b[at_b + n * i : at_b + n * i + 1])
                        for i in range(count_of)
                    )
                    head = shard * own_heads + h
                    kind[:, lat * head : lat * (head + 1)] = row

    def block(x, limit, out_ref, share):
        counted = (lambda a: a) if share is None else (lambda a: a * share)
        normed, rstd = normalize(x.astype(F32))
        inputs_in = (normed * gain + bias).astype(BF)
        key = dot(inputs_in, pair_ref[:, :width]).astype(BF)
        value = dot(inputs_in, pair_ref[:, width:]).astype(BF)
        mask = lax.broadcasted_iota(jnp.int32, (x.shape[0], 1), 0) < limit
        d_keys, d_values = [], []
        for g in range(groups):
            cut = slice(GROUP * HEAD * g, GROUP * HEAD * (g + 1))
            lanes = slice(GROUP * lat * g, GROUP * lat * (g + 1))
            scores = dot(key[:, cut], q_across[g])
            d_probs = dot(value[:, cut], d_across[g])
            probs = jnp.where(mask, jnp.exp2(scores * LOG2E - lse[:, lanes]), 0.0)
            d_scores = (probs * (d_probs - delta[:, lanes])).astype(BF)
            d_values.append(dot(probs.astype(BF), d_down[g]).astype(BF))
            d_keys.append(dot(d_scores, q_down[g]).astype(BF))
            if g == 0:
                table = dot_tn(key[:, cut], d_scores)
                for h, part in enumerate(diagonal_parts(table, lat, own_heads)):
                    d_query[HEAD * h : HEAD * (h + 1)] += counted(part)
        d_key, d_value = jnp.concatenate(d_keys, 1), jnp.concatenate(d_values, 1)
        d_in = dot(d_key, pair_t_ref[:width]) + dot(d_value, pair_t_ref[width:])
        weights_ref[:own] += counted(dot_tn(d_keys[0], inputs_in)[:own])
        weights_ref[own : 2 * own] += counted(dot_tn(d_values[0], inputs_in)[:own])
        weights_ref[3 * own : 3 * own + 8] += counted(row_sums(d_in * normed))
        weights_ref[3 * own + 8 : 3 * own + 16] += counted(row_sums(d_in))
        scaled = d_in * gain
        d_x = rstd * (
            scaled
            - jnp.mean(scaled, -1, keepdims=True)
            - normed * jnp.mean(scaled * normed, -1, keepdims=True)
        )
        out_ref[0] = d_x.astype(BF)

    @pl.when(count > 0)
    def _():
        block(video_ref[0], count, d_video_ref, None)

    @pl.when((plan[at.some + call] == 0) & (step == 0) & (j == 0))
    def _():
        d_video_ref[...] = jnp.zeros_like(d_video_ref)

    @pl.when((j == 0) & alive)
    def _():
        block(text_ref[0], text_count, d_text_ref, plan[at.share].astype(F32))

    @pl.when((j == 0) & jnp.logical_not(alive))
    def _():
        d_text_ref[...] = jnp.zeros_like(d_text_ref)

    @pl.when(j == pl.num_programs(1) - 1)
    def _():
        d_rows = (d_query[...] * HEAD**-0.5).astype(BF)
        d_query_ref[0] = d_rows

        @pl.when(alive)
        def _():
            weights_ref[2 * own : 3 * own] += dot(d_rows, queries[...])

        if final:

            @pl.when(step == pl.num_programs(0) - 1)
            def _():
                half = width // 2
                side = plan[at.mod]
                keep_ref[...] = weights_ref[:, pl.ds(pl.multiple_of(side * half, half), half)]
                send_ref[...] = weights_ref[
                    :, pl.ds(pl.multiple_of((1 - side) * half, half), half)
                ].astype(BF)


WEIGHT_ROWS = 64


def tokens_back(at, plan, call, video, text, latents, params, arrived, filled, before, rows, deps=()):
    first, steps = at.calls()[call]
    span, width = video.shape[1:]
    blocks = span // rows
    lat = latents.shape[1]
    own = params[-1].shape[0] // 4
    groups = width // (GROUP * HEAD)
    full = lambda a: pl.BlockSpec(
        a.shape, lambda s, j, *_: (0,) * a.ndim, pipeline_mode=pl.Buffered(1)
    )
    clip_spec = lambda a: pl.BlockSpec(
        (1,) + a.shape[1:], lambda s, j, p: (p[at.clip + first + s], 0, 0)
    )
    index = lambda p, table, s, j: p[table + (first + s) * blocks + j]
    video_spec = pl.BlockSpec(
        (1, rows, width),
        lambda s, j, p: (index(p, at.back_clip, s, j), index(p, at.back_block, s, j), 0),
    )
    weight_shape = (3 * own + WEIGHT_ROWS, width)
    half_shape = (weight_shape[0], width // 2)
    final = call == len(at.calls()) - 1
    operands = [video, text, latents, *params, *arrived]
    in_specs = [video_spec, clip_spec(text), clip_spec(latents)]
    in_specs += [full(a) for a in params]
    in_specs += [
        pl.BlockSpec(
            (1, 2 * own + 2 * STAT, lat), lambda s, j, *_: ((s + first) // 2 - first // 2, 0, 0)
        )
        for a in arrived
    ]
    start = 1 + len(operands)
    operands += filled
    in_specs += [pl.BlockSpec(memory_space=pl.ANY)] * 2
    if before is not None:
        operands += [before]
        in_specs += [full(before)]
    operands += deps
    in_specs += [pl.BlockSpec(memory_space=pl.ANY)] * len(deps)
    return pl.pallas_call(
        functools.partial(
            tokens_back_kernel, at=at, call=call, carried=before is not None, extra=len(deps)
        ),
        grid_spec=pltpu.PrefetchScalarGridSpec(
            num_scalar_prefetch=1,
            grid=(steps, blocks),
            in_specs=in_specs,
            out_specs=[
                video_spec,
                clip_spec(text),
                pl.BlockSpec(weight_shape, lambda s, j, *_: (0, 0)),
                pl.BlockSpec((1, own, lat), lambda s, j, *_: (s, 0, 0)),
            ]
            + [pl.BlockSpec(half_shape, lambda s, j, *_: (0, 0))] * (2 * final),
            scratch_shapes=[
                pltpu.VMEM((groups, GROUP * lat, GROUP * HEAD), BF),
                pltpu.VMEM((groups, GROUP * HEAD, GROUP * lat), BF),
                pltpu.VMEM((groups, GROUP * lat, GROUP * HEAD), BF),
                pltpu.VMEM((groups, GROUP * HEAD, GROUP * lat), BF),
                pltpu.VMEM((1, groups * GROUP * lat), F32),
                pltpu.VMEM((1, groups * GROUP * lat), F32),
                pltpu.VMEM((own, lat), F32),
                pltpu.VMEM((lat, width), BF),
            ],
        ),
        out_shape=[
            jax.ShapeDtypeStruct(video.shape, BF),
            jax.ShapeDtypeStruct(text.shape, BF),
            jax.ShapeDtypeStruct(weight_shape, F32),
            jax.ShapeDtypeStruct((steps, own, lat), BF),
        ]
        + [jax.ShapeDtypeStruct(half_shape, F32), jax.ShapeDtypeStruct(half_shape, BF)] * final,
        input_output_aliases={start: 0, start + 1: 1},
        compiler_params=pltpu.CompilerParams(
            vmem_limit_bytes=VMEM_LIMIT, dimension_semantics=("arbitrary", "arbitrary")
        ),
        cost_estimate=cost_of((25.0, 10.0)[call]),
        name="tokens_back",
    )(plan, *operands)


def combine_kernel(plan, output_ref, *refs):
    parts, (mine_ref, other_ref, low_ref, *branch_refs) = refs[:-5], refs[-5:]
    own = parts[0].shape[1] - STAT
    lat = parts[0].shape[2]
    heads = own // HEAD
    results = []
    for y in range(2):
        tiles = [p[y, own:].astype(F32) for p in parts]
        attended, logs = [], []
        for h in range(heads):
            peaks = [t[h : h + 1] for t in tiles]
            top = peaks[0]
            for p in peaks[1:]:
                top = jnp.maximum(top, p)
            total = jnp.zeros((1, lat), F32)
            summed = jnp.zeros((HEAD, lat), F32)
            for p, t, peak in zip(parts, tiles, peaks):
                factor = jnp.exp2(peak - top)
                a = t[heads + h : heads + h + 1] + t[2 * heads + h : 2 * heads + h + 1]
                total = total + a * factor
                summed = summed + p[y, HEAD * h : HEAD * (h + 1)].astype(F32) * factor
            some = total > 0.0
            safe = jnp.where(some, total, 1.0)
            attended.append(jnp.where(some, summed / safe, 0.0))
            logs.append(parts_of(jnp.where(some, top + jnp.log2(safe), 0.0), 3))
        stats = [logs[h][i] for i in range(3) for h in range(heads)]
        results.append((jnp.concatenate(attended, 0), stat_tile(stats, STAT).astype(F32)))
    first = plan[SIDE_Y] == 0
    for k, (ref, (a, b)) in enumerate(((mine_ref, results), (other_ref, results[::-1]))):
        low = jnp.where(first, a[0], b[0]).astype(BF)
        ref[:own] = low
        ref[own:] = jnp.where(first, a[1], b[1]).astype(BF)
        low_ref[k] = low
        branch_refs[k][...] = dot_tn(low, output_ref[...]).astype(BF)


def spread(norms_ref, row):
    return norms_ref[row : row + 1], norms_ref[row + 1 : row + 2]


def sum_of(terms):
    total = terms[0]
    for term in terms[1:]:
        total = total + term
    return total


def received_sum(part0, part1):
    return part0[...].astype(F32) + part1[...].astype(F32)


def cross_forward_kernel(
    plan, b0, b1, b2, b3, latents_ref, keep_ref, norms_ref, up0, down0, near, far,
    first_ref, inner_ref, pre_ref, hidden_ref, part_ref, up1, down1,
):
    join_mlp(near, far, plan[MOD], up1, down1)
    branch = received_sum(b0, b1) + received_sum(b2, b3)
    first = latents_ref[...].astype(F32) + keep_ref[...] * branch
    first_ref[...] = first
    inner = normed_rows(first, *spread(norms_ref, 4))
    inner_ref[...] = inner
    terms = []
    for k, (up, down) in enumerate(((up0, down0), (up1, down1))):
        pre = dot(inner, up[...])
        pre_ref[k] = pre
        hidden = (pre * gelu_share(pre)).astype(BF)
        hidden_ref[k] = hidden
        terms.append(dot(hidden, down[...]))
    part_ref[...] = sum_of(terms).astype(BF)


def join_mlp(near, far, mod, up, down):
    half = up.shape[0] // 2
    join_halves(up, near, far, mod, 0, half)
    join_halves(down, near, far, mod, half, half)


def join_self(near, far, mod, targets):
    half, start = targets.shape[1] // 2, targets.shape[2]
    for i in range(4):
        join_halves(targets.at[i], near, far, mod, start + half * i, half)


def self_forward_kernel(
    plan, first_ref, part0, part1, norms_ref, wq, wk, wv, wo, near, far,
    second_ref, inner_ref, rows_ref, query_t_ref, attended_ref, lse_ref, part_ref, joined,
):
    join_self(near, far, plan[MOD], joined)
    second = first_ref[...] + received_sum(part0, part1)
    second_ref[...] = second
    inner = normed_rows(second, *spread(norms_ref, 6))
    inner_ref[...] = inner
    lat = inner.shape[0]
    own = wq.shape[0]
    heads = own // HEAD
    terms = []
    for k, (q, w, v, o) in enumerate(((wq, wk, wv, wo), [joined.at[i] for i in range(4)])):
        query = (dot_nt(inner, q[...]).astype(BF).astype(F32) * HEAD**-0.5).astype(BF)
        key = dot_nt(inner, w[...]).astype(BF)
        value = dot_nt(inner, v[...]).astype(BF)
        for i, a in enumerate((query, key, value)):
            rows_ref[k, i] = a
        query_t = dot_nt(q[...], inner).astype(BF).astype(F32) * HEAD**-0.5
        query_t_ref[k] = query_t.astype(BF)
        scores = dot(key, blocks_across(query_t, heads)) * LOG2E
        top = jnp.max(scores, 0, keepdims=True)
        weights = jnp.exp2(scores - top)
        total = jnp.sum(weights, 0, keepdims=True)
        table = dot_tn(value, weights.astype(BF))
        attended = jnp.concatenate(
            [
                part / total[:, lat * h : lat * (h + 1)]
                for h, part in enumerate(diagonal_parts(table, lat, heads))
            ],
            0,
        )
        attended_ref[k] = attended
        lse_ref[k] = top + jnp.log2(total)
        terms.append(dot_tn(attended.astype(BF), o[...]))
    part_ref[...] = sum_of(terms).astype(BF)


def hidden_back(grad_low, pre, up, down):
    d_hidden = dot_nt(grad_low, down[...])
    d_pre = (d_hidden * gelu_slope(pre)).astype(BF)
    return d_pre, dot_nt(d_pre, up[...])


def last_back_kernel(
    plan, second_ref, part0, part1, cotangent_ref, norms_ref, up0, down0, near, far,
    third_ref, inner_ref, hidden_ref, d_pre_ref, part_ref, moving_ref, up1, down1,
):
    join_mlp(near, far, plan[MOD], up1, down1)
    third = second_ref[...] + received_sum(part0, part1)
    third_ref[...] = third
    inner = normed_rows(third, *spread(norms_ref, 8))
    inner_ref[...] = inner
    terms = []
    for k, (up, down) in enumerate(((up0, down0), (up1, down1))):
        pre = dot(inner, up[...])
        hidden_ref[k] = (pre * gelu_share(pre)).astype(BF)
        d_pre_ref[k], term = hidden_back(cotangent_ref[...], pre, up, down)
        terms.append(term)
    part_ref[...] = sum_of(terms).astype(BF)
    lat = inner.shape[0]
    for i, a in enumerate((inner, d_pre_ref[1], hidden_ref[1])):
        moving_ref[lat * i : lat * (i + 1)] = a


def down_kernel(plan, hidden_ref, down0, near, far, part_ref, down1):
    half = down1.shape[0] // 2
    join_halves(down1, near, far, plan[MOD], half, half)
    part_ref[...] = (dot(hidden_ref[0], down0[...]) + dot(hidden_ref[1], down1[...])).astype(BF)


def self_back_kernel(
    plan, cotangent_ref, third_ref, part0, part1, norms_ref,
    rows_ref, query_t_ref, attended_ref, lse_ref, wq, wk, wv, wo, near, far, self_in_ref,
    grad_ref, sums_ref, branch_ref, d_rows_ref, low_ref, part_ref, moving_ref, joined,
):
    join_self(near, far, plan[MOD], joined)
    d_inner = received_sum(part0, part1)
    d_x, d_gain, d_bias = norm_back(d_inner, third_ref[...], spread(norms_ref, 8)[0])
    grad = cotangent_ref[...].astype(F32) + d_x
    grad_ref[...] = grad
    sums_ref[0:1] = d_gain
    sums_ref[1:2] = d_bias
    branch = grad.astype(BF)
    branch_ref[...] = branch
    lat = grad.shape[0]
    own = wq.shape[0]
    heads = own // HEAD
    terms = []
    for k, weights in enumerate(((wq, wk, wv, wo), [joined.at[i] for i in range(4)])):
        o = weights[3]
        query, key, value = rows_ref[k, 0], rows_ref[k, 1], rows_ref[k, 2]
        d_att = dot_nt(branch, o[...]).astype(BF).astype(F32)
        d_att_t = dot_nt(o[...], branch).astype(BF).astype(F32)
        attended = attended_ref[k]
        low_ref[k] = attended.astype(BF)
        product = d_att_t * attended
        delta = jnp.concatenate(
            [
                jnp.sum(product[HEAD * h : HEAD * (h + 1)], 0, keepdims=True)
                for h in range(heads)
            ],
            1,
        )
        scores = dot(key, blocks_across(query_t_ref[k].astype(F32), heads))
        d_probs = dot(value, blocks_across(d_att_t, heads))
        probs = jnp.exp2(scores * LOG2E - lse_ref[k])
        d_scores = (probs * (d_probs - delta)).astype(BF)
        d_value = dot(probs.astype(BF), blocks_down(d_att, heads)).astype(BF)
        d_key = dot(d_scores, blocks_down(query.astype(F32), heads)).astype(BF)
        table = dot_tn(d_scores, key)
        column = lax.broadcasted_iota(jnp.int32, (lat, own), 1) // HEAD
        d_query = sum_of(
            [jnp.where(column == h, table[lat * h : lat * (h + 1)], 0.0) for h in range(heads)]
        )
        d_query = (d_query * HEAD**-0.5).astype(BF)
        for i, a in enumerate((d_query, d_key, d_value)):
            d_rows_ref[k, i] = a
            terms.append(dot(a, weights[i][...]))
            if k == 1:
                moving_ref[2 * lat :, own * i : own * (i + 1)] = a
    part_ref[...] = sum_of(terms).astype(BF)
    moving_ref[:lat] = self_in_ref[...]
    moving_ref[lat : 2 * lat] = branch
    moving_ref[2 * lat :, 3 * own :] = attended_ref[1].T.astype(BF)


def cross_back_kernel(
    plan, grad_ref, second_ref, part0, part1, norms_ref, pre_ref, up0, down0, near, far,
    inner_ref, hidden_ref,
    out_ref, sums_ref, low_ref, d_pre_ref, part_ref, moving_ref, up1, down1,
):
    join_mlp(near, far, plan[MOD], up1, down1)
    d_inner = received_sum(part0, part1)
    d_x, d_gain, d_bias = norm_back(d_inner, second_ref[...], spread(norms_ref, 6)[0])
    grad = grad_ref[...] + d_x
    out_ref[...] = grad
    sums_ref[0:1] = d_gain
    sums_ref[1:2] = d_bias
    grad_low = grad.astype(BF)
    low_ref[...] = grad_low
    terms = []
    for k, (up, down) in enumerate(((up0, down0), (up1, down1))):
        d_pre_ref[k], term = hidden_back(grad_low, pre_ref[k], up, down)
        terms.append(term)
    part_ref[...] = sum_of(terms).astype(BF)
    lat = grad.shape[0]
    for i, a in enumerate((inner_ref[...], d_pre_ref[1], hidden_ref[1], grad_low)):
        moving_ref[lat * i : lat * (i + 1)] = a


def attended_back_kernel(
    plan, grad_ref, first_ref, part0, part1, norms_ref, keep_ref, a0, a2, o0, near, far,
    branch_ref, packed_ref, first_grad_ref, sums_ref, o2,
):
    own, width = o0.shape
    join_halves(o2, near, far, plan[MOD], width + 2 * own, own // 2)
    d_inner = received_sum(part0, part1)
    d_x, d_gain, d_bias = norm_back(d_inner, first_ref[...], spread(norms_ref, 4)[0])
    grad = grad_ref[...] + d_x
    branch = (keep_ref[...] * grad).astype(BF)
    branch_ref[...] = branch
    own = o0.shape[0]
    heads = own // HEAD
    deltas, logs = [], []
    for k, (a, o) in enumerate(((a0, o0), (a2, o2))):
        d_att_t = dot_nt(o[...], branch).astype(BF)
        packed_ref[own * k : own * (k + 1)] = d_att_t
        product = d_att_t.astype(F32) * a[:own].astype(F32)
        tile = a[own:].astype(F32)
        for h in range(heads):
            deltas.append(
                parts_of(jnp.sum(product[HEAD * h : HEAD * (h + 1)], 0, keepdims=True), 2)
            )
            logs.append([tile[heads * i + h : heads * i + h + 1] for i in range(3)])
    rows = [d[i] for i in range(2) for d in deltas] + [g[i] for i in range(3) for g in logs]
    packed_ref[2 * own : 2 * own + 2 * STAT] = stat_tile(rows, 2 * STAT)
    first_grad_ref[...] = grad
    sums_ref[0:1] = d_gain
    sums_ref[1:2] = d_bias


def half_rows_kernel(plan, third_ref, out0, out1, out_ref, hold):
    half = out_ref.shape[0]
    hold[...] = third_ref[...] + received_sum(out0, out1)
    cut = pl.ds(pl.multiple_of(plan[SIDE_X] * half, half), half)
    out_ref[...] = hold[cut].astype(BF)


def latent_back_kernel(
    plan, grad_ref, latents_ref, norms_ref, d0, d1, d2, d3, query_t_ref,
    cross_sums, self_sums, ffn_sums, out_ref, hold,
):
    own, lat = d0.shape
    half = lat // 2
    d_in = sum_of(
        [dot_tn(d[...], query_t_ref[own * k : own * (k + 1)]) for k, d in enumerate((d0, d1, d2, d3))]
    )
    d_x, d_gain, d_bias = norm_back(
        d_in, latents_ref[...].astype(F32), spread(norms_ref, 0)[0]
    )
    hold[...] = grad_ref[...] + d_x
    cut = pl.ds(pl.multiple_of(plan[SIDE_X] * half, half), half)
    out_ref[:half] = hold[cut].astype(BF)
    sums = [d_gain, d_bias]
    sums += [ref[i : i + 1] for ref in (cross_sums, self_sums, ffn_sums) for i in range(2)]
    out_ref[half:] = stat_tile(sums, STAT)


def tail_pack_kernel(plan, keep_ref, arrived_ref, query_ref, own_ref, *outs, at):
    zones = len(outs) + 1
    own, lat = query_ref.shape[1:]
    step = own_ref.shape[0]
    for k in range(zones):
        cut = pl.ds(pl.multiple_of(lax.rem(plan[at.tok] + k, zones) * step, 16), step)
        total = keep_ref[cut] + arrived_ref[cut].astype(F32)
        if k == 0:
            own_ref[...] = total
            continue
        out = outs[k - 1]
        out[:own] = query_ref[2 * k - 1]
        out[own : 2 * own] = query_ref[2 * k]
        for c in range(total.shape[1] // lat):
            out[2 * own + step * c : 2 * own + step * (c + 1)] = total[
                :, lat * c : lat * (c + 1)
            ].astype(BF)


def tail_sum_kernel(first_ref, query_ref, own_ref, *refs):
    parts, (mine_ref, other_ref, share_ref) = refs[:-3], refs[-3:]
    own, lat = mine_ref.shape
    step = own_ref.shape[0]
    for i, (ref, near) in enumerate(((mine_ref, first_ref), (other_ref, query_ref))):
        cut = slice(own * i, own * (i + 1))
        ref[...] = (near[0].astype(F32) + sum_of([p[cut].astype(F32) for p in parts])).astype(BF)
    for c in range(own_ref.shape[1] // lat):
        lanes = slice(lat * c, lat * (c + 1))
        cut = slice(2 * own + step * c, 2 * own + step * (c + 1))
        total = own_ref[:, lanes] + sum_of([p[cut].astype(F32) for p in parts])
        share_ref[:, lanes] = total.astype(BF)


def token_weights_kernel(plan, mine_ref, other_ref, key_ref, value_ref, query_ref, sums_ref, whole, *, at):
    zones, step, half = mine_ref.shape
    own = key_ref.shape[0]
    side = plan[at.mod]
    for k in range(zones):
        cut = pl.ds(pl.multiple_of(lax.rem(plan[at.tok] + k, zones) * step, 16), step)
        for ref, x in ((mine_ref, side), (other_ref, 1 - side)):
            whole[cut, pl.ds(pl.multiple_of(x * half, half), half)] = ref[k].astype(F32)
    for i, ref in enumerate((key_ref, value_ref, query_ref)):
        ref[...] = whole[own * i : own * (i + 1)]
    for i in range(2):
        rows = whole[3 * own + 8 * i : 3 * own + 8 * (i + 1)]
        sums_ref[i : i + 1] = jnp.sum(rows, 0, keepdims=True)


def out_rows_kernel(plan, halves_ref, out_ref, *, at):
    clips, half = out_ref.shape[0], halves_ref.shape[1]
    for place in range(clips):
        zone = lax.rem(plan[at.tok] + place // 2, clips // 2)
        first = 4 * zone + 2 * lax.rem(plan[SIDE_Y] + place % 2, 2)
        for x in range(2):
            out_ref[plan[at.clip + place], half * x : half * (x + 1)] = halves_ref[first + x]


def in_clip_order_kernel(plan, r0, r1, r2, r3, out_ref, *sums_ref, at):
    half = out_ref.shape[1] // 2
    side = plan[at.side_x]
    for place in range(out_ref.shape[0]):
        same, crossed = (r0, r1) if place % 2 == 0 else (r2, r3)
        clip, zone = plan[at.clip + place], place // 2
        out_ref[clip, pl.ds(pl.multiple_of(side * half, half), half)] = same[zone, :half]
        out_ref[clip, pl.ds(pl.multiple_of((1 - side) * half, half), half)] = crossed[zone, :half]
    for ref in sums_ref:
        ref[...] = sum_of(
            [r[zone, half:].astype(F32)[:8] for zone in range(r0.shape[0]) for r in (r0, r2)]
        )


def in_clip_order(at, plan, lat, results, deps=()):
    height, width = results[0].shape[1:]
    outs = [((at.clips, lat, width), BF)] + [((8, width), F32)] * (height > lat // 2)
    return kernel_call(
        functools.partial(in_clip_order_kernel, at=at), outs, *results,
        name="in_clip_order", scalars=(plan,), deps=deps,
    )


def mlp_grads_kernel(inner, d_pre, hidden, low, low_y, moved, out_ref):
    lat, width = inner.shape
    near = [moved[lat * i : lat * (i + 1)] for i in range(3)]
    last = low_y.shape[0] - lat
    out_ref[:width] = (dot_tn(inner[...], d_pre[0]) + dot_tn(near[0], near[1])).astype(BF)
    out_ref[width:] = (dot_tn(hidden[0], low[:lat]) + dot_tn(near[2], low_y[last:])).astype(BF)


def self_grads_kernel(inner, branch, d_rows, low_t, moved, outs):
    lat = inner.shape[0]
    own = low_t.shape[1]
    heads_in = [moved[2 * lat :, own * i : own * (i + 1)] for i in range(4)]
    for i in range(3):
        part = dot_tn(d_rows[0, i], inner[...]) + dot_tn(heads_in[i], moved[:lat])
        outs[own * i : own * (i + 1)] = part.astype(BF)
    part = dot(low_t[0], branch[...]) + dot_tn(heads_in[3], moved[lat : 2 * lat])
    outs[3 * own :] = part.astype(BF)


def output_grad_kernel(low, branch, branch_y, out_ref):
    part = dot(low[0], branch[...]) + dot(low[1], branch_y[...])
    out_ref[...] = part.astype(BF)


def head_move(x, k):
    n = lax.axis_size("head")
    return lax.ppermute(x, "head", [(i, i ^ k) for i in range(n)])


def mod_move(x):
    return lax.ppermute(x, "mod", [(0, 1), (1, 0)])


def tok_move(x, shift):
    n = lax.axis_size("tok")
    return lax.ppermute(x, "tok", [(i, (i + shift) % n) for i in range(n)])


def after(x, *earlier):
    return lax.optimization_barrier((x, *earlier))[0]


def on_device(
    latents,
    video_tokens,
    text_tokens,
    frame_counts,
    text_lengths,
    drop_mask,
    cotangent,
    norm_latent_gain,
    norm_latent_bias,
    norm_input_gain,
    norm_input_bias,
    cross_query,
    cross_key,
    cross_value,
    cross_output,
    norm_cross_gain,
    norm_cross_bias,
    cross_up,
    cross_down,
    norm_self_gain,
    norm_self_bias,
    self_query,
    self_key,
    self_value,
    self_output,
    norm_ffn_gain,
    norm_ffn_bias,
    self_up,
    self_down,
):
    clips, lat, width = latents.shape
    span = video_tokens.shape[1]
    own = cross_key.shape[1]
    heads = own // HEAD
    shards = lax.axis_size("tok")
    zones = clips // 2
    tok, mod, head = lax.axis_index("tok"), lax.axis_index("mod"), lax.axis_index("head")
    side_x, side_y = lax.rem(head, 2), head // 2
    rows = 784 if span % 784 == 0 else span
    norms = jnp.stack(
        [norm_latent_gain, norm_latent_bias, norm_input_gain, norm_input_bias,
         norm_cross_gain, norm_cross_bias, norm_self_gain, norm_self_bias,
         norm_ffn_gain, norm_ffn_bias]
    )
    cross_kvq = [cross_key.T, cross_value.T, cross_query.T]
    self_weights = [self_query.T, self_key.T, self_value.T, self_output]

    at = Plan(clips, span // rows)
    last = (tok == shards - 1).astype(jnp.int32)
    places = jnp.stack([tok, side_x, side_y, mod, last]).astype(jnp.int32)
    plan = make_plan(at, places, frame_counts, text_lengths, drop_mask, rows, span)

    (pack,) = pack_halves(at, plan, [[cross_up, cross_down] + self_weights + [cross_output]])
    near = head_move(pack, 2)
    tables = jnp.concatenate(cross_kvq, 0)
    if shards == zones:
        part = tables.shape[0] // shards
        tables = lax.dynamic_slice_in_dim(tables, tok * part, part, 0)
        tables = lax.all_gather(tables, ("tok", "head")).reshape(shards, 4, part, width)
    else:
        tables = lax.all_gather(tables, "head")[None]

    d_video, *partial = tokens_forward(
        at, plan, video_tokens, text_tokens, latents, (norms, *cross_kvq), rows
    )
    received = [tok_move(partial[k % zones], k) for k in range(1, shards)]
    (pack3,) = pack_halves(at, tie(plan, partial[0]), [[self_up, self_down]])
    my_latents, my_cotangent, other_cotangent, keep = own_rows(
        at, tie(plan, partial[0]), latents, cotangent
    )
    lw = (lat, width)
    square = ((width, width), BF)
    mine, other, low, branch, branch_other = kernel_call(
        combine_kernel, [(partial[0].shape[1:], BF)] * 2 + [((2, own, lat), BF)] + [(lw, BF)] * 2,
        cross_output, partial[0], *received, name="combine", scalars=(plan,),
    )
    near = tie(near, mine)
    far = mod_move(near)
    branch_parts = [branch, head_move(branch, 1), head_move(branch_other, 2), head_move(branch_other, 3)]

    near3 = head_move(tie(pack3, *branch_parts[1:]), 2)

    first, inner1, pre1, hidden1, part = kernel_call(
        cross_forward_kernel,
        [(lw, F32), (lw, BF), ((2,) + lw, F32), ((2,) + lw, BF), (lw, BF)],
        *branch_parts, my_latents, keep, norms, cross_up, cross_down, near, far,
        name="cross_forward", scalars=(plan,), scratch=[square] * 2,
    )
    mine_y = head_move(tie(other, first), 2)
    second, self_in, self_rows, self_query_t, self_attended, self_lse, part = kernel_call(
        self_forward_kernel,
        [(lw, F32), (lw, BF), ((2, 3, lat, own), BF), ((2, own, lat), BF), ((2, own, lat), F32),
         ((2, 1, heads * lat), F32), (lw, BF)],
        first, part, head_move(part, 1), norms, *self_weights, near, far,
        name="self_forward", scalars=(plan,), scratch=[((4, own, width), BF)],
    )
    near3 = tie(near3, second)
    far3 = mod_move(near3)
    third, inner2, hidden2, d_pre2, part, moving = kernel_call(
        last_back_kernel,
        [(lw, F32), (lw, BF), ((2,) + lw, BF), ((2,) + lw, BF), (lw, BF), ((3 * lat, width), BF)],
        second, part, head_move(part, 1), my_cotangent, norms, self_up, self_down, near3, far3,
        name="last_back", scalars=(plan,), scratch=[square] * 2,
    )
    received = head_move(part, 1)
    halves = head_move(moving, 2)
    (out_part,) = kernel_call(
        down_kernel, [(lw, BF)], hidden2, self_down, near3, far3,
        name="down", beside=3.4, scalars=(plan,), scratch=[square], deps=(part,),
    )
    grad_third, ffn_sums, self_branch, self_d_rows, self_low, part, moving = kernel_call(
        self_back_kernel,
        [(lw, F32), ((2, width), F32), (lw, BF), ((2, 3, lat, own), BF), ((2, own, lat), BF), (lw, BF),
         ((3 * lat, width), BF)],
        my_cotangent, third, part, received, norms,
        self_rows, self_query_t, self_attended, self_lse, *self_weights, near, far, self_in,
        name="self_back", scalars=(plan,), deps=(out_part,), scratch=[((4, own, width), BF)],
    )
    out_moved = head_move(tie(out_part, grad_third), 1)
    moved_self = head_move(moving, 2)
    (out_half,) = kernel_call(
        half_rows_kernel, [((lat // 2, width), BF)], third, out_part, out_moved,
        name="half_rows", beside=1.5, scalars=(plan,), scratch=[(lw, F32)],
    )
    out_halves = lax.all_gather(out_half, ("tok", "head"))
    grad_second, self_sums, low1, d_pre1, part, moving = kernel_call(
        cross_back_kernel,
        [(lw, F32), ((2, width), F32), (lw, BF), ((2,) + lw, BF), (lw, BF), ((4 * lat, width), BF)],
        grad_third, second, part, head_move(part, 1), norms, pre1,
        cross_up, cross_down, near, far, inner1, hidden1,
        name="cross_back", scalars=(plan,), deps=(out_half,), scratch=[square] * 2,
    )

    pair, pair_t, query_t = kernel_call(
        tables_kernel,
        [((width, 2 * width), BF), ((2 * width, width), BF), ((width, width), BF)],
        tables, name="tables", beside=4.7, scalars=(plan,),
    )
    moved = head_move(moving, 2)
    cross_branch, packed, grad_first, cross_sums = kernel_call(
        attended_back_kernel,
        [(lw, BF), ((2 * own + 2 * STAT, lat), BF), (lw, F32), ((2, width), F32)],
        grad_second, first, part, head_move(part, 1), norms, keep,
        mine, mine_y, cross_output, near, far,
        name="attended_back", scalars=(plan,), scratch=[((own, width), BF)], deps=(pair,),
    )

    (stages,) = kernel_call(
        stack_kernel, [((zones,) + packed.shape, BF)],
        packed, *[tok_move(packed, shards - k) for k in range(1, zones)], name="stack",
    )
    arrived = [stages] + [head_move(stages, k) for k in (1, 2, 3)]
    (mlp2,) = kernel_call(
        mlp_grads_kernel, [((2 * width, width), BF)], inner2, d_pre2, hidden2, my_cotangent, other_cotangent, halves,
        name="last_weights", beside=4.0, deps=(packed,),
    )
    branch_y = head_move(cross_branch, 2)
    (self_grads,) = kernel_call(
        self_grads_kernel, [((4 * own, width), BF)],
        self_in, self_branch, self_d_rows, self_low, moved_self, name="self_weights", beside=3.3,
        deps=(stages,),
    )
    (mlp1,) = kernel_call(
        mlp_grads_kernel, [((2 * width, width), BF)], inner1, d_pre1, hidden1,
        low1, moved, moved, name="cross_weights", beside=4.4,
        deps=(stages,),
    )
    (output_grad,) = kernel_call(
        output_grad_kernel, [((own, width), BF)], low, cross_branch, branch_y,
        name="output_weights", beside=2.1,
    )
    counted = lambda grads: [jnp.where(tok < zones, a, 0) if shards > zones else a for a in grads]
    params = (norms, pair, pair_t, query_t)
    tokens = (video_tokens, text_tokens, latents)
    d_text = jnp.zeros_like(text_tokens)
    d_video, d_text, token_weights, first_query = tokens_back(
        at, plan, 0, *tokens, params, arrived, [d_video, d_text], None, rows,
        deps=(mlp2, self_grads, mlp1, output_grad),
    )
    d_video, d_text, token_weights, d_query, keep_half, send_half = tokens_back(
        at, plan, 1, *tokens, params, arrived, [d_video, d_text], token_weights, rows,
        deps=(out_halves,),
    )
    sums = lax.psum(counted([mlp2, self_grads, mlp1, output_grad]), ("tok", "mod"))
    mlp2, self_grads, mlp1, output_grad = (a.astype(F32) for a in sums)
    up1, down1 = mlp1[:width], mlp1[width:]
    up2, down2 = mlp2[:width], mlp2[width:]

    (latents_out,) = kernel_call(
        functools.partial(out_rows_kernel, at=at), [(latents.shape, BF)], out_halves[: 4 * zones],
        name="out_rows", scalars=(plan,),
    )

    whole_rows = token_weights.shape[0]
    step = whole_rows // zones
    if shards == zones:
        token_own, *pieces = kernel_call(
            functools.partial(tail_pack_kernel, at=at),
            [((step, width // 2), F32)] + [((2 * own + step * width // 2 // lat, lat), BF)] * (zones - 1),
            keep_half, mod_move(send_half), d_query,
            name="tail_pack", scalars=(plan,), deps=(latents_out,),
        )
        received = [tok_move(p, k + 1) for k, p in enumerate(pieces)]
        my_query, other_query, share = kernel_call(
            tail_sum_kernel, [((own, lat), BF)] * 2 + [((step, width // 2), BF)],
            first_query, d_query, token_own, *received, name="tail_sum",
        )
        shares = [share] + [tok_move(share, shards - k) for k in range(1, zones)]
        (shares,) = kernel_call(
            stack_kernel, [((zones,) + share.shape, BF)], *shares, name="stack"
        )
        d_key_t, d_value_t, d_query_t, input_sums = kernel_call(
            functools.partial(token_weights_kernel, at=at),
            [((own, width), F32)] * 3 + [((2, width), F32)],
            shares, mod_move(shares), name="token_weights", scalars=(plan,),
            scratch=[((whole_rows, width), F32)],
        )
    else:
        pieces = jnp.concatenate([first_query, d_query], 0).reshape(zones, 2, own, lat)
        received = [tok_move(pieces[k % zones], k) for k in range(1, shards)]
        d_query = sum_of([a.astype(F32) for a in [pieces[0]] + received]).astype(BF)
        my_query, other_query = d_query[0], d_query[1]
        total = lax.psum(token_weights, ("tok", "mod"))
        d_key_t, d_value_t, d_query_t = (total[own * i : own * (i + 1)] for i in range(3))
        input_sums = jnp.sum(total[3 * own : 3 * own + 16].reshape(2, 8, width), 1)
    d_queries = [my_query] + [head_move(a, k) for k, a in ((1, my_query), (2, other_query), (3, other_query))]
    (my_grad,) = kernel_call(
        latent_back_kernel, [((lat // 2 + STAT, width), BF)],
        grad_first, my_latents, norms, *d_queries, query_t, cross_sums, self_sums, ffn_sums,
        name="latent_back", scalars=(plan,), scratch=[(lw, F32)],
    )
    zones_grad = jnp.stack([my_grad] + [tok_move(my_grad, shards - k) for k in range(1, zones)])
    zones_grad = [zones_grad] + [head_move(zones_grad, k) for k in (1, 2, 3)]
    grad_latents, norm_sums = in_clip_order(at, plan, lat, zones_grad)
    norm_sums = norm_sums + mod_move(norm_sums)
    return (
        latents_out,
        grad_latents,
        d_video,
        d_text,
        norm_sums[0],
        norm_sums[1],
        input_sums[0],
        input_sums[1],
        d_query_t.T,
        d_key_t.T,
        d_value_t.T,
        output_grad,
        norm_sums[2],
        norm_sums[3],
        up1,
        down1,
        norm_sums[4],
        norm_sums[5],
        self_grads[:own].T,
        self_grads[own : 2 * own].T,
        self_grads[2 * own : 3 * own].T,
        self_grads[3 * own :],
        norm_sums[6],
        norm_sums[7],
        up2,
        down2,
    )


def solution(mesh):
    in_specs = (
        P("mod", None, None),
        P("mod", "tok", None),
        P("mod", None, None),
        P("mod"),
        P("mod"),
        P("mod"),
        P("mod", None, None),
        P(),
        P(),
        P(),
        P(),
        P(None, "head"),
        P(None, "head"),
        P(None, "head"),
        P("head", None),
        P(),
        P(),
        P(None, "head"),
        P("head", None),
        P(),
        P(),
        P(None, "head"),
        P(None, "head"),
        P(None, "head"),
        P("head", None),
        P(),
        P(),
        P(None, "head"),
        P("head", None),
    )
    out_specs = (
        P("mod", None, None),
        P("mod", None, None),
        P("mod", "tok", None),
        P("mod", None, None),
        P(),
        P(),
        P(),
        P(),
        P(None, "head"),
        P(None, "head"),
        P(None, "head"),
        P("head", None),
        P(),
        P(),
        P(None, "head"),
        P("head", None),
        P(),
        P(),
        P(None, "head"),
        P(None, "head"),
        P(None, "head"),
        P("head", None),
        P(),
        P(),
        P(None, "head"),
        P("head", None),
    )
    return jax.shard_map(
        on_device, mesh=mesh, in_specs=in_specs, out_specs=out_specs, check_vma=False
    )
```

```python
import functools

import jax
import jax.numpy as jnp
from jax import lax
from jax.experimental import pallas as pl
from jax.experimental.pallas import tpu as pltpu
from jax.sharding import PartitionSpec as P

HEAD = 64
PATCH = 392
EPSILON = 1e-05
NEGATIVE = -1e30
LOG2E = 1.4426950408889634
STAT = 16
BF = jnp.bfloat16
F32 = jnp.float32
VMEM_LIMIT = 60 * 2**20
SIDE_X, SIDE_Y, MOD = range(3)


def dot(a, b):
    return jnp.dot(a, b, preferred_element_type=F32)


def dot_tn(a, b):
    return lax.dot_general(a, b, (((0,), (0,)), ((), ())), preferred_element_type=F32)


def dot_nt(a, b):
    return lax.dot_general(a, b, (((1,), (1,)), ((), ())), preferred_element_type=F32)


def normalize(rows):
    mean = jnp.mean(rows, -1, keepdims=True)
    centered = rows - mean
    rstd = lax.rsqrt(jnp.mean(centered * centered, -1, keepdims=True) + EPSILON)
    return centered * rstd, rstd


def normed_rows(rows, gain, bias):
    return (normalize(rows)[0] * gain + bias).astype(BF)


def norm_back(grad_out, rows, gain):
    normed, rstd = normalize(rows)
    scaled = grad_out * gain
    grad_in = rstd * (
        scaled
        - jnp.mean(scaled, -1, keepdims=True)
        - normed * jnp.mean(scaled * normed, -1, keepdims=True)
    )
    return grad_in, jnp.sum(grad_out * normed, 0, keepdims=True), jnp.sum(grad_out, 0, keepdims=True)


def row_sums(a):
    n, width = a.shape
    if n % 8:
        a = jnp.concatenate([a, jnp.zeros((8 - n % 8, width), a.dtype)], 0)
    return jnp.sum(a.reshape(-1, 8, width), 0)


def erf(x):
    x = jnp.clip(x, -4.0, 4.0)
    s = x * x
    top = -2.72614225801306e-10
    for c in (
        2.77068142495902e-08,
        -2.10102402082508e-06,
        -5.69250639462346e-05,
        -7.34990630326855e-04,
        -2.95459980854025e-03,
        -1.60960333262415e-02,
    ):
        top = top * s + c
    low = -1.45660718464996e-05
    for c in (
        -2.13374055278905e-04,
        -1.68282697438203e-03,
        -7.37332916720468e-03,
        -1.42647390514189e-02,
    ):
        low = low * s + c
    return x * top / low


def gelu_share(x):
    return 0.5 * (1.0 + erf(x * 0.7071067811865476))


def gelu_slope(x):
    return gelu_share(x) + x * (0.3989422804014327 * jnp.exp(-0.5 * x * x))


def parts_of(value, count):
    parts = []
    for _ in range(count):
        part = value.astype(BF).astype(F32)
        parts.append(part)
        value = value - part
    return parts


def stat_tile(rows, height):
    place = lax.broadcasted_iota(jnp.int32, (height, rows[0].shape[1]), 0)
    tile = jnp.zeros(place.shape, F32)
    for k, row in enumerate(rows):
        tile = jnp.where(place == k, row, tile)
    return tile.astype(BF)


def diagonal(rows, row_block, column_block, count):
    shape = (row_block * count, column_block * count)
    r = lax.broadcasted_iota(jnp.int32, shape, 0) // row_block
    c = lax.broadcasted_iota(jnp.int32, shape, 1) // column_block
    return jnp.where(r == c, rows, 0.0).astype(BF)


def blocks_down(rows, count):
    return diagonal(jnp.concatenate([rows] * count, 0), rows.shape[0], HEAD, count)


def blocks_across(rows_t, count):
    return diagonal(jnp.concatenate([rows_t] * count, 1), HEAD, rows_t.shape[1], count)


def diagonal_parts(table, lat, count):
    return [
        table[HEAD * h : HEAD * (h + 1), lat * h : lat * (h + 1)] for h in range(count)
    ]


def cost_of(us):
    return pl.CostEstimate(flops=int(us * 1e9), bytes_accessed=0, transcendentals=0)


NO_COST = cost_of(0)


def kernel_call(body, outs, *args, name, scalars=(), scratch=(), deps=(), beside=0.0):
    spec = pl.BlockSpec(memory_space=pltpu.VMEM)
    smem = pl.BlockSpec(memory_space=pltpu.SMEM)
    first, count = len(scalars) + len(args), len(deps)
    return pl.pallas_call(
        lambda *refs: body(*refs[:first], *refs[first + count :]),
        out_shape=[jax.ShapeDtypeStruct(s, t) for s, t in outs],
        in_specs=[smem] * len(scalars)
        + [spec] * len(args)
        + [pl.BlockSpec(memory_space=pl.ANY)] * len(deps),
        out_specs=[spec] * len(outs),
        scratch_shapes=[pltpu.VMEM(s, t) for s, t in scratch],
        compiler_params=pltpu.CompilerParams(vmem_limit_bytes=VMEM_LIMIT),
        cost_estimate=cost_of(beside),
        name=name,
    )(*scalars, *args, *deps)


def tie(x, *deps, beside=0.0):
    anywhere = pl.BlockSpec(memory_space=pl.ANY)
    return pl.pallas_call(
        lambda *refs: None,
        out_shape=jax.ShapeDtypeStruct(x.shape, x.dtype),
        in_specs=[anywhere] * (1 + len(deps)),
        out_specs=anywhere,
        input_output_aliases={0: 0},
        cost_estimate=cost_of(beside),
        name="tie",
    )(x, *deps)


def stack_kernel(*refs):
    for k, ref in enumerate(refs[:-1]):
        refs[-1][k] = ref[...]


def concat_kernel(*refs):
    row = 0
    for ref in refs[:-1]:
        refs[-1][row : row + ref.shape[0]] = ref[...]
        row += ref.shape[0]


def join_halves(target, part, other, mod, at, n):
    target[pl.ds(pl.multiple_of(mod * n, 16), n)] = part[at : at + n]
    target[pl.ds(pl.multiple_of((1 - mod) * n, 16), n)] = other[at : at + n]


def pack_kernel(plan, *refs, counts):
    outs = refs[-len(counts) :]
    at = 0
    for out, count in zip(outs, counts):
        row = 0
        for ref in refs[at : at + count]:
            out[row : row + ref.shape[0]] = ref[...]
            row += ref.shape[0]
        at += count


def pack_halves(at, plan, groups):
    arrays = [a for g in groups for a in g]
    spec = lambda a: pl.BlockSpec((a.shape[0] // 2, a.shape[1]), lambda i, p: (p[at.mod], 0))
    shapes = [(sum(a.shape[0] // 2 for a in g), g[0].shape[1]) for g in groups]
    return pl.pallas_call(
        functools.partial(pack_kernel, counts=[len(g) for g in groups]),
        grid_spec=pltpu.PrefetchScalarGridSpec(
            num_scalar_prefetch=1,
            grid=(1,),
            in_specs=[spec(a) for a in arrays],
            out_specs=[pl.BlockSpec(s, lambda i, m: (0, 0)) for s in shapes],
        ),
        out_shape=[jax.ShapeDtypeStruct(s, BF) for s in shapes],
        compiler_params=pltpu.CompilerParams(vmem_limit_bytes=VMEM_LIMIT),
        cost_estimate=NO_COST,
        name="pack_halves",
    )(plan, *arrays)


def tables_kernel(plan, gathered_ref, pair_ref, pair_t_ref, query_t_ref):
    parts, _, rows, width = gathered_ref.shape
    own = parts * rows // 3
    for k in range(4):
        x, y = lax.rem(plan[SIDE_X] + k % 2, 2), lax.rem(plan[SIDE_Y] + k // 2, 2)
        shard = 2 * y + x
        for i, (target, start) in enumerate(((pair_t_ref, 0), (pair_t_ref, width), (query_t_ref, 0))):
            for p in range(parts):
                low, high = max(own * i, rows * p), min(own * (i + 1), rows * (p + 1))
                if low < high:
                    to = start + own * k + low - own * i
                    target[to : to + high - low] = gathered_ref[
                        p, shard, low - rows * p : high - rows * p
                    ]
    for c in range(0, 2 * width, 256):
        pair_ref[:, c : c + 256] = pair_t_ref[c : c + 256].astype(F32).T.astype(BF)


class Plan:
    def __init__(self, clips, blocks):
        steps = clips * blocks
        self.clips, self.blocks, self.size = clips, blocks, 0
        for name, length in (
            ("side_x", 1), ("side_y", 1), ("mod", 1), ("share", 1), ("some", 1), ("keep", 1), ("tok", 1),
            ("clip_plain", clips), ("count_plain", clips), ("text_plain", clips),
            ("read_clip", steps), ("read_block", steps), ("zero_clip", steps), ("zero_block", steps),
            ("clip", clips), ("count", clips), ("text", clips),
            ("back_clip", steps), ("back_block", steps),
        ):
            setattr(self, name, self.size)
            self.size += length

    def calls(self):
        return ((0, self.clips),)


def plan_kernel(place_ref, frames_ref, lengths_ref, drop_ref, plan, order, *, at, rows, span):
    clips, blocks = at.clips, at.blocks
    zones = clips // 2
    tok, side_x, side_y, mod, last = (place_ref[i] for i in range(5))
    zone = lax.rem(tok, zones)
    plan[at.side_x], plan[at.side_y], plan[at.mod], plan[at.share] = side_x, side_y, mod, last
    plan[at.tok] = tok
    drops = [drop_ref[c] for c in range(clips)]
    for c in range(clips):
        rank = sum(
            (drops[o] < drops[c]).astype(jnp.int32)
            if o > c
            else (drops[o] <= drops[c]).astype(jnp.int32)
            for o in range(clips)
            if o != c
        )
        order[rank] = c

    def tables(side, clip_at, count_at, text_at, share):
        flags = []
        for p in range(clips):
            clip = order[2 * lax.rem(zone + p // 2, zones) + lax.rem(p + side, 2)]
            live = 1 - drop_ref[clip]
            count = jnp.clip(frames_ref[clip] * PATCH - tok * span, 0, span) * live
            plan[clip_at + p] = clip
            plan[count_at + p] = count
            plan[text_at + p] = lengths_ref[clip] * live * share
            flags += [((count > b * rows).astype(jnp.int32), clip, b) for b in range(blocks)]
        return flags

    def hold(flags, wanted, clip_at, block_at):
        clip, block = flags[0][1], jnp.int32(0)
        for flag, c, b in flags[::-1]:
            clip = jnp.where(flag == wanted, c, clip)
            block = jnp.where(flag == wanted, b, block)
        for i, (flag, c, b) in enumerate(flags):
            clip = jnp.where(flag == wanted, c, clip)
            block = jnp.where(flag == wanted, b, block)
            plan[clip_at + i] = clip
            plan[block_at + i] = block

    flags = tables(0, at.clip_plain, at.count_plain, at.text_plain, last)
    hold(flags, 1, at.read_clip, at.read_block)
    hold(flags, 0, at.zero_clip, at.zero_block)
    flags = tables(side_y, at.clip, at.count, at.text, 1)
    for i, (first, count) in enumerate(at.calls()):
        part = flags[first * blocks : (first + count) * blocks]
        hold(part, 1, at.back_clip + first * blocks, at.back_block + first * blocks)
        plan[at.some + i] = sum(f for f, _, _ in part)
    plan[at.keep] = 1 - drop_ref[plan[at.clip]]


def make_plan(at, places, frames, lengths, drops, rows, span):
    smem = pl.BlockSpec(memory_space=pltpu.SMEM)
    return pl.pallas_call(
        functools.partial(plan_kernel, at=at, rows=rows, span=span),
        out_shape=jax.ShapeDtypeStruct((at.size,), jnp.int32),
        in_specs=[smem] * 4,
        out_specs=smem,
        scratch_shapes=[pltpu.SMEM((at.clips,), jnp.int32)],
        cost_estimate=NO_COST,
        name="plan",
    )(places, frames, lengths, drops)


def own_rows_kernel(plan, latents, mine, other, latents_ref, mine_ref, other_ref, keep_ref, *, at):
    latents_ref[...] = latents[0]
    mine_ref[...] = mine[0]
    other_ref[...] = other[0]
    keep_ref[...] = jnp.full(keep_ref.shape, plan[at.keep].astype(F32))


def own_rows(at, plan, latents, cotangent):
    lat, width = latents.shape[1:]
    spec = lambda k: pl.BlockSpec((1, lat, width), lambda i, p: (p[at.clip + k], 0, 0))
    whole = lambda *shape: pl.BlockSpec(shape, lambda i, p: (0,) * len(shape))
    return pl.pallas_call(
        functools.partial(own_rows_kernel, at=at),
        grid_spec=pltpu.PrefetchScalarGridSpec(
            num_scalar_prefetch=1,
            grid=(1,),
            in_specs=[spec(0), spec(0), spec(1)],
            out_specs=[whole(lat, width)] * 3 + [whole(1, width)],
        ),
        out_shape=[
            *[jax.ShapeDtypeStruct((lat, width), BF)] * 3,
            jax.ShapeDtypeStruct((1, width), F32),
        ],
        cost_estimate=NO_COST,
        name="own_rows",
    )(plan, latents, cotangent, cotangent)


def tokens_forward_kernel(
    plan, video_ref, text_ref, latents_ref, norms_ref, key_t_ref, value_t_ref, query_t_ref,
    zero_ref, *refs, at,
):
    outs, (key_ref, value_ref, blocks, peak, total, summed) = refs[:-6], refs[-6:]
    place, j = pl.program_id(0), pl.program_id(1)
    rows = video_ref.shape[1]
    lat = latents_ref.shape[1]
    width = key_ref.shape[1]
    heads = width // HEAD
    clip_count = plan[at.count_plain + place]
    text_count = plan[at.text_plain + place]
    count = clip_count - j * rows
    lat_gain, lat_bias, gain, bias = (norms_ref[i : i + 1] for i in range(4))

    @pl.when((place == 0) & (j == 0))
    def _():
        key_ref[...] = key_t_ref[...].astype(F32).T.astype(BF)
        value_ref[...] = value_t_ref[...].astype(F32).T.astype(BF)

    @pl.when(count <= 0)
    def _():
        zero_ref[...] = jnp.zeros_like(zero_ref)

    @pl.when((j == 0) & ((clip_count > 0) | (text_count > 0)))
    def _():
        queries_in = normed_rows(latents_ref[0].astype(F32), lat_gain, lat_bias)
        rows_t = dot_nt(query_t_ref[...], queries_in).astype(BF).astype(F32) * HEAD**-0.5
        blocks[...] = blocks_across(rows_t, heads)

    @pl.when(j == 0)
    def _():
        peak[...] = jnp.full_like(peak, NEGATIVE).astype(BF).astype(F32)
        total[...] = jnp.zeros_like(total)
        summed[...] = jnp.zeros_like(summed)

    def block(x, limit):
        inputs_in = normed_rows(x.astype(F32), gain, bias)
        key = dot(inputs_in, key_ref[...]).astype(BF)
        value = dot(inputs_in, value_ref[...]).astype(BF)
        mask = lax.broadcasted_iota(jnp.int32, (x.shape[0], 1), 0) < limit
        scores = jnp.where(mask, dot(key, blocks[...]) * LOG2E, NEGATIVE)
        before = peak[...]
        top = jnp.maximum(before, jnp.max(scores, 0, keepdims=True)).astype(BF).astype(F32)
        weights = jnp.exp2(scores - top)
        factor = jnp.exp2(before - top)
        peak[...] = top
        total[...] = total[...] * factor + jnp.sum(weights, 0, keepdims=True)
        table = dot_tn(value, weights.astype(BF))
        for h, part in enumerate(diagonal_parts(table, lat, heads)):
            r = slice(HEAD * h, HEAD * (h + 1))
            summed[r] = summed[r] * factor[:, lat * h : lat * (h + 1)] + part

    @pl.when(count > 0)
    def _():
        block(video_ref[0], count)

    @pl.when((j == 0) & (text_count > 0))
    def _():
        block(text_ref[0], text_count)

    for zone, out_ref in enumerate(outs):

        @pl.when((j == pl.num_programs(1) - 1) & (place // 2 == zone))
        def _(out_ref=out_ref):
            out_ref[0, :width] = summed[...].astype(BF)
            of = [slice(lat * h, lat * (h + 1)) for h in range(heads)]
            totals = [parts_of(total[:, c], 2) for c in of]
            stats = [peak[:, c] for c in of] + [t[0] for t in totals] + [t[1] for t in totals]
            out_ref[0, width:] = stat_tile(stats, STAT)


def tokens_forward(at, plan, video, text, latents, params, rows):
    clips, span, width = video.shape
    lat = latents.shape[1]
    own = params[-1].shape[0]
    blocks = span // rows
    full = lambda a: pl.BlockSpec(a.shape, lambda s, j, *_: (0,) * a.ndim)
    clip_spec = lambda a: pl.BlockSpec(
        (1,) + a.shape[1:], lambda s, j, p: (p[at.clip_plain + s], 0, 0)
    )
    block_spec = lambda clip, block: pl.BlockSpec(
        (1, rows, width), lambda s, j, p: (p[clip + s * blocks + j], p[block + s * blocks + j], 0)
    )
    return pl.pallas_call(
        functools.partial(tokens_forward_kernel, at=at),
        grid_spec=pltpu.PrefetchScalarGridSpec(
            num_scalar_prefetch=1,
            grid=(clips, blocks),
            in_specs=[
                block_spec(at.read_clip, at.read_block),
                clip_spec(text),
                clip_spec(latents),
            ]
            + [full(a) for a in params],
            out_specs=[block_spec(at.zero_clip, at.zero_block)]
            + [
                pl.BlockSpec(
                    (1, own + STAT, lat), lambda s, j, p, z=z: (jnp.clip(s - 2 * z, 0, 1), 0, 0)
                )
                for z in range(clips // 2)
            ],
            scratch_shapes=[
                pltpu.VMEM((width, own), BF),
                pltpu.VMEM((width, own), BF),
                pltpu.VMEM((own, own // HEAD * lat), BF),
                pltpu.VMEM((1, own // HEAD * lat), F32),
                pltpu.VMEM((1, own // HEAD * lat), F32),
                pltpu.VMEM((own, lat), F32),
            ],
        ),
        out_shape=[jax.ShapeDtypeStruct(video.shape, BF)]
        + [jax.ShapeDtypeStruct((2, own + STAT, lat), BF)] * (clips // 2),
        compiler_params=pltpu.CompilerParams(
            vmem_limit_bytes=VMEM_LIMIT, dimension_semantics=("arbitrary", "arbitrary")
        ),
        cost_estimate=cost_of(30.0),
        name="tokens_forward",
    )(plan, video, text, latents, *params)


GROUP = 4


def tokens_back_kernel(
    plan, *refs, at, call, carried, extra,
):
    video_ref, text_ref, latents_ref, norms_ref, pair_ref, pair_t_ref, query_t_ref = refs[:7]
    d0, d1, d2, d3 = refs[7:11]
    refs = refs[13:]
    if carried:
        before_ref, refs = refs[0], refs[1:]
    refs = refs[extra:]
    d_video_ref, d_text_ref, weights_ref, keep_ref, send_ref = refs[:5]
    d_query_refs = refs[5:-8]
    q_down, q_across, d_down, d_across, lse, delta, d_query, queries = refs[-8:]
    step, j = pl.program_id(0), pl.program_id(1)
    place = step + at.calls()[call][0]
    rows, width = video_ref.shape[1:]
    lat = latents_ref.shape[1]
    own = query_t_ref.shape[0] // 4
    own_heads = own // HEAD
    groups = width // (GROUP * HEAD)
    count = plan[at.count + place] - j * rows
    text_count = plan[at.text + place]
    alive = text_count > 0
    lat_gain, lat_bias, gain, bias = (norms_ref[i : i + 1] for i in range(4))

    @pl.when((step == 0) & (j == 0))
    def _():
        weights_ref[...] = before_ref[...] if carried else jnp.zeros_like(weights_ref)
        for ref in (q_down, q_across, d_down, d_across):
            ref[...] = jnp.zeros_like(ref)

    @pl.when(j == 0)
    def _():
        d_query[...] = jnp.zeros_like(d_query)

    @pl.when((j == 0) & alive)
    def _():
        mine = lax.rem(place, 2) == 0
        first = [jnp.where(mine, a[0, :own].astype(F32), b[0, own : 2 * own].astype(F32)) for a, b in ((d0, d2), (d1, d3))]
        second = [jnp.where(mine, a[0, own : 2 * own].astype(F32), b[0, :own].astype(F32)) for a, b in ((d0, d2), (d1, d3))]
        queries_in = normed_rows(latents_ref[0].astype(F32), lat_gain, lat_bias)
        queries[...] = queries_in
        query = dot_nt(queries_in, query_t_ref[...]).astype(BF).astype(F32) * HEAD**-0.5
        d_rows_t = jnp.concatenate(first + second, 0)
        column = lax.broadcasted_iota(jnp.int32, (lat, 2 * HEAD), 1) // HEAD
        for natural, rows_t, down, across in (
            (query, query.T, q_down, q_across),
            (d_rows_t.T, d_rows_t, d_down, d_across),
        ):
            for head in range(groups * GROUP):
                g, h = divmod(head, GROUP)
                across[g, HEAD * h : HEAD * (h + 1), lat * h : lat * (h + 1)] = rows_t[
                    HEAD * head : HEAD * (head + 1)
                ].astype(BF)
                pair = natural[:, 2 * HEAD * (head // 2) : 2 * HEAD * (head // 2 + 1)]
                at = 2 * HEAD * (h // 2)
                down[g, lat * h : lat * (h + 1), at : at + 2 * HEAD] = jnp.where(
                    column == h % 2, pair, 0.0
                ).astype(BF)
        tiles = [d[0, 2 * own : 2 * own + 2 * STAT].astype(F32) for d in (d0, d1, d2, d3)]
        n = 2 * own_heads
        for kind, first_row, count_of in ((delta, 0, 2), (lse, 2 * n, 3)):
            for shard in range(4):
                a, b = tiles[shard % 2], tiles[2 + shard % 2]
                for h in range(own_heads):
                    at_a = first_row + h + own_heads * (shard // 2)
                    at_b = first_row + h + own_heads * (1 - shard // 2)
                    row = sum(
                        jnp.where(mine, a[at_a + n * i : at_a + n * i + 1], b[at_b + n * i : at_b + n * i + 1])
                        for i in range(count_of)
                    )
                    head = shard * own_heads + h
                    kind[:, lat * head : lat * (head + 1)] = row

    share = plan[at.share].astype(F32)

    def block(x, video_rows):
        n = x.shape[0]
        spans = [(0, video_rows, lambda a: a), (video_rows, n, lambda a: a * share)]
        spans = [span for span in spans if span[0] < span[1]]
        normed, rstd = normalize(x.astype(F32))
        inputs_in = (normed * gain + bias).astype(BF)
        key = dot(inputs_in, pair_ref[:, :width]).astype(BF)
        value = dot(inputs_in, pair_ref[:, width:]).astype(BF)
        index = lax.broadcasted_iota(jnp.int32, (n, 1), 0)
        mask = index < count if video_rows else index < text_count
        if 0 < video_rows < n:
            mask = jnp.where(index < video_rows, index, n * n) < count
            mask = mask | ((index >= video_rows) & (index < video_rows + text_count))
        d_keys, d_values = [], []
        for g in range(groups):
            cut = slice(GROUP * HEAD * g, GROUP * HEAD * (g + 1))
            lanes = slice(GROUP * lat * g, GROUP * lat * (g + 1))
            scores = dot(key[:, cut], q_across[g])
            d_probs = dot(value[:, cut], d_across[g])
            probs = jnp.where(mask, jnp.exp2(scores * LOG2E - lse[:, lanes]), 0.0)
            d_scores = (probs * (d_probs - delta[:, lanes])).astype(BF)
            d_values.append(dot(probs.astype(BF), d_down[g]).astype(BF))
            d_keys.append(dot(d_scores, q_down[g]).astype(BF))
            if g == 0:
                for a, b, counted in spans:
                    table = dot_tn(key[a:b, cut], d_scores[a:b])
                    for h, part in enumerate(diagonal_parts(table, lat, own_heads)):
                        d_query[HEAD * h : HEAD * (h + 1)] += counted(part)
        d_key, d_value = jnp.concatenate(d_keys, 1), jnp.concatenate(d_values, 1)
        d_in = dot(d_key, pair_t_ref[:width]) + dot(d_value, pair_t_ref[width:])
        for a, b, counted in spans:
            rows_in, part = inputs_in[a:b], d_in[a:b]
            weights_ref[:own] += counted(dot_tn(d_keys[0][a:b], rows_in)[:own])
            weights_ref[own : 2 * own] += counted(dot_tn(d_values[0][a:b], rows_in)[:own])
            weights_ref[3 * own : 3 * own + 8] += counted(row_sums(part * normed[a:b]))
            weights_ref[3 * own + 8 : 3 * own + 16] += counted(row_sums(part))
        scaled = d_in * gain
        d_x = rstd * (
            scaled
            - jnp.mean(scaled, -1, keepdims=True)
            - normed * jnp.mean(scaled * normed, -1, keepdims=True)
        )
        if video_rows:
            d_video_ref[0] = d_x[:video_rows].astype(BF)
        if video_rows < n:
            d_text_ref[0] = d_x[video_rows:].astype(BF)

    joined = rows % 16 == 0

    @pl.when((count > 0) & (j > 0 if joined else True))
    def _():
        block(video_ref[0], rows)

    if joined:

        @pl.when((j == 0) & alive & (count > 0))
        def _():
            block(jnp.concatenate([video_ref[0], text_ref[0]], 0), rows)

    @pl.when((plan[at.some + call] == 0) & (step == 0) & (j == 0))
    def _():
        d_video_ref[...] = jnp.zeros_like(d_video_ref)

    @pl.when((j == 0) & alive & ((count <= 0) if joined else True))
    def _():
        block(text_ref[0], 0)

    @pl.when((j == 0) & jnp.logical_not(alive))
    def _():
        d_text_ref[...] = jnp.zeros_like(d_text_ref)

    @pl.when(j == pl.num_programs(1) - 1)
    def _():
        d_rows = (d_query[...] * HEAD**-0.5).astype(BF)
        for zone, d_query_ref in enumerate(d_query_refs):

            @pl.when(place // 2 == zone)
            def _(d_query_ref=d_query_ref):
                d_query_ref[0] = d_rows

        @pl.when(alive)
        def _():
            weights_ref[2 * own : 3 * own] += dot(d_rows, queries[...])

        @pl.when(step == pl.num_programs(0) - 1)
        def _():
            half = width // 2
            side = plan[at.mod]
            keep_ref[...] = weights_ref[:, pl.ds(pl.multiple_of(side * half, half), half)]
            send_ref[...] = weights_ref[
                :, pl.ds(pl.multiple_of((1 - side) * half, half), half)
            ].astype(BF)


WEIGHT_ROWS = 64


def tokens_back(at, plan, call, video, text, latents, params, arrived, filled, before, rows, deps=()):
    first, steps = at.calls()[call]
    span, width = video.shape[1:]
    blocks = span // rows
    lat = latents.shape[1]
    own = params[-1].shape[0] // 4
    groups = width // (GROUP * HEAD)
    full = lambda a: pl.BlockSpec(
        a.shape, lambda s, j, *_: (0,) * a.ndim, pipeline_mode=pl.Buffered(1)
    )
    clip_spec = lambda a: pl.BlockSpec(
        (1,) + a.shape[1:], lambda s, j, p: (p[at.clip + first + s], 0, 0)
    )
    index = lambda p, table, s, j: p[table + (first + s) * blocks + j]
    video_spec = pl.BlockSpec(
        (1, rows, width),
        lambda s, j, p: (index(p, at.back_clip, s, j), index(p, at.back_block, s, j), 0),
    )
    weight_shape = (3 * own + WEIGHT_ROWS, width)
    half_shape = (weight_shape[0], width // 2)
    operands = [video, text, latents, *params, *arrived]
    in_specs = [video_spec, clip_spec(text), clip_spec(latents)]
    in_specs += [full(a) for a in params]
    in_specs += [
        pl.BlockSpec(
            (1, 2 * own + 2 * STAT, lat), lambda s, j, *_: ((s + first) // 2 - first // 2, 0, 0)
        )
        for a in arrived
    ]
    start = 1 + len(operands)
    operands += filled
    in_specs += [pl.BlockSpec(memory_space=pl.ANY)] * 2
    if before is not None:
        operands += [before]
        in_specs += [full(before)]
    operands += deps
    in_specs += [pl.BlockSpec(memory_space=pl.ANY)] * len(deps)
    return pl.pallas_call(
        functools.partial(
            tokens_back_kernel, at=at, call=call, carried=before is not None, extra=len(deps)
        ),
        grid_spec=pltpu.PrefetchScalarGridSpec(
            num_scalar_prefetch=1,
            grid=(steps, blocks),
            in_specs=in_specs,
            out_specs=[
                video_spec,
                clip_spec(text),
                pl.BlockSpec(weight_shape, lambda s, j, *_: (0, 0)),
            ]
            + [pl.BlockSpec(half_shape, lambda s, j, *_: (0, 0))] * 2
            + [
                pl.BlockSpec((1, own, lat), lambda s, j, p, z=z: (jnp.clip(s - 2 * z, 0, 1), 0, 0))
                for z in range(at.clips // 2)
            ],
            scratch_shapes=[
                pltpu.VMEM((groups, GROUP * lat, GROUP * HEAD), BF),
                pltpu.VMEM((groups, GROUP * HEAD, GROUP * lat), BF),
                pltpu.VMEM((groups, GROUP * lat, GROUP * HEAD), BF),
                pltpu.VMEM((groups, GROUP * HEAD, GROUP * lat), BF),
                pltpu.VMEM((1, groups * GROUP * lat), F32),
                pltpu.VMEM((1, groups * GROUP * lat), F32),
                pltpu.VMEM((own, lat), F32),
                pltpu.VMEM((lat, width), BF),
            ],
        ),
        out_shape=[
            jax.ShapeDtypeStruct(video.shape, BF),
            jax.ShapeDtypeStruct(text.shape, BF),
            jax.ShapeDtypeStruct(weight_shape, F32),
            jax.ShapeDtypeStruct(half_shape, F32),
            jax.ShapeDtypeStruct(half_shape, BF),
        ]
        + [jax.ShapeDtypeStruct((2, own, lat), BF)] * (at.clips // 2),
        input_output_aliases={start: 0, start + 1: 1},
        compiler_params=pltpu.CompilerParams(
            vmem_limit_bytes=VMEM_LIMIT, dimension_semantics=("arbitrary", "arbitrary")
        ),
        cost_estimate=cost_of(10.0),
        name="tokens_back",
    )(plan, *operands)


def combine_kernel(plan, output_ref, *refs):
    parts, (mine_ref, other_ref, low_ref, *branch_refs) = refs[:-5], refs[-5:]
    own = parts[0].shape[1] - STAT
    lat = parts[0].shape[2]
    heads = own // HEAD
    results = []
    for y in range(2):
        tiles = [p[y, own:].astype(F32) for p in parts]
        attended, logs = [], []
        for h in range(heads):
            peaks = [t[h : h + 1] for t in tiles]
            top = peaks[0]
            for p in peaks[1:]:
                top = jnp.maximum(top, p)
            total = jnp.zeros((1, lat), F32)
            summed = jnp.zeros((HEAD, lat), F32)
            for p, t, peak in zip(parts, tiles, peaks):
                factor = jnp.exp2(peak - top)
                a = t[heads + h : heads + h + 1] + t[2 * heads + h : 2 * heads + h + 1]
                total = total + a * factor
                summed = summed + p[y, HEAD * h : HEAD * (h + 1)].astype(F32) * factor
            some = total > 0.0
            safe = jnp.where(some, total, 1.0)
            attended.append(jnp.where(some, summed / safe, 0.0))
            logs.append(parts_of(jnp.where(some, top + jnp.log2(safe), 0.0), 3))
        stats = [logs[h][i] for i in range(3) for h in range(heads)]
        results.append((jnp.concatenate(attended, 0), stat_tile(stats, STAT).astype(F32)))
    first = plan[SIDE_Y] == 0
    for k, (ref, (a, b)) in enumerate(((mine_ref, results), (other_ref, results[::-1]))):
        low = jnp.where(first, a[0], b[0]).astype(BF)
        ref[:own] = low
        ref[own:] = jnp.where(first, a[1], b[1]).astype(BF)
        low_ref[k] = low
        branch_refs[k][...] = dot_tn(low, output_ref[...]).astype(BF)


def spread(norms_ref, row):
    return norms_ref[row : row + 1], norms_ref[row + 1 : row + 2]


def sum_of(terms):
    total = terms[0]
    for term in terms[1:]:
        total = total + term
    return total


def received_sum(part0, part1):
    return part0[...].astype(F32) + part1[...].astype(F32)


def cross_forward_kernel(
    plan, b0, b1, b2, b3, latents_ref, keep_ref, norms_ref, up0, down0, near, far,
    first_ref, inner_ref, pre_ref, hidden_ref, part_ref, up1, down1,
):
    join_mlp(near, far, plan[MOD], up1, down1)
    branch = received_sum(b0, b1) + received_sum(b2, b3)
    first = latents_ref[...].astype(F32) + keep_ref[...] * branch
    first_ref[...] = first
    inner = normed_rows(first, *spread(norms_ref, 4))
    inner_ref[...] = inner
    terms = []
    for k, (up, down) in enumerate(((up0, down0), (up1, down1))):
        pre = dot(inner, up[...])
        pre_ref[k] = pre
        hidden = (pre * gelu_share(pre)).astype(BF)
        hidden_ref[k] = hidden
        terms.append(dot(hidden, down[...]))
    part_ref[...] = sum_of(terms).astype(BF)


def join_mlp(near, far, mod, up, down):
    half = up.shape[0] // 2
    join_halves(up, near, far, mod, 0, half)
    join_halves(down, near, far, mod, half, half)


def join_self(near, far, mod, targets):
    half, start = targets.shape[1] // 2, targets.shape[2]
    for i in range(4):
        join_halves(targets.at[i], near, far, mod, start + half * i, half)


def self_forward_kernel(
    plan, first_ref, part0, part1, norms_ref, wq, wk, wv, wo, near, far, inner1_ref, hidden1_ref,
    second_ref, inner_ref, rows_ref, query_t_ref, attended_ref, lse_ref, part_ref, moving_ref, joined,
):
    join_self(near, far, plan[MOD], joined)
    second = first_ref[...] + received_sum(part0, part1)
    second_ref[...] = second
    inner = normed_rows(second, *spread(norms_ref, 6))
    inner_ref[...] = inner
    lat = inner.shape[0]
    own = wq.shape[0]
    heads = own // HEAD
    terms = []
    for k, (q, w, v, o) in enumerate(((wq, wk, wv, wo), [joined.at[i] for i in range(4)])):
        query = (dot_nt(inner, q[...]).astype(BF).astype(F32) * HEAD**-0.5).astype(BF)
        key = dot_nt(inner, w[...]).astype(BF)
        value = dot_nt(inner, v[...]).astype(BF)
        for i, a in enumerate((query, key, value)):
            rows_ref[k, i] = a
        query_t = dot_nt(q[...], inner).astype(BF).astype(F32) * HEAD**-0.5
        query_t_ref[k] = query_t.astype(BF)
        scores = dot(key, blocks_across(query_t, heads)) * LOG2E
        top = jnp.max(scores, 0, keepdims=True)
        weights = jnp.exp2(scores - top)
        total = jnp.sum(weights, 0, keepdims=True)
        table = dot_tn(value, weights.astype(BF))
        attended = jnp.concatenate(
            [
                part / total[:, lat * h : lat * (h + 1)]
                for h, part in enumerate(diagonal_parts(table, lat, heads))
            ],
            0,
        )
        attended_ref[k] = attended
        lse_ref[k] = top + jnp.log2(total)
        terms.append(dot_tn(attended.astype(BF), o[...]))
    part_ref[...] = sum_of(terms).astype(BF)
    for i, a in enumerate((inner1_ref[...], hidden1_ref[1], inner)):
        moving_ref[lat * i : lat * (i + 1)] = a


def hidden_back(grad_low, pre, up, down):
    d_hidden = dot_nt(grad_low, down[...])
    d_pre = (d_hidden * gelu_slope(pre)).astype(BF)
    return d_pre, dot_nt(d_pre, up[...])


def last_back_kernel(
    plan, second_ref, part0, part1, cotangent_ref, norms_ref, up0, down0, near, far,
    third_ref, inner_ref, hidden_ref, d_pre_ref, part_ref, moving_ref, up1, down1,
):
    join_mlp(near, far, plan[MOD], up1, down1)
    third = second_ref[...] + received_sum(part0, part1)
    third_ref[...] = third
    inner = normed_rows(third, *spread(norms_ref, 8))
    inner_ref[...] = inner
    terms = []
    for k, (up, down) in enumerate(((up0, down0), (up1, down1))):
        pre = dot(inner, up[...])
        hidden_ref[k] = (pre * gelu_share(pre)).astype(BF)
        d_pre_ref[k], term = hidden_back(cotangent_ref[...], pre, up, down)
        terms.append(term)
    part_ref[...] = sum_of(terms).astype(BF)
    lat = inner.shape[0]
    for i, a in enumerate((inner, d_pre_ref[1], hidden_ref[1])):
        moving_ref[lat * i : lat * (i + 1)] = a


def down_kernel(plan, hidden_ref, down0, near, far, part_ref, down1):
    half = down1.shape[0] // 2
    join_halves(down1, near, far, plan[MOD], half, half)
    part_ref[...] = (dot(hidden_ref[0], down0[...]) + dot(hidden_ref[1], down1[...])).astype(BF)


def self_back_kernel(
    plan, cotangent_ref, third_ref, part0, part1, norms_ref,
    rows_ref, query_t_ref, attended_ref, lse_ref, wq, wk, wv, wo, near, far,
    grad_ref, sums_ref, branch_ref, d_rows_ref, low_ref, part_ref, moving_ref, joined,
):
    join_self(near, far, plan[MOD], joined)
    d_inner = received_sum(part0, part1)
    d_x, d_gain, d_bias = norm_back(d_inner, third_ref[...], spread(norms_ref, 8)[0])
    grad = cotangent_ref[...].astype(F32) + d_x
    grad_ref[...] = grad
    sums_ref[0:1] = d_gain
    sums_ref[1:2] = d_bias
    branch = grad.astype(BF)
    branch_ref[...] = branch
    lat = grad.shape[0]
    own = wq.shape[0]
    heads = own // HEAD
    terms = []
    for k, weights in enumerate(((wq, wk, wv, wo), [joined.at[i] for i in range(4)])):
        o = weights[3]
        query, key, value = rows_ref[k, 0], rows_ref[k, 1], rows_ref[k, 2]
        d_att = dot_nt(branch, o[...]).astype(BF).astype(F32)
        d_att_t = dot_nt(o[...], branch).astype(BF).astype(F32)
        attended = attended_ref[k]
        low_ref[k] = attended.astype(BF)
        product = d_att_t * attended
        delta = jnp.concatenate(
            [
                jnp.sum(product[HEAD * h : HEAD * (h + 1)], 0, keepdims=True)
                for h in range(heads)
            ],
            1,
        )
        scores = dot(key, blocks_across(query_t_ref[k].astype(F32), heads))
        d_probs = dot(value, blocks_across(d_att_t, heads))
        probs = jnp.exp2(scores * LOG2E - lse_ref[k])
        d_scores = (probs * (d_probs - delta)).astype(BF)
        d_value = dot(probs.astype(BF), blocks_down(d_att, heads)).astype(BF)
        d_key = dot(d_scores, blocks_down(query.astype(F32), heads)).astype(BF)
        table = dot_tn(d_scores, key)
        column = lax.broadcasted_iota(jnp.int32, (lat, own), 1) // HEAD
        d_query = sum_of(
            [jnp.where(column == h, table[lat * h : lat * (h + 1)], 0.0) for h in range(heads)]
        )
        d_query = (d_query * HEAD**-0.5).astype(BF)
        for i, a in enumerate((d_query, d_key, d_value)):
            d_rows_ref[k, i] = a
            terms.append(dot(a, weights[i][...]))
            if k == 1:
                moving_ref[lat:, own * i : own * (i + 1)] = a
    part_ref[...] = sum_of(terms).astype(BF)
    moving_ref[:lat] = branch
    moving_ref[lat:, 3 * own :] = attended_ref[1].T.astype(BF)


def cross_back_kernel(
    plan, grad_ref, second_ref, part0, part1, norms_ref, pre_ref, up0, down0, near, far,
    out_ref, sums_ref, low_ref, d_pre_ref, part_ref, moving_ref, up1, down1,
):
    join_mlp(near, far, plan[MOD], up1, down1)
    d_inner = received_sum(part0, part1)
    d_x, d_gain, d_bias = norm_back(d_inner, second_ref[...], spread(norms_ref, 6)[0])
    grad = grad_ref[...] + d_x
    out_ref[...] = grad
    sums_ref[0:1] = d_gain
    sums_ref[1:2] = d_bias
    grad_low = grad.astype(BF)
    low_ref[...] = grad_low
    terms = []
    for k, (up, down) in enumerate(((up0, down0), (up1, down1))):
        d_pre_ref[k], term = hidden_back(grad_low, pre_ref[k], up, down)
        terms.append(term)
    part_ref[...] = sum_of(terms).astype(BF)
    lat = grad.shape[0]
    moving_ref[:lat] = d_pre_ref[1]
    moving_ref[lat:] = grad_low


def attended_back_kernel(
    plan, grad_ref, first_ref, part0, part1, norms_ref, keep_ref, a0, a2, o0, near, far,
    branch_ref, packed_ref, first_grad_ref, sums_ref, o2,
):
    own, width = o0.shape
    join_halves(o2, near, far, plan[MOD], width + 2 * own, own // 2)
    d_inner = received_sum(part0, part1)
    d_x, d_gain, d_bias = norm_back(d_inner, first_ref[...], spread(norms_ref, 4)[0])
    grad = grad_ref[...] + d_x
    branch = (keep_ref[...] * grad).astype(BF)
    branch_ref[...] = branch
    own = o0.shape[0]
    heads = own // HEAD
    deltas, logs = [], []
    for k, (a, o) in enumerate(((a0, o0), (a2, o2))):
        d_att_t = dot_nt(o[...], branch).astype(BF)
        packed_ref[own * k : own * (k + 1)] = d_att_t
        product = d_att_t.astype(F32) * a[:own].astype(F32)
        tile = a[own:].astype(F32)
        for h in range(heads):
            deltas.append(
                parts_of(jnp.sum(product[HEAD * h : HEAD * (h + 1)], 0, keepdims=True), 2)
            )
            logs.append([tile[heads * i + h : heads * i + h + 1] for i in range(3)])
    rows = [d[i] for i in range(2) for d in deltas] + [g[i] for i in range(3) for g in logs]
    packed_ref[2 * own : 2 * own + 2 * STAT] = stat_tile(rows, 2 * STAT)
    first_grad_ref[...] = grad
    sums_ref[0:1] = d_gain
    sums_ref[1:2] = d_bias


def half_rows_kernel(plan, third_ref, out0, out1, out_ref, hold):
    half = out_ref.shape[0]
    hold[...] = third_ref[...] + received_sum(out0, out1)
    cut = pl.ds(pl.multiple_of(plan[SIDE_X] * half, half), half)
    out_ref[...] = hold[cut].astype(BF)


def latent_back_kernel(
    plan, grad_ref, latents_ref, norms_ref, d0, d1, d2, d3, query_t_ref,
    cross_sums, self_sums, ffn_sums, out_ref, hold,
):
    own, lat = d0.shape
    half = lat // 2
    d_in = sum_of(
        [dot_tn(d[...], query_t_ref[own * k : own * (k + 1)]) for k, d in enumerate((d0, d1, d2, d3))]
    )
    d_x, d_gain, d_bias = norm_back(
        d_in, latents_ref[...].astype(F32), spread(norms_ref, 0)[0]
    )
    hold[...] = grad_ref[...] + d_x
    cut = pl.ds(pl.multiple_of(plan[SIDE_X] * half, half), half)
    out_ref[:half] = hold[cut].astype(BF)
    sums = [d_gain, d_bias]
    sums += [ref[i : i + 1] for ref in (cross_sums, self_sums, ffn_sums) for i in range(2)]
    out_ref[half:] = stat_tile(sums, STAT)


def tail_pack_kernel(plan, keep_ref, arrived_ref, own_ref, *outs, at):
    zones = len(outs) + 1
    step = own_ref.shape[0]
    for k, out in enumerate((own_ref, *outs)):
        cut = pl.ds(pl.multiple_of(lax.rem(plan[at.tok] + k, zones) * step, 16), step)
        out[...] = (keep_ref[cut] + arrived_ref[cut].astype(F32)).astype(out.dtype)


def query_sum_kernel(*refs):
    parts, outs = refs[:-2], refs[-2:]
    for i, out in enumerate(outs):
        out[...] = sum_of([p[i].astype(F32) for p in parts]).astype(BF)


def share_sum_kernel(*refs):
    refs[-1][...] = sum_of([p[...].astype(F32) for p in refs[:-1]]).astype(BF)


def token_weights_kernel(plan, mine_ref, other_ref, key_ref, value_ref, query_ref, sums_ref, whole, *, at):
    zones, step, half = mine_ref.shape
    own = key_ref.shape[0]
    side = plan[at.mod]
    for k in range(zones):
        cut = pl.ds(pl.multiple_of(lax.rem(plan[at.tok] + k, zones) * step, 16), step)
        for ref, x in ((mine_ref, side), (other_ref, 1 - side)):
            whole[cut, pl.ds(pl.multiple_of(x * half, half), half)] = ref[k].astype(F32)
    for i, ref in enumerate((key_ref, value_ref, query_ref)):
        ref[...] = whole[own * i : own * (i + 1)]
    for i in range(2):
        rows = whole[3 * own + 8 * i : 3 * own + 8 * (i + 1)]
        sums_ref[i : i + 1] = jnp.sum(rows, 0, keepdims=True)


def out_rows_kernel(plan, halves_ref, out_ref, *, at):
    clips, half = out_ref.shape[0], halves_ref.shape[1]
    for place in range(clips):
        zone = lax.rem(plan[at.tok] + place // 2, clips // 2)
        first = 4 * zone + 2 * lax.rem(plan[SIDE_Y] + place % 2, 2)
        for x in range(2):
            out_ref[plan[at.clip + place], half * x : half * (x + 1)] = halves_ref[first + x]


def in_clip_order_kernel(plan, r0, r1, r2, r3, out_ref, *sums_ref, at):
    half = out_ref.shape[1] // 2
    side = plan[at.side_x]
    for place in range(out_ref.shape[0]):
        same, crossed = (r0, r1) if place % 2 == 0 else (r2, r3)
        clip, zone = plan[at.clip + place], place // 2
        out_ref[clip, pl.ds(pl.multiple_of(side * half, half), half)] = same[zone, :half]
        out_ref[clip, pl.ds(pl.multiple_of((1 - side) * half, half), half)] = crossed[zone, :half]
    for ref in sums_ref:
        ref[...] = sum_of(
            [r[zone, half:].astype(F32)[:8] for zone in range(r0.shape[0]) for r in (r0, r2)]
        )


def in_clip_order(at, plan, lat, results, deps=()):
    height, width = results[0].shape[1:]
    outs = [((at.clips, lat, width), BF)] + [((8, width), F32)] * (height > lat // 2)
    return kernel_call(
        functools.partial(in_clip_order_kernel, at=at), outs, *results,
        name="in_clip_order", scalars=(plan,), deps=deps,
    )


def mlp_grads_kernel(inner, d_pre, hidden, low, *refs, cuts):
    lat, width = inner.shape
    out_ref = refs[-1]
    near = [refs[k][lat * i : lat * (i + 1)] for k, i in cuts]
    out_ref[:width] = (dot_tn(inner[...], d_pre[0]) + dot_tn(near[0], near[1])).astype(BF)
    out_ref[width:] = (dot_tn(hidden[0], low[...]) + dot_tn(near[2], near[3])).astype(BF)


def self_grads_kernel(inner, branch, d_rows, low_t, early, moved, outs):
    lat = inner.shape[0]
    own = low_t.shape[1]
    heads_in = [moved[lat:, own * i : own * (i + 1)] for i in range(4)]
    for i in range(3):
        part = dot_tn(d_rows[0, i], inner[...]) + dot_tn(heads_in[i], early[2 * lat :])
        outs[own * i : own * (i + 1)] = part.astype(BF)
    part = dot(low_t[0], branch[...]) + dot_tn(heads_in[3], moved[:lat])
    outs[3 * own :] = part.astype(BF)


def output_grad_kernel(low, branch, branch_y, out_ref):
    part = dot(low[0], branch[...]) + dot(low[1], branch_y[...])
    out_ref[...] = part.astype(BF)


def head_move(x, k):
    n = lax.axis_size("head")
    return lax.ppermute(x, "head", [(i, i ^ k) for i in range(n)])


def mod_move(x):
    return lax.ppermute(x, "mod", [(0, 1), (1, 0)])


def tok_move(x, shift):
    n = lax.axis_size("tok")
    return lax.ppermute(x, "tok", [(i, (i + shift) % n) for i in range(n)])


def after(x, *earlier):
    return lax.optimization_barrier((x, *earlier))[0]


def on_device(
    latents,
    video_tokens,
    text_tokens,
    frame_counts,
    text_lengths,
    drop_mask,
    cotangent,
    norm_latent_gain,
    norm_latent_bias,
    norm_input_gain,
    norm_input_bias,
    cross_query,
    cross_key,
    cross_value,
    cross_output,
    norm_cross_gain,
    norm_cross_bias,
    cross_up,
    cross_down,
    norm_self_gain,
    norm_self_bias,
    self_query,
    self_key,
    self_value,
    self_output,
    norm_ffn_gain,
    norm_ffn_bias,
    self_up,
    self_down,
):
    clips, lat, width = latents.shape
    span = video_tokens.shape[1]
    own = cross_key.shape[1]
    heads = own // HEAD
    shards = lax.axis_size("tok")
    zones = clips // 2
    tok, mod, head = lax.axis_index("tok"), lax.axis_index("mod"), lax.axis_index("head")
    side_x, side_y = lax.rem(head, 2), head // 2
    rows = 784 if span % 784 == 0 else span
    norms = jnp.stack(
        [norm_latent_gain, norm_latent_bias, norm_input_gain, norm_input_bias,
         norm_cross_gain, norm_cross_bias, norm_self_gain, norm_self_bias,
         norm_ffn_gain, norm_ffn_bias]
    )
    cross_kvq = [cross_key.T, cross_value.T, cross_query.T]
    self_weights = [self_query.T, self_key.T, self_value.T, self_output]

    at = Plan(clips, span // rows)
    last = (tok == shards - 1).astype(jnp.int32)
    places = jnp.stack([tok, side_x, side_y, mod, last]).astype(jnp.int32)
    plan = make_plan(at, places, frame_counts, text_lengths, drop_mask, rows, span)

    (pack,) = pack_halves(at, plan, [[cross_up, cross_down] + self_weights + [cross_output]])
    near = head_move(pack, 2)
    tables = jnp.concatenate(cross_kvq, 0)
    if shards == zones:
        part = tables.shape[0] // shards
        tables = lax.dynamic_slice_in_dim(tables, tok * part, part, 0)
        tables = lax.all_gather(tables, ("tok", "head")).reshape(shards, 4, part, width)
    else:
        tables = lax.all_gather(tables, "head")[None]

    d_video, *partial = tokens_forward(
        at, plan, video_tokens, text_tokens, latents, (norms, *cross_kvq), rows
    )
    received = [tok_move(partial[k % zones], k) for k in range(1, shards)]
    (pack3,) = pack_halves(at, tie(plan, partial[0]), [[self_up, self_down]])
    my_latents, my_cotangent, other_cotangent, keep = own_rows(
        at, tie(plan, partial[0]), latents, cotangent
    )
    lw = (lat, width)
    square = ((width, width), BF)
    mine, other, low, branch, branch_other = kernel_call(
        combine_kernel, [(partial[0].shape[1:], BF)] * 2 + [((2, own, lat), BF)] + [(lw, BF)] * 2,
        cross_output, partial[0], *received, name="combine", scalars=(plan,),
    )
    near = tie(near, mine)
    far = mod_move(near)
    branch_parts = [branch, head_move(branch, 1), head_move(branch_other, 2), head_move(branch_other, 3)]

    near3 = head_move(tie(pack3, *branch_parts[1:]), 2)

    first, inner1, pre1, hidden1, part = kernel_call(
        cross_forward_kernel,
        [(lw, F32), (lw, BF), ((2,) + lw, F32), ((2,) + lw, BF), (lw, BF)],
        *branch_parts, my_latents, keep, norms, cross_up, cross_down, near, far,
        name="cross_forward", scalars=(plan,), scratch=[square] * 2,
    )
    mine_y = head_move(tie(other, first), 2)
    second, self_in, self_rows, self_query_t, self_attended, self_lse, part, moving = kernel_call(
        self_forward_kernel,
        [(lw, F32), (lw, BF), ((2, 3, lat, own), BF), ((2, own, lat), BF), ((2, own, lat), F32),
         ((2, 1, heads * lat), F32), (lw, BF), ((3 * lat, width), BF)],
        first, part, head_move(part, 1), norms, *self_weights, near, far, inner1, hidden1,
        name="self_forward", scalars=(plan,), scratch=[((4, own, width), BF)],
    )
    early = head_move(moving, 2)
    near3 = tie(near3, second)
    far3 = mod_move(near3)
    third, inner2, hidden2, d_pre2, part, moving = kernel_call(
        last_back_kernel,
        [(lw, F32), (lw, BF), ((2,) + lw, BF), ((2,) + lw, BF), (lw, BF), ((3 * lat, width), BF)],
        second, part, head_move(part, 1), my_cotangent, norms, self_up, self_down, near3, far3,
        name="last_back", scalars=(plan,), scratch=[square] * 2,
    )
    received = head_move(part, 1)
    halves = head_move(moving, 2)
    (out_part,) = kernel_call(
        down_kernel, [(lw, BF)], hidden2, self_down, near3, far3,
        name="down", beside=3.4, scalars=(plan,), scratch=[square], deps=(part,),
    )
    grad_third, ffn_sums, self_branch, self_d_rows, self_low, part, moving = kernel_call(
        self_back_kernel,
        [(lw, F32), ((2, width), F32), (lw, BF), ((2, 3, lat, own), BF), ((2, own, lat), BF), (lw, BF),
         ((2 * lat, width), BF)],
        my_cotangent, third, part, received, norms,
        self_rows, self_query_t, self_attended, self_lse, *self_weights, near, far,
        name="self_back", scalars=(plan,), deps=(out_part, early), scratch=[((4, own, width), BF)],
    )
    out_moved = head_move(tie(out_part, grad_third), 1)
    moved_self = head_move(moving, 2)
    (out_half,) = kernel_call(
        half_rows_kernel, [((lat // 2, width), BF)], third, out_part, out_moved,
        name="half_rows", beside=1.5, scalars=(plan,), scratch=[(lw, F32)],
    )
    out_halves = lax.all_gather(out_half, ("tok", "head"))
    grad_second, self_sums, low1, d_pre1, part, moving = kernel_call(
        cross_back_kernel,
        [(lw, F32), ((2, width), F32), (lw, BF), ((2,) + lw, BF), (lw, BF), ((2 * lat, width), BF)],
        grad_third, second, part, head_move(part, 1), norms, pre1,
        cross_up, cross_down, near, far,
        name="cross_back", scalars=(plan,), deps=(out_half, halves), scratch=[square] * 2,
    )

    pair, pair_t, query_t = kernel_call(
        tables_kernel,
        [((width, 2 * width), BF), ((2 * width, width), BF), ((width, width), BF)],
        tables, name="tables", beside=4.7, scalars=(plan,),
    )
    moved = head_move(moving, 2)
    cross_branch, packed, grad_first, cross_sums = kernel_call(
        attended_back_kernel,
        [(lw, BF), ((2 * own + 2 * STAT, lat), BF), (lw, F32), ((2, width), F32)],
        grad_second, first, part, head_move(part, 1), norms, keep,
        mine, mine_y, cross_output, near, far,
        name="attended_back", scalars=(plan,), scratch=[((own, width), BF)],
        deps=(pair, moved_self),
    )

    (stages,) = kernel_call(
        stack_kernel, [((zones,) + packed.shape, BF)],
        packed, *[tok_move(packed, shards - k) for k in range(1, zones)], name="stack",
        deps=(moved,),
    )
    arrived = [stages] + [head_move(stages, k) for k in (1, 2, 3)]
    (mlp2,) = kernel_call(
        functools.partial(mlp_grads_kernel, cuts=((0, 0), (0, 1), (0, 2), (1, 0))),
        [((2 * width, width), BF)], inner2, d_pre2, hidden2, my_cotangent, halves, other_cotangent,
        name="last_weights", beside=4.0, deps=(packed,),
    )
    branch_y = head_move(cross_branch, 2)
    (self_grads,) = kernel_call(
        self_grads_kernel, [((4 * own, width), BF)],
        self_in, self_branch, self_d_rows, self_low, early, moved_self, name="self_weights", beside=3.3,
        deps=(stages,),
    )
    (mlp1,) = kernel_call(
        functools.partial(mlp_grads_kernel, cuts=((0, 0), (1, 0), (0, 1), (1, 1))),
        [((2 * width, width), BF)], inner1, d_pre1, hidden1, low1, early, moved, name="cross_weights", beside=4.4,
        deps=(stages,),
    )
    (output_grad,) = kernel_call(
        output_grad_kernel, [((own, width), BF)], low, cross_branch, branch_y,
        name="output_weights", beside=2.1,
    )
    counted = lambda grads: [jnp.where(tok < zones, a, 0) if shards > zones else a for a in grads]
    params = (norms, pair, pair_t, query_t)
    tokens = (video_tokens, text_tokens, latents)
    d_text = jnp.zeros_like(text_tokens)
    d_video = tie(d_video, mlp2, self_grads, mlp1, output_grad, *arrived[1:], beside=25.0)
    d_video, d_text, token_weights, keep_half, send_half, *d_query = tokens_back(
        at, plan, 0, *tokens, params, arrived, [d_video, d_text], None, rows, deps=(out_halves,)
    )
    sums = lax.psum(counted([mlp2, self_grads, mlp1, output_grad]), ("tok", "mod"))
    mlp2, self_grads, mlp1, output_grad = (a.astype(F32) for a in sums)
    up1, down1 = mlp1[:width], mlp1[width:]
    up2, down2 = mlp2[:width], mlp2[width:]

    (latents_out,) = kernel_call(
        functools.partial(out_rows_kernel, at=at), [(latents.shape, BF)], out_halves[: 4 * zones],
        name="out_rows", scalars=(plan,),
    )

    whole_rows = token_weights.shape[0]
    step = whole_rows // zones
    received = [tok_move(d_query[k % zones], k) for k in range(1, shards)]
    my_query, other_query = kernel_call(
        query_sum_kernel, [((own, lat), BF)] * 2, d_query[0], *received, name="query_sum"
    )
    if shards == zones:
        token_own, *pieces = kernel_call(
            functools.partial(tail_pack_kernel, at=at),
            [((step, width // 2), F32)] + [((step, width // 2), BF)] * (zones - 1),
            keep_half, mod_move(send_half), name="tail_pack", scalars=(plan,),
        )
        received = [tok_move(p, k + 1) for k, p in enumerate(pieces)]
        (share,) = kernel_call(
            share_sum_kernel, [((step, width // 2), BF)], token_own, *received,
            name="share_sum", deps=(my_query, latents_out),
        )
        shares = [share] + [tok_move(share, shards - k) for k in range(1, zones)]
        (shares,) = kernel_call(
            stack_kernel, [((zones,) + share.shape, BF)], *shares, name="stack"
        )
        d_key_t, d_value_t, d_query_t, input_sums = kernel_call(
            functools.partial(token_weights_kernel, at=at),
            [((own, width), F32)] * 3 + [((2, width), F32)],
            shares, mod_move(shares), name="token_weights", scalars=(plan,),
            scratch=[((whole_rows, width), F32)],
        )
    else:
        total = lax.psum(token_weights, ("tok", "mod"))
        d_key_t, d_value_t, d_query_t = (total[own * i : own * (i + 1)] for i in range(3))
        input_sums = jnp.sum(total[3 * own : 3 * own + 16].reshape(2, 8, width), 1)
    d_queries = [my_query] + [head_move(a, k) for k, a in ((1, my_query), (2, other_query), (3, other_query))]
    (my_grad,) = kernel_call(
        latent_back_kernel, [((lat // 2 + STAT, width), BF)],
        grad_first, my_latents, norms, *d_queries, query_t, cross_sums, self_sums, ffn_sums,
        name="latent_back", scalars=(plan,), scratch=[(lw, F32)],
    )
    zones_grad = jnp.stack([my_grad] + [tok_move(my_grad, shards - k) for k in range(1, zones)])
    zones_grad = [zones_grad] + [head_move(zones_grad, k) for k in (1, 2, 3)]
    grad_latents, norm_sums = in_clip_order(at, plan, lat, zones_grad)
    norm_sums = norm_sums + mod_move(norm_sums)
    return (
        latents_out,
        grad_latents,
        d_video,
        d_text,
        norm_sums[0],
        norm_sums[1],
        input_sums[0],
        input_sums[1],
        d_query_t.T,
        d_key_t.T,
        d_value_t.T,
        output_grad,
        norm_sums[2],
        norm_sums[3],
        up1,
        down1,
        norm_sums[4],
        norm_sums[5],
        self_grads[:own].T,
        self_grads[own : 2 * own].T,
        self_grads[2 * own : 3 * own].T,
        self_grads[3 * own :],
        norm_sums[6],
        norm_sums[7],
        up2,
        down2,
    )


def solution(mesh):
    in_specs = (
        P("mod", None, None),
        P("mod", "tok", None),
        P("mod", None, None),
        P("mod"),
        P("mod"),
        P("mod"),
        P("mod", None, None),
        P(),
        P(),
        P(),
        P(),
        P(None, "head"),
        P(None, "head"),
        P(None, "head"),
        P("head", None),
        P(),
        P(),
        P(None, "head"),
        P("head", None),
        P(),
        P(),
        P(None, "head"),
        P(None, "head"),
        P(None, "head"),
        P("head", None),
        P(),
        P(),
        P(None, "head"),
        P("head", None),
    )
    out_specs = (
        P("mod", None, None),
        P("mod", None, None),
        P("mod", "tok", None),
        P("mod", None, None),
        P(),
        P(),
        P(),
        P(),
        P(None, "head"),
        P(None, "head"),
        P(None, "head"),
        P("head", None),
        P(),
        P(),
        P(None, "head"),
        P("head", None),
        P(),
        P(),
        P(None, "head"),
        P(None, "head"),
        P(None, "head"),
        P("head", None),
        P(),
        P(),
        P(None, "head"),
        P("head", None),
    )
    return jax.shard_map(
        on_device, mesh=mesh, in_specs=in_specs, out_specs=out_specs, check_vma=False
    )
```

```python
import functools

import jax
import jax.numpy as jnp
from jax import lax
from jax.experimental import pallas as pl
from jax.experimental.pallas import tpu as pltpu
from jax.sharding import PartitionSpec as P

HEAD = 64
PATCH = 392
EPSILON = 1e-05
NEGATIVE = -1e30
LOG2E = 1.4426950408889634
STAT = 16
BF = jnp.bfloat16
F32 = jnp.float32
VMEM_LIMIT = 60 * 2**20
SIDE_X, SIDE_Y, MOD = range(3)


def dot(a, b):
    return jnp.dot(a, b, preferred_element_type=F32)


def dot_tn(a, b):
    return lax.dot_general(a, b, (((0,), (0,)), ((), ())), preferred_element_type=F32)


def dot_nt(a, b):
    return lax.dot_general(a, b, (((1,), (1,)), ((), ())), preferred_element_type=F32)


def normalize(rows):
    mean = jnp.mean(rows, -1, keepdims=True)
    centered = rows - mean
    rstd = lax.rsqrt(jnp.mean(centered * centered, -1, keepdims=True) + EPSILON)
    return centered * rstd, rstd


def normed_rows(rows, gain, bias):
    return (normalize(rows)[0] * gain + bias).astype(BF)


def norm_back(grad_out, rows, gain):
    normed, rstd = normalize(rows)
    scaled = grad_out * gain
    grad_in = rstd * (
        scaled
        - jnp.mean(scaled, -1, keepdims=True)
        - normed * jnp.mean(scaled * normed, -1, keepdims=True)
    )
    return grad_in, jnp.sum(grad_out * normed, 0, keepdims=True), jnp.sum(grad_out, 0, keepdims=True)


def row_sums(a):
    n, width = a.shape
    if n % 8:
        a = jnp.concatenate([a, jnp.zeros((8 - n % 8, width), a.dtype)], 0)
    return jnp.sum(a.reshape(-1, 8, width), 0)


def erf(x):
    x = jnp.clip(x, -4.0, 4.0)
    s = x * x
    top = -2.72614225801306e-10
    for c in (
        2.77068142495902e-08,
        -2.10102402082508e-06,
        -5.69250639462346e-05,
        -7.34990630326855e-04,
        -2.95459980854025e-03,
        -1.60960333262415e-02,
    ):
        top = top * s + c
    low = -1.45660718464996e-05
    for c in (
        -2.13374055278905e-04,
        -1.68282697438203e-03,
        -7.37332916720468e-03,
        -1.42647390514189e-02,
    ):
        low = low * s + c
    return x * top / low


def gelu_share(x):
    return 0.5 * (1.0 + erf(x * 0.7071067811865476))


def gelu_slope(x):
    return gelu_share(x) + x * (0.3989422804014327 * jnp.exp(-0.5 * x * x))


def parts_of(value, count):
    parts = []
    for _ in range(count):
        part = value.astype(BF).astype(F32)
        parts.append(part)
        value = value - part
    return parts


def stat_tile(rows, height):
    place = lax.broadcasted_iota(jnp.int32, (height, rows[0].shape[1]), 0)
    tile = jnp.zeros(place.shape, F32)
    for k, row in enumerate(rows):
        tile = jnp.where(place == k, row, tile)
    return tile.astype(BF)


def diagonal(rows, row_block, column_block, count):
    shape = (row_block * count, column_block * count)
    r = lax.broadcasted_iota(jnp.int32, shape, 0) // row_block
    c = lax.broadcasted_iota(jnp.int32, shape, 1) // column_block
    return jnp.where(r == c, rows, 0.0).astype(BF)


def blocks_down(rows, count):
    return diagonal(jnp.concatenate([rows] * count, 0), rows.shape[0], HEAD, count)


def blocks_across(rows_t, count):
    return diagonal(jnp.concatenate([rows_t] * count, 1), HEAD, rows_t.shape[1], count)


def diagonal_parts(table, lat, count):
    return [
        table[HEAD * h : HEAD * (h + 1), lat * h : lat * (h + 1)] for h in range(count)
    ]


def cost_of(us):
    return pl.CostEstimate(flops=int(us * 1e9), bytes_accessed=0, transcendentals=0)


NO_COST = cost_of(0)


def kernel_call(body, outs, *args, name, scalars=(), scratch=(), deps=(), beside=0.0):
    spec = pl.BlockSpec(memory_space=pltpu.VMEM)
    smem = pl.BlockSpec(memory_space=pltpu.SMEM)
    first, count = len(scalars) + len(args), len(deps)
    return pl.pallas_call(
        lambda *refs: body(*refs[:first], *refs[first + count :]),
        out_shape=[jax.ShapeDtypeStruct(s, t) for s, t in outs],
        in_specs=[smem] * len(scalars)
        + [spec] * len(args)
        + [pl.BlockSpec(memory_space=pl.ANY)] * len(deps),
        out_specs=[spec] * len(outs),
        scratch_shapes=[pltpu.VMEM(s, t) for s, t in scratch],
        compiler_params=pltpu.CompilerParams(vmem_limit_bytes=VMEM_LIMIT),
        cost_estimate=cost_of(beside),
        name=name,
    )(*scalars, *args, *deps)


def tie(x, *deps, beside=0.0):
    anywhere = pl.BlockSpec(memory_space=pl.ANY)
    return pl.pallas_call(
        lambda *refs: None,
        out_shape=jax.ShapeDtypeStruct(x.shape, x.dtype),
        in_specs=[anywhere] * (1 + len(deps)),
        out_specs=anywhere,
        input_output_aliases={0: 0},
        cost_estimate=cost_of(beside),
        name="tie",
    )(x, *deps)


def stack_kernel(*refs):
    for k, ref in enumerate(refs[:-1]):
        refs[-1][k] = ref[...]


def concat_kernel(*refs):
    row = 0
    for ref in refs[:-1]:
        refs[-1][row : row + ref.shape[0]] = ref[...]
        row += ref.shape[0]


def join_halves(target, part, other, mod, at, n):
    target[pl.ds(pl.multiple_of(mod * n, 16), n)] = part[at : at + n]
    target[pl.ds(pl.multiple_of((1 - mod) * n, 16), n)] = other[at : at + n]


def pack_kernel(plan, *refs, counts):
    outs = refs[-len(counts) :]
    at = 0
    for out, count in zip(outs, counts):
        row = 0
        for ref in refs[at : at + count]:
            out[row : row + ref.shape[0]] = ref[...]
            row += ref.shape[0]
        at += count


def pack_halves(at, plan, groups):
    arrays = [a for g in groups for a in g]
    spec = lambda a: pl.BlockSpec((a.shape[0] // 2, a.shape[1]), lambda i, p: (p[at.mod], 0))
    shapes = [(sum(a.shape[0] // 2 for a in g), g[0].shape[1]) for g in groups]
    return pl.pallas_call(
        functools.partial(pack_kernel, counts=[len(g) for g in groups]),
        grid_spec=pltpu.PrefetchScalarGridSpec(
            num_scalar_prefetch=1,
            grid=(1,),
            in_specs=[spec(a) for a in arrays],
            out_specs=[pl.BlockSpec(s, lambda i, m: (0, 0)) for s in shapes],
        ),
        out_shape=[jax.ShapeDtypeStruct(s, BF) for s in shapes],
        compiler_params=pltpu.CompilerParams(vmem_limit_bytes=VMEM_LIMIT),
        cost_estimate=NO_COST,
        name="pack_halves",
    )(plan, *arrays)


def tables_kernel(plan, gathered_ref, pair_ref, pair_t_ref, query_t_ref):
    parts, _, rows, width = gathered_ref.shape
    own = parts * rows // 3
    for k in range(4):
        x, y = lax.rem(plan[SIDE_X] + k % 2, 2), lax.rem(plan[SIDE_Y] + k // 2, 2)
        shard = 2 * y + x
        for i, (target, start) in enumerate(((pair_t_ref, 0), (pair_t_ref, width), (query_t_ref, 0))):
            for p in range(parts):
                low, high = max(own * i, rows * p), min(own * (i + 1), rows * (p + 1))
                if low < high:
                    to = start + own * k + low - own * i
                    target[to : to + high - low] = gathered_ref[
                        p, shard, low - rows * p : high - rows * p
                    ]
    for c in range(0, 2 * width, 256):
        pair_ref[:, c : c + 256] = pair_t_ref[c : c + 256].astype(F32).T.astype(BF)


class Plan:
    def __init__(self, clips, blocks):
        steps = clips * blocks
        self.clips, self.blocks, self.size = clips, blocks, 0
        for name, length in (
            ("side_x", 1), ("side_y", 1), ("mod", 1), ("share", 1), ("some", 1), ("keep", 1), ("tok", 1),
            ("clip_plain", clips), ("count_plain", clips), ("text_plain", clips),
            ("read_clip", steps), ("read_block", steps), ("zero_clip", steps), ("zero_block", steps),
            ("clip", clips), ("count", clips), ("text", clips),
            ("back_clip", steps), ("back_block", steps),
        ):
            setattr(self, name, self.size)
            self.size += length

    def calls(self):
        return ((0, self.clips),)


def plan_kernel(place_ref, frames_ref, lengths_ref, drop_ref, plan, order, *, at, rows, span):
    clips, blocks = at.clips, at.blocks
    zones = clips // 2
    tok, side_x, side_y, mod, last = (place_ref[i] for i in range(5))
    zone = lax.rem(tok, zones)
    plan[at.side_x], plan[at.side_y], plan[at.mod], plan[at.share] = side_x, side_y, mod, last
    plan[at.tok] = tok
    drops = [drop_ref[c] for c in range(clips)]
    for c in range(clips):
        rank = sum(
            (drops[o] < drops[c]).astype(jnp.int32)
            if o > c
            else (drops[o] <= drops[c]).astype(jnp.int32)
            for o in range(clips)
            if o != c
        )
        order[rank] = c

    def tables(side, clip_at, count_at, text_at, share):
        flags = []
        for p in range(clips):
            clip = order[2 * lax.rem(zone + p // 2, zones) + lax.rem(p + side, 2)]
            live = 1 - drop_ref[clip]
            count = jnp.clip(frames_ref[clip] * PATCH - tok * span, 0, span) * live
            plan[clip_at + p] = clip
            plan[count_at + p] = count
            plan[text_at + p] = lengths_ref[clip] * live * share
            flags += [((count > b * rows).astype(jnp.int32), clip, b) for b in range(blocks)]
        return flags

    def hold(flags, wanted, clip_at, block_at):
        clip, block = flags[0][1], jnp.int32(0)
        for flag, c, b in flags[::-1]:
            clip = jnp.where(flag == wanted, c, clip)
            block = jnp.where(flag == wanted, b, block)
        for i, (flag, c, b) in enumerate(flags):
            clip = jnp.where(flag == wanted, c, clip)
            block = jnp.where(flag == wanted, b, block)
            plan[clip_at + i] = clip
            plan[block_at + i] = block

    flags = tables(0, at.clip_plain, at.count_plain, at.text_plain, last)
    hold(flags, 1, at.read_clip, at.read_block)
    hold(flags, 0, at.zero_clip, at.zero_block)
    flags = tables(side_y, at.clip, at.count, at.text, 1)
    for i, (first, count) in enumerate(at.calls()):
        part = flags[first * blocks : (first + count) * blocks]
        hold(part, 1, at.back_clip + first * blocks, at.back_block + first * blocks)
        plan[at.some + i] = sum(f for f, _, _ in part)
    plan[at.keep] = 1 - drop_ref[plan[at.clip]]


def make_plan(at, places, frames, lengths, drops, rows, span):
    smem = pl.BlockSpec(memory_space=pltpu.SMEM)
    return pl.pallas_call(
        functools.partial(plan_kernel, at=at, rows=rows, span=span),
        out_shape=jax.ShapeDtypeStruct((at.size,), jnp.int32),
        in_specs=[smem] * 4,
        out_specs=smem,
        scratch_shapes=[pltpu.SMEM((at.clips,), jnp.int32)],
        cost_estimate=NO_COST,
        name="plan",
    )(places, frames, lengths, drops)


def own_rows_kernel(plan, latents, mine, other, latents_ref, mine_ref, other_ref, keep_ref, *, at):
    latents_ref[...] = latents[0]
    mine_ref[...] = mine[0]
    other_ref[...] = other[0]
    keep_ref[...] = jnp.full(keep_ref.shape, plan[at.keep].astype(F32))


def own_rows(at, plan, latents, cotangent):
    lat, width = latents.shape[1:]
    spec = lambda k: pl.BlockSpec((1, lat, width), lambda i, p: (p[at.clip + k], 0, 0))
    whole = lambda *shape: pl.BlockSpec(shape, lambda i, p: (0,) * len(shape))
    return pl.pallas_call(
        functools.partial(own_rows_kernel, at=at),
        grid_spec=pltpu.PrefetchScalarGridSpec(
            num_scalar_prefetch=1,
            grid=(1,),
            in_specs=[spec(0), spec(0), spec(1)],
            out_specs=[whole(lat, width)] * 3 + [whole(1, width)],
        ),
        out_shape=[
            *[jax.ShapeDtypeStruct((lat, width), BF)] * 3,
            jax.ShapeDtypeStruct((1, width), F32),
        ],
        cost_estimate=NO_COST,
        name="own_rows",
    )(plan, latents, cotangent, cotangent)


def tokens_forward_kernel(
    plan, video_ref, text_ref, latents_ref, norms_ref, key_t_ref, value_t_ref, query_t_ref,
    zero_ref, *refs, at,
):
    outs, (key_ref, value_ref, blocks, peak, total, summed) = refs[:-6], refs[-6:]
    place, j = pl.program_id(0), pl.program_id(1)
    rows = video_ref.shape[1]
    lat = latents_ref.shape[1]
    width = key_ref.shape[1]
    heads = width // HEAD
    clip_count = plan[at.count_plain + place]
    text_count = plan[at.text_plain + place]
    count = clip_count - j * rows
    lat_gain, lat_bias, gain, bias = (norms_ref[i : i + 1] for i in range(4))

    @pl.when((place == 0) & (j == 0))
    def _():
        key_ref[...] = key_t_ref[...].astype(F32).T.astype(BF)
        value_ref[...] = value_t_ref[...].astype(F32).T.astype(BF)

    @pl.when(count <= 0)
    def _():
        zero_ref[...] = jnp.zeros_like(zero_ref)

    @pl.when((j == 0) & ((clip_count > 0) | (text_count > 0)))
    def _():
        queries_in = normed_rows(latents_ref[0].astype(F32), lat_gain, lat_bias)
        rows_t = dot_nt(query_t_ref[...], queries_in).astype(BF).astype(F32) * HEAD**-0.5
        blocks[...] = blocks_across(rows_t, heads)

    @pl.when(j == 0)
    def _():
        peak[...] = jnp.full_like(peak, NEGATIVE).astype(BF).astype(F32)
        total[...] = jnp.zeros_like(total)
        summed[...] = jnp.zeros_like(summed)

    def block(x, limit):
        inputs_in = normed_rows(x.astype(F32), gain, bias)
        key = dot(inputs_in, key_ref[...]).astype(BF)
        value = dot(inputs_in, value_ref[...]).astype(BF)
        mask = lax.broadcasted_iota(jnp.int32, (x.shape[0], 1), 0) < limit
        scores = jnp.where(mask, dot(key, blocks[...]) * LOG2E, NEGATIVE)
        before = peak[...]
        top = jnp.maximum(before, jnp.max(scores, 0, keepdims=True)).astype(BF).astype(F32)
        weights = jnp.exp2(scores - top)
        factor = jnp.exp2(before - top)
        peak[...] = top
        total[...] = total[...] * factor + jnp.sum(weights, 0, keepdims=True)
        table = dot_tn(value, weights.astype(BF))
        for h, part in enumerate(diagonal_parts(table, lat, heads)):
            r = slice(HEAD * h, HEAD * (h + 1))
            summed[r] = summed[r] * factor[:, lat * h : lat * (h + 1)] + part

    @pl.when(count > 0)
    def _():
        block(video_ref[0], count)

    @pl.when((j == 0) & (text_count > 0))
    def _():
        block(text_ref[0], text_count)

    for zone, out_ref in enumerate(outs):

        @pl.when((j == pl.num_programs(1) - 1) & (place // 2 == zone))
        def _(out_ref=out_ref):
            out_ref[0, :width] = summed[...].astype(BF)
            of = [slice(lat * h, lat * (h + 1)) for h in range(heads)]
            totals = [parts_of(total[:, c], 2) for c in of]
            stats = [peak[:, c] for c in of] + [t[0] for t in totals] + [t[1] for t in totals]
            out_ref[0, width:] = stat_tile(stats, STAT)


def tokens_forward(at, plan, video, text, latents, params, rows):
    clips, span, width = video.shape
    lat = latents.shape[1]
    own = params[-1].shape[0]
    blocks = span // rows
    full = lambda a: pl.BlockSpec(a.shape, lambda s, j, *_: (0,) * a.ndim)
    clip_spec = lambda a: pl.BlockSpec(
        (1,) + a.shape[1:], lambda s, j, p: (p[at.clip_plain + s], 0, 0)
    )
    block_spec = lambda clip, block: pl.BlockSpec(
        (1, rows, width), lambda s, j, p: (p[clip + s * blocks + j], p[block + s * blocks + j], 0)
    )
    return pl.pallas_call(
        functools.partial(tokens_forward_kernel, at=at),
        grid_spec=pltpu.PrefetchScalarGridSpec(
            num_scalar_prefetch=1,
            grid=(clips, blocks),
            in_specs=[
                block_spec(at.read_clip, at.read_block),
                clip_spec(text),
                clip_spec(latents),
            ]
            + [full(a) for a in params],
            out_specs=[block_spec(at.zero_clip, at.zero_block)]
            + [
                pl.BlockSpec(
                    (1, own + STAT, lat), lambda s, j, p, z=z: (jnp.clip(s - 2 * z, 0, 1), 0, 0)
                )
                for z in range(clips // 2)
            ],
            scratch_shapes=[
                pltpu.VMEM((width, own), BF),
                pltpu.VMEM((width, own), BF),
                pltpu.VMEM((own, own // HEAD * lat), BF),
                pltpu.VMEM((1, own // HEAD * lat), F32),
                pltpu.VMEM((1, own // HEAD * lat), F32),
                pltpu.VMEM((own, lat), F32),
            ],
        ),
        out_shape=[jax.ShapeDtypeStruct(video.shape, BF)]
        + [jax.ShapeDtypeStruct((2, own + STAT, lat), BF)] * (clips // 2),
        compiler_params=pltpu.CompilerParams(
            vmem_limit_bytes=VMEM_LIMIT, dimension_semantics=("arbitrary", "arbitrary")
        ),
        cost_estimate=cost_of(30.0),
        name="tokens_forward",
    )(plan, video, text, latents, *params)


GROUP = 4


def tokens_back_kernel(
    plan, *refs, at, call, carried, extra,
):
    video_ref, text_ref, latents_ref, norms_ref, pair_ref, pair_t_ref, query_t_ref = refs[:7]
    d0, d1, d2, d3 = refs[7:11]
    refs = refs[13:]
    if carried:
        before_ref, refs = refs[0], refs[1:]
    refs = refs[extra:]
    d_video_ref, d_text_ref, weights_ref, keep_ref, send_ref = refs[:5]
    d_query_refs = refs[5:-8]
    q_down, q_across, d_down, d_across, lse, delta, d_query, queries = refs[-8:]
    step, j = pl.program_id(0), pl.program_id(1)
    place = step + at.calls()[call][0]
    rows, width = video_ref.shape[1:]
    lat = latents_ref.shape[1]
    own = query_t_ref.shape[0] // 4
    own_heads = own // HEAD
    groups = width // (GROUP * HEAD)
    count = plan[at.count + place] - j * rows
    text_count = plan[at.text + place]
    alive = text_count > 0
    lat_gain, lat_bias, gain, bias = (norms_ref[i : i + 1] for i in range(4))

    @pl.when((step == 0) & (j == 0))
    def _():
        weights_ref[...] = before_ref[...] if carried else jnp.zeros_like(weights_ref)
        for ref in (q_down, q_across, d_down, d_across):
            ref[...] = jnp.zeros_like(ref)

    @pl.when(j == 0)
    def _():
        d_query[...] = jnp.zeros_like(d_query)

    @pl.when((j == 0) & alive)
    def _():
        mine = lax.rem(place, 2) == 0
        first = [jnp.where(mine, a[0, :own].astype(F32), b[0, own : 2 * own].astype(F32)) for a, b in ((d0, d2), (d1, d3))]
        second = [jnp.where(mine, a[0, own : 2 * own].astype(F32), b[0, :own].astype(F32)) for a, b in ((d0, d2), (d1, d3))]
        queries_in = normed_rows(latents_ref[0].astype(F32), lat_gain, lat_bias)
        queries[...] = queries_in
        query = dot_nt(queries_in, query_t_ref[...]).astype(BF).astype(F32) * HEAD**-0.5
        d_rows_t = jnp.concatenate(first + second, 0)
        column = lax.broadcasted_iota(jnp.int32, (lat, 2 * HEAD), 1) // HEAD
        for natural, rows_t, down, across in (
            (query, query.T, q_down, q_across),
            (d_rows_t.T, d_rows_t, d_down, d_across),
        ):
            for head in range(groups * GROUP):
                g, h = divmod(head, GROUP)
                across[g, HEAD * h : HEAD * (h + 1), lat * h : lat * (h + 1)] = rows_t[
                    HEAD * head : HEAD * (head + 1)
                ].astype(BF)
                pair = natural[:, 2 * HEAD * (head // 2) : 2 * HEAD * (head // 2 + 1)]
                at = 2 * HEAD * (h // 2)
                down[g, lat * h : lat * (h + 1), at : at + 2 * HEAD] = jnp.where(
                    column == h % 2, pair, 0.0
                ).astype(BF)
        tiles = [d[0, 2 * own : 2 * own + 2 * STAT].astype(F32) for d in (d0, d1, d2, d3)]
        n = 2 * own_heads
        for kind, first_row, count_of in ((delta, 0, 2), (lse, 2 * n, 3)):
            for shard in range(4):
                a, b = tiles[shard % 2], tiles[2 + shard % 2]
                for h in range(own_heads):
                    at_a = first_row + h + own_heads * (shard // 2)
                    at_b = first_row + h + own_heads * (1 - shard // 2)
                    row = sum(
                        jnp.where(mine, a[at_a + n * i : at_a + n * i + 1], b[at_b + n * i : at_b + n * i + 1])
                        for i in range(count_of)
                    )
                    head = shard * own_heads + h
                    kind[:, lat * head : lat * (head + 1)] = row

    share = plan[at.share].astype(F32)

    def block(x, video_rows):
        n = x.shape[0]
        spans = [(0, video_rows, lambda a: a), (video_rows, n, lambda a: a * share)]
        spans = [span for span in spans if span[0] < span[1]]
        normed, rstd = normalize(x.astype(F32))
        inputs_in = (normed * gain + bias).astype(BF)
        key = dot(inputs_in, pair_ref[:, :width]).astype(BF)
        value = dot(inputs_in, pair_ref[:, width:]).astype(BF)
        index = lax.broadcasted_iota(jnp.int32, (n, 1), 0)
        mask = index < count if video_rows else index < text_count
        if 0 < video_rows < n:
            mask = jnp.where(index < video_rows, index, n * n) < count
            mask = mask | ((index >= video_rows) & (index < video_rows + text_count))
        d_keys, d_values = [], []
        for g in range(groups):
            cut = slice(GROUP * HEAD * g, GROUP * HEAD * (g + 1))
            lanes = slice(GROUP * lat * g, GROUP * lat * (g + 1))
            scores = dot(key[:, cut], q_across[g])
            d_probs = dot(value[:, cut], d_across[g])
            probs = jnp.where(mask, jnp.exp2(scores * LOG2E - lse[:, lanes]), 0.0)
            d_scores = (probs * (d_probs - delta[:, lanes])).astype(BF)
            d_values.append(dot(probs.astype(BF), d_down[g]).astype(BF))
            d_keys.append(dot(d_scores, q_down[g]).astype(BF))
            if g == 0:
                for a, b, counted in spans:
                    table = dot_tn(key[a:b, cut], d_scores[a:b])
                    for h, part in enumerate(diagonal_parts(table, lat, own_heads)):
                        d_query[HEAD * h : HEAD * (h + 1)] += counted(part)
        d_key, d_value = jnp.concatenate(d_keys, 1), jnp.concatenate(d_values, 1)
        d_in = dot(d_key, pair_t_ref[:width]) + dot(d_value, pair_t_ref[width:])
        for a, b, counted in spans:
            rows_in, part = inputs_in[a:b], d_in[a:b]
            weights_ref[:own] += counted(dot_tn(d_keys[0][a:b], rows_in)[:own])
            weights_ref[own : 2 * own] += counted(dot_tn(d_values[0][a:b], rows_in)[:own])
            weights_ref[3 * own : 3 * own + 8] += counted(row_sums(part * normed[a:b]))
            weights_ref[3 * own + 8 : 3 * own + 16] += counted(row_sums(part))
        scaled = d_in * gain
        d_x = rstd * (
            scaled
            - jnp.mean(scaled, -1, keepdims=True)
            - normed * jnp.mean(scaled * normed, -1, keepdims=True)
        )
        if video_rows:
            d_video_ref[0] = d_x[:video_rows].astype(BF)
        if video_rows < n:
            d_text_ref[0] = d_x[video_rows:].astype(BF)

    joined = rows % 16 == 0

    @pl.when((count > 0) & (j > 0 if joined else True))
    def _():
        block(video_ref[0], rows)

    if joined:

        @pl.when((j == 0) & alive & (count > 0))
        def _():
            block(jnp.concatenate([video_ref[0], text_ref[0]], 0), rows)

    @pl.when((plan[at.some + call] == 0) & (step == 0) & (j == 0))
    def _():
        d_video_ref[...] = jnp.zeros_like(d_video_ref)

    @pl.when((j == 0) & alive & ((count <= 0) if joined else True))
    def _():
        block(text_ref[0], 0)

    @pl.when((j == 0) & jnp.logical_not(alive))
    def _():
        d_text_ref[...] = jnp.zeros_like(d_text_ref)

    @pl.when(j == pl.num_programs(1) - 1)
    def _():
        d_rows = (d_query[...] * HEAD**-0.5).astype(BF)
        for zone, d_query_ref in enumerate(d_query_refs):

            @pl.when(place // 2 == zone)
            def _(d_query_ref=d_query_ref):
                d_query_ref[0] = d_rows

        @pl.when(alive)
        def _():
            weights_ref[2 * own : 3 * own] += dot(d_rows, queries[...])

        @pl.when(step == pl.num_programs(0) - 1)
        def _():
            half = width // 2
            side = plan[at.mod]
            keep_ref[...] = weights_ref[:, pl.ds(pl.multiple_of(side * half, half), half)]
            send_ref[...] = weights_ref[
                :, pl.ds(pl.multiple_of((1 - side) * half, half), half)
            ].astype(BF)


WEIGHT_ROWS = 64


def tokens_back(at, plan, call, video, text, latents, params, arrived, filled, before, rows, deps=()):
    first, steps = at.calls()[call]
    span, width = video.shape[1:]
    blocks = span // rows
    lat = latents.shape[1]
    own = params[-1].shape[0] // 4
    groups = width // (GROUP * HEAD)
    full = lambda a: pl.BlockSpec(
        a.shape, lambda s, j, *_: (0,) * a.ndim, pipeline_mode=pl.Buffered(1)
    )
    clip_spec = lambda a: pl.BlockSpec(
        (1,) + a.shape[1:], lambda s, j, p: (p[at.clip + first + s], 0, 0)
    )
    index = lambda p, table, s, j: p[table + (first + s) * blocks + j]
    video_spec = pl.BlockSpec(
        (1, rows, width),
        lambda s, j, p: (index(p, at.back_clip, s, j), index(p, at.back_block, s, j), 0),
    )
    weight_shape = (3 * own + WEIGHT_ROWS, width)
    half_shape = (weight_shape[0], width // 2)
    operands = [video, text, latents, *params, *arrived]
    in_specs = [video_spec, clip_spec(text), clip_spec(latents)]
    in_specs += [full(a) for a in params]
    in_specs += [
        pl.BlockSpec(
            (1, 2 * own + 2 * STAT, lat), lambda s, j, *_: ((s + first) // 2 - first // 2, 0, 0)
        )
        for a in arrived
    ]
    start = 1 + len(operands)
    operands += filled
    in_specs += [pl.BlockSpec(memory_space=pl.ANY)] * 2
    if before is not None:
        operands += [before]
        in_specs += [full(before)]
    operands += deps
    in_specs += [pl.BlockSpec(memory_space=pl.ANY)] * len(deps)
    return pl.pallas_call(
        functools.partial(
            tokens_back_kernel, at=at, call=call, carried=before is not None, extra=len(deps)
        ),
        grid_spec=pltpu.PrefetchScalarGridSpec(
            num_scalar_prefetch=1,
            grid=(steps, blocks),
            in_specs=in_specs,
            out_specs=[
                video_spec,
                clip_spec(text),
                pl.BlockSpec(weight_shape, lambda s, j, *_: (0, 0)),
            ]
            + [pl.BlockSpec(half_shape, lambda s, j, *_: (0, 0))] * 2
            + [
                pl.BlockSpec((1, own, lat), lambda s, j, p, z=z: (jnp.clip(s - 2 * z, 0, 1), 0, 0))
                for z in range(at.clips // 2)
            ],
            scratch_shapes=[
                pltpu.VMEM((groups, GROUP * lat, GROUP * HEAD), BF),
                pltpu.VMEM((groups, GROUP * HEAD, GROUP * lat), BF),
                pltpu.VMEM((groups, GROUP * lat, GROUP * HEAD), BF),
                pltpu.VMEM((groups, GROUP * HEAD, GROUP * lat), BF),
                pltpu.VMEM((1, groups * GROUP * lat), F32),
                pltpu.VMEM((1, groups * GROUP * lat), F32),
                pltpu.VMEM((own, lat), F32),
                pltpu.VMEM((lat, width), BF),
            ],
        ),
        out_shape=[
            jax.ShapeDtypeStruct(video.shape, BF),
            jax.ShapeDtypeStruct(text.shape, BF),
            jax.ShapeDtypeStruct(weight_shape, F32),
            jax.ShapeDtypeStruct(half_shape, F32),
            jax.ShapeDtypeStruct(half_shape, BF),
        ]
        + [jax.ShapeDtypeStruct((2, own, lat), BF)] * (at.clips // 2),
        input_output_aliases={start: 0, start + 1: 1},
        compiler_params=pltpu.CompilerParams(
            vmem_limit_bytes=VMEM_LIMIT, dimension_semantics=("arbitrary", "arbitrary")
        ),
        cost_estimate=cost_of(10.0),
        name="tokens_back",
    )(plan, *operands)


def combine_kernel(plan, output_ref, *refs):
    parts, (mine_ref, other_ref, low_ref, *branch_refs) = refs[:-5], refs[-5:]
    own = parts[0].shape[1] - STAT
    lat = parts[0].shape[2]
    heads = own // HEAD
    results = []
    for y in range(2):
        tiles = [p[y, own:].astype(F32) for p in parts]
        attended, logs = [], []
        for h in range(heads):
            peaks = [t[h : h + 1] for t in tiles]
            top = peaks[0]
            for p in peaks[1:]:
                top = jnp.maximum(top, p)
            total = jnp.zeros((1, lat), F32)
            summed = jnp.zeros((HEAD, lat), F32)
            for p, t, peak in zip(parts, tiles, peaks):
                factor = jnp.exp2(peak - top)
                a = t[heads + h : heads + h + 1] + t[2 * heads + h : 2 * heads + h + 1]
                total = total + a * factor
                summed = summed + p[y, HEAD * h : HEAD * (h + 1)].astype(F32) * factor
            some = total > 0.0
            safe = jnp.where(some, total, 1.0)
            attended.append(jnp.where(some, summed / safe, 0.0))
            logs.append(parts_of(jnp.where(some, top + jnp.log2(safe), 0.0), 3))
        stats = [logs[h][i] for i in range(3) for h in range(heads)]
        results.append((jnp.concatenate(attended, 0), stat_tile(stats, STAT).astype(F32)))
    first = plan[SIDE_Y] == 0
    for k, (ref, (a, b)) in enumerate(((mine_ref, results), (other_ref, results[::-1]))):
        low = jnp.where(first, a[0], b[0]).astype(BF)
        ref[:own] = low
        ref[own:] = jnp.where(first, a[1], b[1]).astype(BF)
        low_ref[k] = low
        branch_refs[k][...] = dot_tn(low, output_ref[...]).astype(BF)


def spread(norms_ref, row):
    return norms_ref[row : row + 1], norms_ref[row + 1 : row + 2]


def sum_of(terms):
    total = terms[0]
    for term in terms[1:]:
        total = total + term
    return total


def received_sum(part0, part1):
    return part0[...].astype(F32) + part1[...].astype(F32)


def cross_forward_kernel(
    plan, b0, b1, b2, b3, latents_ref, keep_ref, norms_ref, up0, down0, near, far,
    first_ref, inner_ref, pre_ref, hidden_ref, part_ref, up1, down1,
):
    join_mlp(near, far, plan[MOD], up1, down1)
    branch = received_sum(b0, b1) + received_sum(b2, b3)
    first = latents_ref[...].astype(F32) + keep_ref[...] * branch
    first_ref[...] = first
    inner = normed_rows(first, *spread(norms_ref, 4))
    inner_ref[...] = inner
    terms = []
    for k, (up, down) in enumerate(((up0, down0), (up1, down1))):
        pre = dot(inner, up[...])
        pre_ref[k] = pre
        hidden = (pre * gelu_share(pre)).astype(BF)
        hidden_ref[k] = hidden
        terms.append(dot(hidden, down[...]))
    part_ref[...] = sum_of(terms).astype(BF)


def join_mlp(near, far, mod, up, down):
    half = up.shape[0] // 2
    join_halves(up, near, far, mod, 0, half)
    join_halves(down, near, far, mod, half, half)


def join_self(near, far, mod, targets):
    half, start = targets.shape[1] // 2, targets.shape[2]
    for i in range(4):
        join_halves(targets.at[i], near, far, mod, start + half * i, half)


def self_forward_kernel(
    plan, first_ref, part0, part1, norms_ref, wq, wk, wv, wo, near, far, inner1_ref, hidden1_ref,
    second_ref, inner_ref, rows_ref, query_t_ref, attended_ref, lse_ref, part_ref, moving_ref, joined,
):
    join_self(near, far, plan[MOD], joined)
    second = first_ref[...] + received_sum(part0, part1)
    second_ref[...] = second
    inner = normed_rows(second, *spread(norms_ref, 6))
    inner_ref[...] = inner
    lat = inner.shape[0]
    own = wq.shape[0]
    heads = own // HEAD
    terms = []
    for k, (q, w, v, o) in enumerate(((wq, wk, wv, wo), [joined.at[i] for i in range(4)])):
        query = (dot_nt(inner, q[...]).astype(BF).astype(F32) * HEAD**-0.5).astype(BF)
        key = dot_nt(inner, w[...]).astype(BF)
        value = dot_nt(inner, v[...]).astype(BF)
        for i, a in enumerate((query, key, value)):
            rows_ref[k, i] = a
        query_t = dot_nt(q[...], inner).astype(BF).astype(F32) * HEAD**-0.5
        query_t_ref[k] = query_t.astype(BF)
        scores = dot(key, blocks_across(query_t, heads)) * LOG2E
        top = jnp.max(scores, 0, keepdims=True)
        weights = jnp.exp2(scores - top)
        total = jnp.sum(weights, 0, keepdims=True)
        table = dot_tn(value, weights.astype(BF))
        attended = jnp.concatenate(
            [
                part / total[:, lat * h : lat * (h + 1)]
                for h, part in enumerate(diagonal_parts(table, lat, heads))
            ],
            0,
        )
        attended_ref[k] = attended
        lse_ref[k] = top + jnp.log2(total)
        terms.append(dot_tn(attended.astype(BF), o[...]))
    part_ref[...] = sum_of(terms).astype(BF)
    for i, a in enumerate((inner1_ref[...], hidden1_ref[1], inner)):
        moving_ref[lat * i : lat * (i + 1)] = a


def hidden_back(grad_low, pre, up, down):
    d_hidden = dot_nt(grad_low, down[...])
    d_pre = (d_hidden * gelu_slope(pre)).astype(BF)
    return d_pre, dot_nt(d_pre, up[...])


def last_back_kernel(
    plan, second_ref, part0, part1, cotangent_ref, norms_ref, up0, down0, near, far,
    third_ref, inner_ref, hidden_ref, d_pre_ref, part_ref, moving_ref, up1, down1,
):
    join_mlp(near, far, plan[MOD], up1, down1)
    third = second_ref[...] + received_sum(part0, part1)
    third_ref[...] = third
    inner = normed_rows(third, *spread(norms_ref, 8))
    inner_ref[...] = inner
    terms = []
    for k, (up, down) in enumerate(((up0, down0), (up1, down1))):
        pre = dot(inner, up[...])
        hidden_ref[k] = (pre * gelu_share(pre)).astype(BF)
        d_pre_ref[k], term = hidden_back(cotangent_ref[...], pre, up, down)
        terms.append(term)
    part_ref[...] = sum_of(terms).astype(BF)
    lat = inner.shape[0]
    for i, a in enumerate((inner, d_pre_ref[1], hidden_ref[1])):
        moving_ref[lat * i : lat * (i + 1)] = a


def down_kernel(plan, hidden_ref, down0, near, far, part_ref, down1):
    half = down1.shape[0] // 2
    join_halves(down1, near, far, plan[MOD], half, half)
    part_ref[...] = (dot(hidden_ref[0], down0[...]) + dot(hidden_ref[1], down1[...])).astype(BF)


def self_back_kernel(
    plan, cotangent_ref, third_ref, part0, part1, norms_ref,
    rows_ref, query_t_ref, attended_ref, lse_ref, wq, wk, wv, wo, near, far,
    grad_ref, sums_ref, branch_ref, d_rows_ref, low_ref, part_ref, moving_ref, joined,
):
    join_self(near, far, plan[MOD], joined)
    d_inner = received_sum(part0, part1)
    d_x, d_gain, d_bias = norm_back(d_inner, third_ref[...], spread(norms_ref, 8)[0])
    grad = cotangent_ref[...].astype(F32) + d_x
    grad_ref[...] = grad
    sums_ref[0:1] = d_gain
    sums_ref[1:2] = d_bias
    branch = grad.astype(BF)
    branch_ref[...] = branch
    lat = grad.shape[0]
    own = wq.shape[0]
    heads = own // HEAD
    terms = []
    for k, weights in enumerate(((wq, wk, wv, wo), [joined.at[i] for i in range(4)])):
        o = weights[3]
        query, key, value = rows_ref[k, 0], rows_ref[k, 1], rows_ref[k, 2]
        d_att = dot_nt(branch, o[...]).astype(BF).astype(F32)
        d_att_t = dot_nt(o[...], branch).astype(BF).astype(F32)
        attended = attended_ref[k]
        low_ref[k] = attended.astype(BF)
        product = d_att_t * attended
        delta = jnp.concatenate(
            [
                jnp.sum(product[HEAD * h : HEAD * (h + 1)], 0, keepdims=True)
                for h in range(heads)
            ],
            1,
        )
        scores = dot(key, blocks_across(query_t_ref[k].astype(F32), heads))
        d_probs = dot(value, blocks_across(d_att_t, heads))
        probs = jnp.exp2(scores * LOG2E - lse_ref[k])
        d_scores = (probs * (d_probs - delta)).astype(BF)
        d_value = dot(probs.astype(BF), blocks_down(d_att, heads)).astype(BF)
        d_key = dot(d_scores, blocks_down(query.astype(F32), heads)).astype(BF)
        table = dot_tn(d_scores, key)
        column = lax.broadcasted_iota(jnp.int32, (lat, own), 1) // HEAD
        d_query = sum_of(
            [jnp.where(column == h, table[lat * h : lat * (h + 1)], 0.0) for h in range(heads)]
        )
        d_query = (d_query * HEAD**-0.5).astype(BF)
        for i, a in enumerate((d_query, d_key, d_value)):
            d_rows_ref[k, i] = a
            terms.append(dot(a, weights[i][...]))
            if k == 1:
                moving_ref[lat:, own * i : own * (i + 1)] = a
    part_ref[...] = sum_of(terms).astype(BF)
    moving_ref[:lat] = branch
    moving_ref[lat:, 3 * own :] = attended_ref[1].T.astype(BF)


def cross_back_kernel(
    plan, grad_ref, second_ref, part0, part1, norms_ref, pre_ref, up0, down0, near, far,
    out_ref, sums_ref, low_ref, d_pre_ref, part_ref, moving_ref, up1, down1,
):
    join_mlp(near, far, plan[MOD], up1, down1)
    d_inner = received_sum(part0, part1)
    d_x, d_gain, d_bias = norm_back(d_inner, second_ref[...], spread(norms_ref, 6)[0])
    grad = grad_ref[...] + d_x
    out_ref[...] = grad
    sums_ref[0:1] = d_gain
    sums_ref[1:2] = d_bias
    grad_low = grad.astype(BF)
    low_ref[...] = grad_low
    terms = []
    for k, (up, down) in enumerate(((up0, down0), (up1, down1))):
        d_pre_ref[k], term = hidden_back(grad_low, pre_ref[k], up, down)
        terms.append(term)
    part_ref[...] = sum_of(terms).astype(BF)
    lat = grad.shape[0]
    moving_ref[:lat] = d_pre_ref[1]
    moving_ref[lat:] = grad_low


def attended_back_kernel(
    plan, grad_ref, first_ref, part0, part1, norms_ref, keep_ref, a0, a2, o0, near, far,
    branch_ref, packed_ref, first_grad_ref, sums_ref, o2,
):
    own, width = o0.shape
    join_halves(o2, near, far, plan[MOD], width + 2 * own, own // 2)
    d_inner = received_sum(part0, part1)
    d_x, d_gain, d_bias = norm_back(d_inner, first_ref[...], spread(norms_ref, 4)[0])
    grad = grad_ref[...] + d_x
    branch = (keep_ref[...] * grad).astype(BF)
    branch_ref[...] = branch
    own = o0.shape[0]
    heads = own // HEAD
    deltas, logs = [], []
    for k, (a, o) in enumerate(((a0, o0), (a2, o2))):
        d_att_t = dot_nt(o[...], branch).astype(BF)
        packed_ref[own * k : own * (k + 1)] = d_att_t
        product = d_att_t.astype(F32) * a[:own].astype(F32)
        tile = a[own:].astype(F32)
        for h in range(heads):
            deltas.append(
                parts_of(jnp.sum(product[HEAD * h : HEAD * (h + 1)], 0, keepdims=True), 2)
            )
            logs.append([tile[heads * i + h : heads * i + h + 1] for i in range(3)])
    rows = [d[i] for i in range(2) for d in deltas] + [g[i] for i in range(3) for g in logs]
    packed_ref[2 * own : 2 * own + 2 * STAT] = stat_tile(rows, 2 * STAT)
    first_grad_ref[...] = grad
    sums_ref[0:1] = d_gain
    sums_ref[1:2] = d_bias


def half_rows_kernel(plan, third_ref, out0, out1, out_ref, hold):
    half = out_ref.shape[0]
    hold[...] = third_ref[...] + received_sum(out0, out1)
    cut = pl.ds(pl.multiple_of(plan[SIDE_X] * half, half), half)
    out_ref[...] = hold[cut].astype(BF)


def latent_back_kernel(
    plan, grad_ref, latents_ref, norms_ref, d0, d1, d2, d3, query_t_ref,
    cross_sums, self_sums, ffn_sums, out_ref, hold,
):
    own, lat = d0.shape
    half = lat // 2
    d_in = sum_of(
        [dot_tn(d[...], query_t_ref[own * k : own * (k + 1)]) for k, d in enumerate((d0, d1, d2, d3))]
    )
    d_x, d_gain, d_bias = norm_back(
        d_in, latents_ref[...].astype(F32), spread(norms_ref, 0)[0]
    )
    hold[...] = grad_ref[...] + d_x
    cut = pl.ds(pl.multiple_of(plan[SIDE_X] * half, half), half)
    out_ref[:half] = hold[cut].astype(BF)
    sums = [d_gain, d_bias]
    sums += [ref[i : i + 1] for ref in (cross_sums, self_sums, ffn_sums) for i in range(2)]
    out_ref[half:] = stat_tile(sums, STAT)


def tail_pack_kernel(plan, keep_ref, arrived_ref, own_ref, *outs, at):
    zones = len(outs) + 1
    step = own_ref.shape[0]
    for k, out in enumerate((own_ref, *outs)):
        cut = pl.ds(pl.multiple_of(lax.rem(plan[at.tok] + k, zones) * step, 16), step)
        out[...] = (keep_ref[cut] + arrived_ref[cut].astype(F32)).astype(out.dtype)


def query_sum_kernel(*refs):
    parts, outs = refs[:-2], refs[-2:]
    for i, out in enumerate(outs):
        out[...] = sum_of([p[i].astype(F32) for p in parts]).astype(BF)


def share_sum_kernel(*refs):
    refs[-1][...] = sum_of([p[...].astype(F32) for p in refs[:-1]]).astype(BF)


def token_weights_kernel(plan, mine_ref, other_ref, key_ref, value_ref, query_ref, sums_ref, whole, *, at):
    zones, step, half = mine_ref.shape
    own = key_ref.shape[0]
    side = plan[at.mod]
    for k in range(zones):
        cut = pl.ds(pl.multiple_of(lax.rem(plan[at.tok] + k, zones) * step, 16), step)
        for ref, x in ((mine_ref, side), (other_ref, 1 - side)):
            whole[cut, pl.ds(pl.multiple_of(x * half, half), half)] = ref[k].astype(F32)
    for i, ref in enumerate((key_ref, value_ref, query_ref)):
        ref[...] = whole[own * i : own * (i + 1)]
    for i in range(2):
        rows = whole[3 * own + 8 * i : 3 * own + 8 * (i + 1)]
        sums_ref[i : i + 1] = jnp.sum(rows, 0, keepdims=True)


def out_rows_kernel(plan, halves_ref, out_ref, *, at):
    clips, half = out_ref.shape[0], halves_ref.shape[1]
    for place in range(clips):
        zone = lax.rem(plan[at.tok] + place // 2, clips // 2)
        first = 4 * zone + 2 * lax.rem(plan[SIDE_Y] + place % 2, 2)
        for x in range(2):
            out_ref[plan[at.clip + place], half * x : half * (x + 1)] = halves_ref[first + x]


def in_clip_order_kernel(plan, r0, r1, r2, r3, out_ref, *sums_ref, at):
    half = out_ref.shape[1] // 2
    side = plan[at.side_x]
    for place in range(out_ref.shape[0]):
        same, crossed = (r0, r1) if place % 2 == 0 else (r2, r3)
        clip, zone = plan[at.clip + place], place // 2
        out_ref[clip, pl.ds(pl.multiple_of(side * half, half), half)] = same[zone, :half]
        out_ref[clip, pl.ds(pl.multiple_of((1 - side) * half, half), half)] = crossed[zone, :half]
    for ref in sums_ref:
        ref[...] = sum_of(
            [r[zone, half:].astype(F32)[:8] for zone in range(r0.shape[0]) for r in (r0, r2)]
        )


def in_clip_order(at, plan, lat, results, deps=()):
    height, width = results[0].shape[1:]
    outs = [((at.clips, lat, width), BF)] + [((8, width), F32)] * (height > lat // 2)
    return kernel_call(
        functools.partial(in_clip_order_kernel, at=at), outs, *results,
        name="in_clip_order", scalars=(plan,), deps=deps,
    )


def mlp_grads_kernel(inner, d_pre, hidden, low, *refs, cuts):
    lat, width = inner.shape
    out_ref = refs[-1]
    near = [refs[k][lat * i : lat * (i + 1)] for k, i in cuts]
    out_ref[:width] = (dot_tn(inner[...], d_pre[0]) + dot_tn(near[0], near[1])).astype(BF)
    out_ref[width:] = (dot_tn(hidden[0], low[...]) + dot_tn(near[2], near[3])).astype(BF)


def self_grads_kernel(inner, branch, d_rows, low_t, early, moved, outs):
    lat = inner.shape[0]
    own = low_t.shape[1]
    heads_in = [moved[lat:, own * i : own * (i + 1)] for i in range(4)]
    for i in range(3):
        part = dot_tn(d_rows[0, i], inner[...]) + dot_tn(heads_in[i], early[2 * lat :])
        outs[own * i : own * (i + 1)] = part.astype(BF)
    part = dot(low_t[0], branch[...]) + dot_tn(heads_in[3], moved[:lat])
    outs[3 * own :] = part.astype(BF)


def output_grad_kernel(low, branch, branch_y, out_ref):
    part = dot(low[0], branch[...]) + dot(low[1], branch_y[...])
    out_ref[...] = part.astype(BF)


def head_move(x, k):
    n = lax.axis_size("head")
    return lax.ppermute(x, "head", [(i, i ^ k) for i in range(n)])


def mod_move(x):
    return lax.ppermute(x, "mod", [(0, 1), (1, 0)])


def tok_move(x, shift):
    n = lax.axis_size("tok")
    return lax.ppermute(x, "tok", [(i, (i + shift) % n) for i in range(n)])


def after(x, *earlier):
    return lax.optimization_barrier((x, *earlier))[0]


def on_device(
    latents,
    video_tokens,
    text_tokens,
    frame_counts,
    text_lengths,
    drop_mask,
    cotangent,
    norm_latent_gain,
    norm_latent_bias,
    norm_input_gain,
    norm_input_bias,
    cross_query,
    cross_key,
    cross_value,
    cross_output,
    norm_cross_gain,
    norm_cross_bias,
    cross_up,
    cross_down,
    norm_self_gain,
    norm_self_bias,
    self_query,
    self_key,
    self_value,
    self_output,
    norm_ffn_gain,
    norm_ffn_bias,
    self_up,
    self_down,
):
    clips, lat, width = latents.shape
    span = video_tokens.shape[1]
    own = cross_key.shape[1]
    heads = own // HEAD
    shards = lax.axis_size("tok")
    zones = clips // 2
    tok, mod, head = lax.axis_index("tok"), lax.axis_index("mod"), lax.axis_index("head")
    side_x, side_y = lax.rem(head, 2), head // 2
    rows = 784 if span % 784 == 0 else span
    norms = jnp.stack(
        [norm_latent_gain, norm_latent_bias, norm_input_gain, norm_input_bias,
         norm_cross_gain, norm_cross_bias, norm_self_gain, norm_self_bias,
         norm_ffn_gain, norm_ffn_bias]
    )
    cross_kvq = [cross_key.T, cross_value.T, cross_query.T]
    self_weights = [self_query.T, self_key.T, self_value.T, self_output]

    at = Plan(clips, span // rows)
    last = (tok == shards - 1).astype(jnp.int32)
    places = jnp.stack([tok, side_x, side_y, mod, last]).astype(jnp.int32)
    plan = make_plan(at, places, frame_counts, text_lengths, drop_mask, rows, span)

    (pack,) = pack_halves(at, plan, [[cross_up, cross_down] + self_weights + [cross_output]])
    near = head_move(pack, 2)
    tables = jnp.concatenate(cross_kvq, 0)
    if shards == zones:
        part = tables.shape[0] // shards
        tables = lax.dynamic_slice_in_dim(tables, tok * part, part, 0)
        tables = lax.all_gather(tables, ("tok", "head")).reshape(shards, 4, part, width)
    else:
        tables = lax.all_gather(tables, "head")[None]

    d_video, *partial = tokens_forward(
        at, plan, video_tokens, text_tokens, latents, (norms, *cross_kvq), rows
    )
    received = [tok_move(partial[k % zones], k) for k in range(1, shards)]
    (pack3,) = pack_halves(at, tie(plan, partial[0]), [[self_up, self_down]])
    my_latents, my_cotangent, other_cotangent, keep = own_rows(
        at, tie(plan, partial[0]), latents, cotangent
    )
    lw = (lat, width)
    square = ((width, width), BF)
    mine, other, low, branch, branch_other = kernel_call(
        combine_kernel, [(partial[0].shape[1:], BF)] * 2 + [((2, own, lat), BF)] + [(lw, BF)] * 2,
        cross_output, partial[0], *received, name="combine", scalars=(plan,), deps=(my_latents,),
    )
    near = tie(near, mine)
    far = mod_move(near)
    branch_parts = [branch, head_move(branch, 1), head_move(branch_other, 2), head_move(branch_other, 3)]

    near3 = head_move(tie(pack3, *branch_parts[1:]), 2)

    first, inner1, pre1, hidden1, part = kernel_call(
        cross_forward_kernel,
        [(lw, F32), (lw, BF), ((2,) + lw, F32), ((2,) + lw, BF), (lw, BF)],
        *branch_parts, my_latents, keep, norms, cross_up, cross_down, near, far,
        name="cross_forward", scalars=(plan,), scratch=[square] * 2,
    )
    mine_y = head_move(tie(other, first), 2)
    second, self_in, self_rows, self_query_t, self_attended, self_lse, part, moving = kernel_call(
        self_forward_kernel,
        [(lw, F32), (lw, BF), ((2, 3, lat, own), BF), ((2, own, lat), BF), ((2, own, lat), F32),
         ((2, 1, heads * lat), F32), (lw, BF), ((3 * lat, width), BF)],
        first, part, head_move(part, 1), norms, *self_weights, near, far, inner1, hidden1,
        name="self_forward", scalars=(plan,), scratch=[((4, own, width), BF)],
    )
    early = head_move(moving, 2)
    near3 = tie(near3, second)
    far3 = mod_move(near3)
    pair, pair_t, query_t = kernel_call(
        tables_kernel,
        [((width, 2 * width), BF), ((2 * width, width), BF), ((width, width), BF)],
        tables, name="tables", beside=4.7, scalars=(plan,),
    )
    third, inner2, hidden2, d_pre2, part, moving = kernel_call(
        last_back_kernel,
        [(lw, F32), (lw, BF), ((2,) + lw, BF), ((2,) + lw, BF), (lw, BF), ((3 * lat, width), BF)],
        second, part, head_move(part, 1), my_cotangent, norms, self_up, self_down, near3, far3,
        name="last_back", scalars=(plan,), deps=(pair,), scratch=[square] * 2,
    )
    received = head_move(part, 1)
    halves = head_move(moving, 2)
    (out_part,) = kernel_call(
        down_kernel, [(lw, BF)], hidden2, self_down, near3, far3,
        name="down", beside=3.4, scalars=(plan,), scratch=[square], deps=(part,),
    )
    grad_third, ffn_sums, self_branch, self_d_rows, self_low, part, moving = kernel_call(
        self_back_kernel,
        [(lw, F32), ((2, width), F32), (lw, BF), ((2, 3, lat, own), BF), ((2, own, lat), BF), (lw, BF),
         ((2 * lat, width), BF)],
        my_cotangent, third, part, received, norms,
        self_rows, self_query_t, self_attended, self_lse, *self_weights, near, far,
        name="self_back", scalars=(plan,), deps=(out_part, early), scratch=[((4, own, width), BF)],
    )
    out_moved = head_move(out_part, 1)
    moved_self = head_move(moving, 2)
    (out_half,) = kernel_call(
        half_rows_kernel, [((lat // 2, width), BF)], third, out_part, out_moved,
        name="half_rows", beside=1.5, scalars=(plan,), scratch=[(lw, F32)],
    )
    out_halves = lax.all_gather(out_half, ("tok", "head"))
    grad_second, self_sums, low1, d_pre1, part, moving = kernel_call(
        cross_back_kernel,
        [(lw, F32), ((2, width), F32), (lw, BF), ((2,) + lw, BF), (lw, BF), ((2 * lat, width), BF)],
        grad_third, second, part, head_move(part, 1), norms, pre1,
        cross_up, cross_down, near, far,
        name="cross_back", scalars=(plan,), deps=(out_half, halves), scratch=[square] * 2,
    )

    moved = head_move(moving, 2)
    cross_branch, packed, grad_first, cross_sums = kernel_call(
        attended_back_kernel,
        [(lw, BF), ((2 * own + 2 * STAT, lat), BF), (lw, F32), ((2, width), F32)],
        grad_second, first, part, head_move(part, 1), norms, keep,
        mine, mine_y, cross_output, near, far,
        name="attended_back", scalars=(plan,), scratch=[((own, width), BF)],
        deps=(moved_self,),
    )

    (stages,) = kernel_call(
        stack_kernel, [((zones,) + packed.shape, BF)],
        packed, *[tok_move(packed, shards - k) for k in range(1, zones)], name="stack",
        deps=(moved,),
    )
    arrived = [stages] + [head_move(stages, k) for k in (1, 2, 3)]
    (mlp2,) = kernel_call(
        functools.partial(mlp_grads_kernel, cuts=((0, 0), (0, 1), (0, 2), (1, 0))),
        [((2 * width, width), BF)], inner2, d_pre2, hidden2, my_cotangent, halves, other_cotangent,
        name="last_weights", beside=4.0, deps=(packed,),
    )
    branch_y = head_move(cross_branch, 2)
    (self_grads,) = kernel_call(
        self_grads_kernel, [((4 * own, width), BF)],
        self_in, self_branch, self_d_rows, self_low, early, moved_self, name="self_weights", beside=3.3,
        deps=(stages,),
    )
    (mlp1,) = kernel_call(
        functools.partial(mlp_grads_kernel, cuts=((0, 0), (1, 0), (0, 1), (1, 1))),
        [((2 * width, width), BF)], inner1, d_pre1, hidden1, low1, early, moved, name="cross_weights", beside=4.4,
        deps=(stages,),
    )
    (output_grad,) = kernel_call(
        output_grad_kernel, [((own, width), BF)], low, cross_branch, branch_y,
        name="output_weights", beside=2.1,
    )
    counted = lambda grads: [jnp.where(tok < zones, a, 0) if shards > zones else a for a in grads]
    params = (norms, pair, pair_t, query_t)
    tokens = (video_tokens, text_tokens, latents)
    d_text = jnp.zeros_like(text_tokens)
    d_video = tie(d_video, mlp2, self_grads, mlp1, output_grad, *arrived[1:], beside=25.0)
    d_video, d_text, token_weights, keep_half, send_half, *d_query = tokens_back(
        at, plan, 0, *tokens, params, arrived, [d_video, d_text], None, rows, deps=(out_halves,)
    )
    sums = lax.psum(counted([mlp2, self_grads, mlp1, output_grad]), ("tok", "mod"))
    mlp2, self_grads, mlp1, output_grad = (a.astype(F32) for a in sums)
    up1, down1 = mlp1[:width], mlp1[width:]
    up2, down2 = mlp2[:width], mlp2[width:]

    (latents_out,) = kernel_call(
        functools.partial(out_rows_kernel, at=at), [(latents.shape, BF)], out_halves[: 4 * zones],
        name="out_rows", scalars=(plan,),
    )

    whole_rows = token_weights.shape[0]
    step = whole_rows // zones
    received = [tok_move(d_query[k % zones], k) for k in range(1, shards)]
    my_query, other_query = kernel_call(
        query_sum_kernel, [((own, lat), BF)] * 2, d_query[0], *received, name="query_sum"
    )
    if shards == zones:
        token_own, *pieces = kernel_call(
            functools.partial(tail_pack_kernel, at=at),
            [((step, width // 2), F32)] + [((step, width // 2), BF)] * (zones - 1),
            keep_half, mod_move(send_half), name="tail_pack", scalars=(plan,),
        )
        received = [tok_move(p, k + 1) for k, p in enumerate(pieces)]
        (share,) = kernel_call(
            share_sum_kernel, [((step, width // 2), BF)], token_own, *received,
            name="share_sum", deps=(my_query, latents_out),
        )
        shares = [share] + [tok_move(share, shards - k) for k in range(1, zones)]
        (shares,) = kernel_call(
            stack_kernel, [((zones,) + share.shape, BF)], *shares, name="stack"
        )
        d_key_t, d_value_t, d_query_t, input_sums = kernel_call(
            functools.partial(token_weights_kernel, at=at),
            [((own, width), F32)] * 3 + [((2, width), F32)],
            shares, mod_move(shares), name="token_weights", scalars=(plan,),
            scratch=[((whole_rows, width), F32)],
        )
    else:
        total = lax.psum(token_weights, ("tok", "mod"))
        d_key_t, d_value_t, d_query_t = (total[own * i : own * (i + 1)] for i in range(3))
        input_sums = jnp.sum(total[3 * own : 3 * own + 16].reshape(2, 8, width), 1)
    d_queries = [my_query] + [head_move(a, k) for k, a in ((1, my_query), (2, other_query), (3, other_query))]
    (my_grad,) = kernel_call(
        latent_back_kernel, [((lat // 2 + STAT, width), BF)],
        grad_first, my_latents, norms, *d_queries, query_t, cross_sums, self_sums, ffn_sums,
        name="latent_back", scalars=(plan,), scratch=[(lw, F32)],
    )
    zones_grad = jnp.stack([my_grad] + [tok_move(my_grad, shards - k) for k in range(1, zones)])
    zones_grad = [zones_grad] + [head_move(zones_grad, k) for k in (1, 2, 3)]
    grad_latents, norm_sums = in_clip_order(at, plan, lat, zones_grad)
    norm_sums = norm_sums + mod_move(norm_sums)
    return (
        latents_out,
        grad_latents,
        d_video,
        d_text,
        norm_sums[0],
        norm_sums[1],
        input_sums[0],
        input_sums[1],
        d_query_t.T,
        d_key_t.T,
        d_value_t.T,
        output_grad,
        norm_sums[2],
        norm_sums[3],
        up1,
        down1,
        norm_sums[4],
        norm_sums[5],
        self_grads[:own].T,
        self_grads[own : 2 * own].T,
        self_grads[2 * own : 3 * own].T,
        self_grads[3 * own :],
        norm_sums[6],
        norm_sums[7],
        up2,
        down2,
    )


def solution(mesh):
    in_specs = (
        P("mod", None, None),
        P("mod", "tok", None),
        P("mod", None, None),
        P("mod"),
        P("mod"),
        P("mod"),
        P("mod", None, None),
        P(),
        P(),
        P(),
        P(),
        P(None, "head"),
        P(None, "head"),
        P(None, "head"),
        P("head", None),
        P(),
        P(),
        P(None, "head"),
        P("head", None),
        P(),
        P(),
        P(None, "head"),
        P(None, "head"),
        P(None, "head"),
        P("head", None),
        P(),
        P(),
        P(None, "head"),
        P("head", None),
    )
    out_specs = (
        P("mod", None, None),
        P("mod", None, None),
        P("mod", "tok", None),
        P("mod", None, None),
        P(),
        P(),
        P(),
        P(),
        P(None, "head"),
        P(None, "head"),
        P(None, "head"),
        P("head", None),
        P(),
        P(),
        P(None, "head"),
        P("head", None),
        P(),
        P(),
        P(None, "head"),
        P(None, "head"),
        P(None, "head"),
        P("head", None),
        P(),
        P(),
        P(None, "head"),
        P("head", None),
    )
    return jax.shard_map(
        on_device, mesh=mesh, in_specs=in_specs, out_specs=out_specs, check_vma=False
    )
```
